32 devices in a mesh: dp: 8 (over z, x), mp: 4 (over y, core).
Axes of the slice: x: 2, y: 2, z: 4, core: 2. Of those that a mesh axis runs over, the one named last changes fastest.
Arguments:
- tokens: bfloat16 [12288, 768], P(('dp', 'mp')), may hold values from -6 to 6
- out_grad: bfloat16 [12288, 768], P(('dp', 'mp')), may hold values from -6 to 6
- segment_ids: int32 [24, 512], P('dp'), may hold values from 0 to 1, as said below
- group_ids: int32 [24, 512], P('dp'), may hold values from 0 to 3
- answer_ids: int32 [24, 512], P('dp'), may hold values 0 or 1
- pad_lengths: int32 [24], P('dp'), may hold values from 256 to 512, as said below
- qkv_master: float32 [3, 768, 768], P(None, 'dp', 'mp'), may hold values from -0.21875 to 0.21875
- out_master: float32 [768, 768], P('mp', 'dp'), may hold values from -1.25 to 1.25
- up_master: float32 [768, 3072], P('dp', 'mp')
- down_master: float32 [3072, 768], P('mp', 'dp'), may hold values from -0.15625 to 0.15625
- norm_master: float32 [6, 4, 192], P(None, 'mp', 'dp')
- bias_master: float32 [4, 1152], P('mp', 'dp'), may hold values from -2 to 2
- qkv_first: float32 [3, 768, 768], P(None, 'dp', 'mp')
- out_first: float32 [768, 768], P('mp', 'dp')
- up_first: float32 [768, 3072], P('dp', 'mp')
- down_first: float32 [3072, 768], P('mp', 'dp')
- norm_first: float32 [6, 4, 192], P(None, 'mp', 'dp')
- bias_first: float32 [4, 1152], P('mp', 'dp')
- qkv_second: float32 [3, 768, 768], P(None, 'dp', 'mp')
- out_second: float32 [768, 768], P('mp', 'dp')
- up_second: float32 [768, 3072], P('dp', 'mp')
- down_second: float32 [3072, 768], P('mp', 'dp')
- norm_second: float32 [6, 4, 192], P(None, 'mp', 'dp')
- bias_second: float32 [4, 1152], P('mp', 'dp')
Outputs:
- block_out: bfloat16 [12288, 768], P(('dp', 'mp'))
- input_grad: bfloat16 [12288, 768], P(('dp', 'mp'))
- grad_norm: float32 [], replicated
- new_qkv: float32 [3, 768, 768], P(None, 'dp', 'mp')
- new_out: float32 [768, 768], P('mp', 'dp')
- new_up: float32 [768, 3072], P('dp', 'mp')
- new_down: float32 [3072, 768], P('mp', 'dp')
- new_norm: float32 [6, 4, 192], P(None, 'mp', 'dp')
- new_bias: float32 [4, 1152], P('mp', 'dp')
- first_qkv: float32 [3, 768, 768], P(None, 'dp', 'mp')
- first_out: float32 [768, 768], P('mp', 'dp')
- first_up: float32 [768, 3072], P('dp', 'mp')
- first_down: float32 [3072, 768], P('mp', 'dp')
- first_norm: float32 [6, 4, 192], P(None, 'mp', 'dp')
- first_bias: float32 [4, 1152], P('mp', 'dp')
- second_qkv: float32 [3, 768, 768], P(None, 'dp', 'mp')
- second_out: float32 [768, 768], P('mp', 'dp')
- second_up: float32 [768, 3072], P('dp', 'mp')
- second_down: float32 [3072, 768], P('mp', 'dp')
- second_norm: float32 [6, 4, 192], P(None, 'mp', 'dp')
- second_bias: float32 [4, 1152], P('mp', 'dp')
The draws below stay inside these ranges and needn't reach their ends.
Inputs may be any that keep to these rules, and one draw needn't show every extreme that they name: `segment_ids`: each sequence's question (segment 0) is a first run of 1 to 129 positions; segment 1 follows. `pad_lengths`: some sequence in every draw has no padding.
All inputs are finite; a program needn't handle non-finite values. No bound on the sum of `answer_ids` on one device may be relied on, other than what follows from the above.
Results may differ from the reference program's by a relative error of at most 0.025.
Values may be sent and summed in bfloat16 or wider, within the bound.
A program may use at most 128 MiB of HBM per device.

```python
import math
import jax
import jax.numpy as jnp
from jax import lax

D = 768
H = 12
HD = 64
FF = 3072
LEN = 512
STEP = 5
SEQS = 24
TOKENS = 12288
CB = 1152
PARAMS = 7087104
N_MP = 4


clip_limit = 0.05


def moment_scale(factor):
    return factor * clip_limit / math.sqrt(PARAMS)


def first_draw(key, shape, factor):
    return jax.random.normal(key, shape, jnp.float32) * moment_scale(factor)


def second_draw(key, shape, factor):
    base = moment_scale(factor)
    exponent = jax.random.uniform(key, shape, jnp.float32, math.log(0.5), math.log(8.0))
    return jnp.exp(exponent) * (base * base)


def draw_segment_ids(key, part):
    key = jax.random.fold_in(key, 1)
    first = jax.random.randint(key, (SEQS, 1), 1, LEN // 4 + 2)
    positions = jnp.arange(LEN, dtype=jnp.int32)[None, :]
    return (positions >= first).astype(jnp.int32)


def draw_pad_lengths(key, part):
    key = jax.random.fold_in(key, 2)
    key_len, key_pick = jax.random.split(key)
    lengths = jax.random.randint(key_len, (SEQS,), LEN // 2, LEN + 1)
    chosen = jax.random.randint(key_pick, (), 0, SEQS)
    return jnp.where(jnp.arange(SEQS, dtype=jnp.int32) == chosen, LEN, lengths).astype(jnp.int32)


def draw_up_master(key, part):
    key = jax.random.fold_in(key, 3)
    ramp = jnp.arange(FF, dtype=jnp.float32) / (FF - 1)
    entries = jax.random.normal(key, (D, FF), jnp.float32)
    column_scale = 0.6 + 1.2 * ramp
    return entries * column_scale[None, :] / math.sqrt(D)


def draw_norm_master(key, part):
    key = jax.random.fold_in(key, 4)
    key_gain, key_shift = jax.random.split(key)
    ramp = jnp.arange(D, dtype=jnp.float32) / (D - 1)
    rising = 0.6 + 1.2 * ramp
    wobble = 1.0 + 0.1 * jax.random.normal(key_gain, (2, D), jnp.float32)
    gains = rising[None, :] * wobble
    shifts = 0.3 * jax.random.normal(key_shift, (4, D), jnp.float32)
    table = jnp.stack([gains[0], shifts[0], shifts[1], gains[1], shifts[2], shifts[3]])
    return table.reshape(6, N_MP, D // N_MP)


def draw_qkv_first(key, part):
    key = jax.random.fold_in(key, 11)
    return first_draw(key, (3, D, D), 0.5)


def draw_out_first(key, part):
    key = jax.random.fold_in(key, 12)
    return first_draw(key, (D, D), 1.0)


def draw_up_first(key, part):
    key = jax.random.fold_in(key, 13)
    return first_draw(key, (D, FF), 1.0)


def draw_down_first(key, part):
    key = jax.random.fold_in(key, 14)
    return first_draw(key, (FF, D), 1.0)


def draw_norm_first(key, part):
    key = jax.random.fold_in(key, 15)
    return first_draw(key, (6, N_MP, D // N_MP), 3.0)


def draw_bias_first(key, part):
    key = jax.random.fold_in(key, 16)
    return first_draw(key, (N_MP, CB), 2.0)


def draw_qkv_second(key, part):
    key = jax.random.fold_in(key, 21)
    return second_draw(key, (3, D, D), 0.5)


def draw_out_second(key, part):
    key = jax.random.fold_in(key, 22)
    return second_draw(key, (D, D), 1.0)


def draw_up_second(key, part):
    key = jax.random.fold_in(key, 23)
    return second_draw(key, (D, FF), 1.0)


def draw_down_second(key, part):
    key = jax.random.fold_in(key, 24)
    return second_draw(key, (FF, D), 1.0)


def draw_norm_second(key, part):
    key = jax.random.fold_in(key, 25)
    return second_draw(key, (6, N_MP, D // N_MP), 3.0)


def draw_bias_second(key, part):
    key = jax.random.fold_in(key, 26)
    return second_draw(key, (N_MP, CB), 2.0)


def touch_ends(values, key, low, high):
    index_at = [jax.random.randint(jax.random.fold_in(key, axis), (), 0, length) for axis, length in enumerate(values.shape)]
    longest = values.shape.index(max(values.shape))
    beside = index_at[:longest] + [(index_at[longest] + 1) % values.shape[longest]] + index_at[longest + 1:]
    return values.at[tuple(index_at)].set(low).at[tuple(beside)].set(high)


def levels(stream_key, shape, cuts, least, top_value):
    level, own = 1.0, jax.random.fold_in(stream_key, 6)
    for axis_at, parts in cuts:
        steps = jnp.exp(jax.random.uniform(jax.random.fold_in(own, axis_at), (parts,), jnp.float32, least / len(cuts), top_value / len(cuts)))
        level = level * jnp.repeat(steps, shape[axis_at] // parts).reshape([-1 if axis == axis_at else 1 for axis in range(len(shape))])
    return level


def scatter_about(own_key, extent, scale, bound, shards=(), held_as=jnp.bfloat16):
    values = scale * jax.random.normal(own_key, extent, jnp.float32)
    if shards:
        values = values * levels(own_key, extent, shards, -0.22, 0.18)
    return jnp.clip(values, -bound, bound).astype(held_as)


def setup_inputs(seed: int = 0) -> dict:
    seeds = jax.random.split(jax.random.key(seed), 25)
    tokens = scatter_about(seeds[0], (TOKENS, D), 1.0, 6.0, ((0, 32),))
    out_grad = scatter_about(seeds[1], (TOKENS, D), 1.0, 6.0, ((0, 32),))
    segment_ids = draw_segment_ids(jax.random.fold_in(seeds[24], 71), 0)
    group_ids = touch_ends(jax.random.randint(seeds[3], (SEQS, LEN), 0, 4), jax.random.fold_in(seeds[3], 1), 0, 3).astype(jnp.int32)
    answer_ids = touch_ends((jax.random.randint(seeds[4], (SEQS, LEN), 0, 8) < 1).astype(jnp.int32), jax.random.fold_in(seeds[4], 1), 0, 1)
    pad_lengths = draw_pad_lengths(jax.random.fold_in(seeds[24], 71), 0)
    qkv_master = scatter_about(seeds[6], (3, D, D), D ** -0.5, 0.21875, ((1, 8), (2, 4)), jnp.float32)
    out_master = scatter_about(seeds[7], (D, D), (D // 32) ** -0.5, 1.25, ((0, 4), (1, 8)), jnp.float32)
    up_master = draw_up_master(jax.random.fold_in(seeds[24], 71), 0)
    down_master = scatter_about(seeds[9], (FF, D), (FF // 2) ** -0.5, 0.15625, ((0, 4), (1, 8)), jnp.float32)
    norm_master = draw_norm_master(jax.random.fold_in(seeds[24], 71), 0)
    bias_master = scatter_about(seeds[11], (N_MP, CB), 0.3, 2.0, ((0, 4), (1, 8)), jnp.float32)
    qkv_first = draw_qkv_first(jax.random.fold_in(seeds[24], 71), 0)
    out_first = draw_out_first(jax.random.fold_in(seeds[24], 71), 0)
    up_first = draw_up_first(jax.random.fold_in(seeds[24], 71), 0)
    down_first = draw_down_first(jax.random.fold_in(seeds[24], 71), 0)
    norm_first = draw_norm_first(jax.random.fold_in(seeds[24], 71), 0)
    bias_first = draw_bias_first(jax.random.fold_in(seeds[24], 71), 0)
    qkv_second = draw_qkv_second(jax.random.fold_in(seeds[24], 71), 0)
    out_second = draw_out_second(jax.random.fold_in(seeds[24], 71), 0)
    up_second = draw_up_second(jax.random.fold_in(seeds[24], 71), 0)
    down_second = draw_down_second(jax.random.fold_in(seeds[24], 71), 0)
    norm_second = draw_norm_second(jax.random.fold_in(seeds[24], 71), 0)
    bias_second = draw_bias_second(jax.random.fold_in(seeds[24], 71), 0)
    return dict(tokens=tokens, out_grad=out_grad, segment_ids=segment_ids, group_ids=group_ids, answer_ids=answer_ids, pad_lengths=pad_lengths, qkv_master=qkv_master, out_master=out_master, up_master=up_master, down_master=down_master, norm_master=norm_master, bias_master=bias_master, qkv_first=qkv_first, out_first=out_first, up_first=up_first, down_first=down_first, norm_first=norm_first, bias_first=bias_first, qkv_second=qkv_second, out_second=out_second, up_second=up_second, down_second=down_second, norm_second=norm_second, bias_second=bias_second)


norm_epsilon = 1e-06
adam_epsilon = 1e-08
learn_rates = (0.02, 0.1, 0.02, 0.02, 0.5, 0.5)
beta_first = 0.5
beta_second = 0.5
decay_rate = 0.01
clip_limit = 0.05
mask_fill = -1000000000.0
score_scale = 0.125
highest = lax.Precision.HIGHEST

@jax.custom_vjp
def low(v):
    return lax.optimization_barrier(v.astype(jnp.bfloat16)).astype(jnp.float32)

@jax.custom_vjp
def low_back(v):
    return v

def low_keep(v):
    return (low(v), None)

def low_pass(kept, grad):
    return (grad,)

def back_keep(v):
    return (v, None)

def back_low(kept, grad):
    return (low(grad),)
low.defvjp(low_keep, low_pass)
low_back.defvjp(back_keep, back_low)

def layer_norm(rows, gain, shift):
    mean = lax.optimization_barrier(jnp.mean(rows, -1, keepdims=True))
    centred = rows - mean
    spread = lax.optimization_barrier(jnp.mean(centred * centred, -1, keepdims=True))
    return centred * lax.rsqrt(spread + norm_epsilon) * gain + shift

def visible_mask(segment, group, answer, length):
    positions = jnp.arange(segment.shape[-1], dtype=jnp.int32)
    valid_key = positions[None, :] < length[:, None]
    open_key = (segment == 0) | (answer == 1)
    rule = (segment[:, :, None] == 0) | open_key[:, None, :] | (group[:, :, None] == group[:, None, :])
    return rule & valid_key[:, None, :]

def adam_update(weight, grad, first, second, factor, decayed, rate):
    clipped = grad * factor
    first_new = beta_first * first + (1.0 - beta_first) * clipped
    second_new = beta_second * second + (1.0 - beta_second) * clipped * clipped
    ratio = first_new / (1.0 - beta_first ** STEP) / (jnp.sqrt(second_new / (1.0 - beta_second ** STEP)) + adam_epsilon)
    if decayed:
        ratio = ratio + decay_rate * weight
    return (weight - rate * ratio, first_new, second_new)

def reference(tokens, out_grad, segment_ids, group_ids, answer_ids, pad_lengths, qkv_master, out_master, up_master, down_master, norm_master, bias_master, qkv_first, out_first, up_first, down_first, norm_first, bias_first, qkv_second, out_second, up_second, down_second, norm_second, bias_second):
    seq_total = tokens.shape[0] // LEN
    group_size = math.gcd(seq_total, max(1, 4096 // LEN))
    blocks = seq_total // group_size
    visible = visible_mask(segment_ids, group_ids, answer_ids, pad_lengths)
    local_width = D // N_MP

    def forward(inputs, joint_master, output_master, upper_master, lower_master, table_master, column_master):
        joint_weight = low(joint_master)
        out_weight = low(output_master)
        up_weight = low(upper_master)
        down_weight = low(lower_master)
        gains = low(table_master).reshape(6, D)
        column_bias = low(column_master)
        bias_query = column_bias[:, :local_width].reshape(D)
        bias_value = column_bias[:, local_width:2 * local_width].reshape(D)
        bias_up = column_bias[:, 2 * local_width:].reshape(FF)
        bias_joint = jnp.stack([bias_query, jnp.zeros_like(bias_query), bias_value])

        def block(rows, allowed):
            projected = jnp.einsum('td,cdj->tcj', rows, joint_weight, precision=highest) + bias_joint[None]
            projected = low_back(low(projected))
            shaped = projected.reshape(group_size, LEN, 3, H, HD)
            queries = shaped[:, :, 0]
            keys = shaped[:, :, 1]
            values = shaped[:, :, 2]
            scores = jnp.einsum('bqhe,bkhe->bhqk', queries, keys, precision=highest) * score_scale
            scores = low_back(scores)
            scores = jnp.where(allowed[:, None], scores, mask_fill)
            peak = lax.optimization_barrier(jnp.max(scores, -1, keepdims=True))
            expo = jnp.exp(scores - peak)
            shares = expo / lax.optimization_barrier(jnp.sum(expo, -1, keepdims=True))
            mixed = jnp.einsum('bhqk,bkhe->bqhe', low(shares), values, precision=highest)
            mixed = low_back(low(mixed.reshape(group_size * LEN, D)))
            branch = low_back(jnp.dot(mixed, out_weight, precision=highest) + gains[2])
            normed = layer_norm(rows + branch, gains[0], gains[1])
            hidden = low_back(jnp.dot(low(normed), up_weight, precision=highest) + bias_up)
            active = low(jax.nn.gelu(hidden, approximate=False))
            second = low_back(jnp.dot(active, down_weight, precision=highest) + gains[5])
            return layer_norm(normed + second, gains[3], gains[4])
        block = jax.checkpoint(block)

        def stepper(carry, items):
            return (carry, block(items[0], items[1]))
        _, outputs = lax.scan(stepper, jnp.zeros((), jnp.float32), (inputs.reshape(blocks, group_size * LEN, D), visible.reshape(blocks, group_size, LEN, LEN)))
        return outputs.reshape(-1, D)
    masters = (qkv_master, out_master, up_master, down_master, norm_master, bias_master)
    result, pullback = jax.vjp(forward, tokens.astype(jnp.float32), *masters)
    grads = pullback(out_grad.astype(jnp.float32))
    input_grad = grads[0].astype(jnp.bfloat16)
    weight_grads = grads[1:]
    squares = jnp.zeros((), jnp.float32)
    for grad in weight_grads:
        squares = squares + jnp.sum(grad * grad)
    grad_norm = jnp.sqrt(squares)
    factor = jnp.minimum(1.0, clip_limit / grad_norm)
    firsts = (qkv_first, out_first, up_first, down_first, norm_first, bias_first)
    seconds = (qkv_second, out_second, up_second, down_second, norm_second, bias_second)
    updated = []
    for index in range(6):
        updated.append(adam_update(masters[index], weight_grads[index], firsts[index], seconds[index], factor, index < 4, learn_rates[index]))
    return (result.astype(jnp.bfloat16), input_grad, grad_norm, updated[0][0], updated[1][0], updated[2][0], updated[3][0], updated[4][0], updated[5][0], updated[0][1], updated[1][1], updated[2][1], updated[3][1], updated[4][1], updated[5][1], updated[0][2], updated[1][2], updated[2][2], updated[3][2], updated[4][2], updated[5][2])
```

```python
import functools
import jax
import jax.numpy as jnp
import numpy as np
from jax import lax
from jax.sharding import Mesh, PartitionSpec as P
from jax.experimental import pallas as pl
from jax.experimental.pallas import tpu as pltpu

MESH = pl.DeviceIdType.MESH
F32 = jnp.float32
BF16 = jnp.bfloat16
HD = 64
STEP = 5

norm_epsilon = 1e-06
adam_epsilon = 1e-08
learn_rates = (0.02, 0.1, 0.02, 0.02, 0.5, 0.5)
beta_first = 0.5
beta_second = 0.5
decay_rate = 0.01
clip_limit = 0.05
mask_fill = -1000000000.0
score_scale = 0.125

ATT, UP, DOWN = 0, 1, 2


def pick(index, values):
    out = values[-1]
    for k in range(len(values) - 1):
        out = jnp.where(index == k, values[k], out)
    return out


class Place:
    def __init__(self):
        outer = lax.axis_index("outer")
        self.sub = lax.axis_index("inner")
        self.m = lax.axis_index("mp")
        self.z = outer // 2
        self.x = lax.rem(outer, 2)
        self.y = self.m // 2
        self.c = lax.rem(self.m, 2)
        self.first = self.c == 0
        self.sib = self.at(c=1 - self.c)
        x, y = self.line(1, 0)
        self.second = self.at(x=x, y=y)
        x, y = self.line(0, 1)
        self.third = self.at(x=x, y=y)

    def at(self, z=None, x=None, y=None, c=None):
        z = self.z if z is None else z
        x = self.x if x is None else x
        y = self.y if y is None else y
        c = self.c if c is None else c
        return (z * 2 + x, self.sub, y * 2 + c)

    def mate(self, m):
        return (self.z * 2 + self.x, self.sub, m)

    def line(self, side, far, other_core=False):
        first = (1 - self.c if other_core else self.c) == 0
        x = jnp.where(first, side, far)
        y = jnp.where(first, far, side)
        return self.x + x - 2 * self.x * x, self.y + y - 2 * self.y * y

    def order(self, t):
        return pick(self.z, [(0, 1, 2, 3), (1, 0, 3, 2), (2, 2, 1, 1), (3, 3, 0, 0)][t])


def remote(src, dst, send, recv, device):
    return pltpu.make_async_remote_copy(
        src_ref=src, dst_ref=dst, send_sem=send, recv_sem=recv, device_id=device, device_id_type=MESH
    )


def greet(place, mids):
    barrier = pltpu.get_barrier_semaphore()

    def hello(device):
        pl.semaphore_signal(barrier, inc=1, device_id=device, device_id_type=MESH)

    z = place.z
    hello(place.sib)
    hello(place.second)
    hello(place.third)
    hello(place.at(z=z + 2 - 4 * (z // 2)))
    pl.when(z > 0)(lambda: hello(place.at(z=z - 1)))
    pl.when(z < 3)(lambda: hello(place.at(z=z + 1)))
    count = 4 + jnp.where(z > 0, 1, 0) + jnp.where(z < 3, 1, 0)
    if mids:
        inside = (place.m == 1) | (place.m == 2)
        pl.when(inside)(lambda: hello((place.z * 2 + place.x, place.sub, 3 - place.m)))
        count = count + jnp.where(inside, 1, 0)
    pl.semaphore_wait(barrier, count)


class Gather:
    def __init__(self, place, g, chunks, sems):
        self.p, self.g, self.chunks = place, g, chunks
        self.sems = sems
        self.width = g.shape[4] // 4
        self.sent = []

    def piece(self, j, z, side, far, core=False):
        x, y = self.p.line(side, far, core)
        c = 1 - self.p.c if core else self.p.c
        a, low, w = self.chunks[j]
        cols = pl.ds(pl.multiple_of((y * 2 + c) * self.width + low, 128), w)
        if z is None:
            return self.g.at[a, :, x, :, cols]
        return self.g.at[a, z, x, :, cols]

    def go(self, ref, send, recv, device, when=None):
        copy = remote(ref, ref, send, recv, device)
        if when is None:
            copy.start()
        else:
            pl.when(when)(copy.start)
        self.sent.append((copy, when))

    def arrived(self, ref, recv):
        remote(ref, ref, recv, recv, self.p.sib).wait_recv()

    def z_send(self, a, src, index, to, when):
        zs, zr = self.sems[0], self.sems[1]
        self.go(self.piece(a, src, 0, 0), zs.at[a, index], zr.at[a, src], self.p.at(z=to), when)

    def side_sends(self, a, src):
        zs, zr, ps, pr, ts, tr, cs, cr = self.sems
        self.go(self.piece(a, src, 0, 0), ts.at[a, src], tr.at[a, src], self.p.third)
        self.go(self.piece(a, src, 0, 0), ps.at[a, src], pr.at[a, src], self.p.second)

    def core_send(self, a, k, side, far):
        cs, cr = self.sems[6], self.sems[7]
        self.go(self.piece(a, None, side, far), cs.at[a, k], cr.at[a, k], self.p.sib)

    def own(self, a):
        z = self.p.z
        self.z_send(a, z, z, z + 1, z < 3)
        self.z_send(a, z, 4, z - 1, z > 0)
        self.side_sends(a, z)

    def z_step(self, a, t):
        z = self.p.z
        src = self.p.order(t)
        self.arrived(self.piece(a, src, 0, 0), self.sems[1].at[a, src])
        to = jnp.where(z > src, z + 1, z - 1)
        self.z_send(a, src, src, to, (to >= 0) & (to <= 3))
        self.side_sends(a, src)
        if t == 3:
            self.core_send(a, 0, 0, 0)

    def p_step(self, a, t):
        src = self.p.order(t)
        ts, tr = self.sems[4], self.sems[5]
        self.arrived(self.piece(a, src, 1, 0), self.sems[3].at[a, src])
        self.go(self.piece(a, src, 1, 0), ts.at[a, 4 + src], tr.at[a, 4 + src], self.p.third)
        if t == 3:
            self.core_send(a, 1, 1, 0)

    def t_step(self, a, side):
        for t in range(4):
            src = self.p.order(t)
            self.arrived(self.piece(a, src, side, 1), self.sems[5].at[a, side * 4 + src])
        self.core_send(a, 2 + side, side, 1)

    def front(self, a):
        for t in range(4):
            if t:
                self.z_step(a, t)
            if t:
                self.p_step(a, t - 1)
        self.p_step(a, 3)

    def core_wait(self, a):
        for k, (side, far) in enumerate(((0, 0), (1, 0), (0, 1), (1, 1))):
            self.arrived(self.piece(a, None, side, far, True), self.sems[7].at[a, k])

    def finish(self):
        for copy, when in self.sent:
            if when is None:
                copy.wait_send()
            else:
                pl.when(when)(copy.wait_send)


def gather_sems(chunks):
    sizes = (5, 4, 4, 4, 8, 8, 4, 4)
    return [pltpu.SemaphoreType.DMA((chunks, n)) for n in sizes]


def overlaps(rows, length):
    pairs = []
    for m in range(3):
        edge = (m + 1) * rows
        low = edge // length * length
        if low == edge:
            continue
        pairs.append((m, m + 1, max(low, m * rows), edge))
        pairs.append((m + 1, m, edge, min(low + length, edge + rows)))
    return pairs


class Share:
    def __init__(self, place, pairs, src, dst, sems):
        self.p, self.pairs, self.src, self.dst, self.sems = place, pairs, src, dst, sems

    def copy(self, pair):
        source, target, low, high = pair
        k = 0 if source < target else 1
        return remote(self.src(low, high, target), self.dst(low, high, target), self.sems.at[k], self.sems.at[2 + k], self.p.mate(target))

    def start(self):
        for pair in self.pairs:
            pl.when(self.p.m == pair[0])(self.copy(pair).start)

    def wait_recv(self):
        for pair in self.pairs:
            pl.when(self.p.m == pair[1])(self.copy(pair).wait_recv)

    def wait_send(self):
        for pair in self.pairs:
            pl.when(self.p.m == pair[0])(self.copy(pair).wait_send)


class Sum5:
    def __init__(self, place, table, slots, sems):
        self.p, self.table, self.slots, self.sems = place, table, slots, sems
        z = place.z
        self.peers = [
            place.at(z=z + 1 - 2 * lax.rem(z, 2)),
            place.at(z=z + 2 - 4 * (z // 2)),
            place.at(x=1 - place.x),
            place.at(y=1 - place.y),
            place.sib,
        ]

    def copy(self, k):
        return remote(self.slots.at[5 + k], self.slots.at[k], self.sems.at[k], self.sems.at[5 + k], self.peers[k])

    def start(self, k):
        self.slots[5 + k] = self.table[...]
        self.copy(k).start()

    def end(self, k):
        self.copy(k).wait_recv()
        self.table[...] = self.table[...] + self.slots[k]

    def finish(self):
        for k in range(5):
            self.copy(k).wait_send()


class Scatter:
    def __init__(self, place, g, chunks, rc, r3, r2, ru, rd, sems, emit):
        self.p, self.g, self.chunks = place, g, chunks
        self.rc, self.r3, self.r2, self.ru, self.rd = rc, r3, r2, ru, rd
        self.sems = sems
        self.emit = emit
        self.width = g.shape[4] // 4
        self.sent = []

    def cols(self, j, y, c):
        a, low, w = self.chunks[j]
        return pl.ds(pl.multiple_of((y * 2 + c) * self.width + low, 128), w)

    def region(self, j, side, far, core=False):
        x, y = self.p.line(side, far, core)
        c = 1 - self.p.c if core else self.p.c
        return (self.chunks[j][0], slice(None), x, slice(None), self.cols(j, y, c))

    def go(self, src, dst, send, recv, device, when=None):
        copy = remote(src, dst, send, recv, device)
        if when is None:
            copy.start()
        else:
            pl.when(when)(copy.start)
        self.sent.append((copy, when))

    def arrived(self, ref, recv):
        remote(ref, ref, recv, recv, self.p.sib).wait_recv()

    def core_start(self, j):
        cs, cr = self.sems[0], self.sems[1]
        for far in (1, 0):
            for side in (1, 0):
                k = far * 2 + side
                self.go(
                    self.g.at[self.region(j, side, far, True)], self.rc.at[j, k], cs.at[j, k], cr.at[j, k], self.p.sib
                )

    def add(self, j, side, far, other):
        a, z, x, r, cols = self.region(j, side, far)

        def step(k):
            here = self.g[a, k, x, :, cols].astype(F32)
            self.g[a, k, x, :, cols] = (here + other(k).astype(F32)).astype(BF16)

        pl.loop(0, 4)(step)

    def core_end(self, j):
        ts, tr = self.sems[2], self.sems[3]
        for far in (1, 0):
            for side in (1, 0):
                k = far * 2 + side
                self.arrived(self.rc.at[j, k], self.sems[1].at[j, k])
                self.add(j, side, far, lambda q, k=k: self.rc[j, k, q])
                if far == 1:
                    self.go(
                        self.g.at[self.region(j, side, 1)], self.r3.at[j, side], ts.at[j, side], tr.at[j, side], self.p.third
                    )

    def third_end(self, j):
        ps, pr = self.sems[4], self.sems[5]
        for side in (1, 0):
            self.arrived(self.r3.at[j, side], self.sems[3].at[j, side])
            self.add(j, side, 0, lambda q, side=side: self.r3[j, side, q])
            if side == 1:
                self.go(self.g.at[self.region(j, 1, 0)], self.r2.at[j], ps.at[j], pr.at[j], self.p.second)

    def line_ref(self, j, z):
        a, _, x, r, cols = self.region(j, 0, 0)
        return self.g.at[a, z, x, r, cols]

    def up(self, j, d, when):
        us, ur = self.sems[6], self.sems[7]
        self.go(self.line_ref(j, d), self.ru.at[j, d], us.at[j, d], ur.at[j, d], self.p.at(z=self.p.z + 1), when)

    def down(self, j, d, when):
        ds, dr = self.sems[8], self.sems[9]
        self.go(self.line_ref(j, d), self.rd.at[j, d], ds.at[j, d], dr.at[j, d], self.p.at(z=self.p.z - 1), when)

    def second_end(self, j):
        z = self.p.z
        self.arrived(self.r2.at[j], self.sems[5].at[j])
        self.add(j, 0, 0, lambda q: self.r2[j, q])
        for d in range(3):
            self.up(j, 3 - d, z == 0)
            self.down(j, d, z == 3)

    def relay(self, j, d, buf, recv, when, send):
        def run():
            self.arrived(buf.at[j, d], recv.at[j, d])
            ref = self.line_ref(j, d)
            ref[...] = (ref[...].astype(F32) + buf[j, d].astype(F32)).astype(BF16)

        pl.when(when)(run)
        send(j, d, when)

    def z_step(self, j, t):
        z = self.p.z
        up, down = 3 - t, t
        if up >= 2:
            self.relay(j, up, self.ru, self.sems[7], (z > 0) & (z < up), self.up)
        if down <= 1:
            self.relay(j, down, self.rd, self.sems[9], (z < 3) & (z > down), self.down)

    def last(self, j):
        z = self.p.z
        a, low, w = self.chunks[j]
        x, y = self.p.x, self.p.y
        total = self.g[a, z, x, :, self.cols(j, y, self.p.c)].astype(F32)
        self.emit(j, total, True)

        def from_below():
            self.arrived(self.ru.at[j, z], self.sems[7].at[j, z])
            self.emit(j, self.ru[j, z].astype(F32), False)

        def from_above():
            self.arrived(self.rd.at[j, z], self.sems[9].at[j, z])
            self.emit(j, self.rd[j, z].astype(F32), False)

        pl.when(z > 0)(from_below)
        pl.when(z < 3)(from_above)

    def finish(self):
        for copy, when in self.sent:
            if when is None:
                copy.wait_send()
            else:
                pl.when(when)(copy.wait_send)


def scatter_scratch(chunks, rows):
    n = len(chunks)
    w = chunks[0][2]
    return [
        pltpu.VMEM((n, 4, 4, rows, w), BF16),
        pltpu.VMEM((n, 2, 4, rows, w), BF16),
        pltpu.VMEM((n, 4, rows, w), BF16),
        pltpu.VMEM((n, 4, rows, w), BF16),
        pltpu.VMEM((n, 4, rows, w), BF16),
    ], [
        pltpu.SemaphoreType.DMA(s)
        for s in ((n, 4), (n, 4), (n, 2), (n, 2), (n,), (n,), (n, 4), (n, 4), (n, 4), (n, 4))
    ]


def pipeline(stages, count):
    for step in range(count + len(stages) - 1):
        for s in range(len(stages)):
            j = step - s
            if 0 <= j < count:
                stages[s](j)


def nt(a, b):
    return lax.dot_general(a, b, (((1,), (1,)), ((), ())), preferred_element_type=F32)


def tn(a, b):
    return lax.dot_general(a, b, (((0,), (0,)), ((), ())), preferred_element_type=F32)


def nn(a, b):
    return jnp.dot(a, b, preferred_element_type=F32)


def even_lanes(shape):
    return lax.broadcasted_iota(jnp.int32, shape, 1) < HD


def keep(values, even):
    mask = even_lanes(values.shape)
    zero = jnp.zeros_like(values)
    return jnp.where(mask, values, zero) if even else jnp.where(mask, zero, values)


def col_sum(values):
    return jnp.sum(values, 0, keepdims=True)


class Layer:
    def __init__(self, refs, place):
        self.__dict__.update(refs)
        self.p = place
        self.rows, self.width = self.tok.shape
        self.length = self.seg.shape[1]
        self.blocks = self.rows // 128
        self.cols = self.g.shape[4] // 4
        self.hidden = self.g.shape[4]
        self.s0 = self.rows * place.m // self.length
        self.s1 = (self.rows * place.m + self.rows - 1) // self.length
        self.window = self.kv.shape[1]

    def w(self, a, low, size):
        return self.g[a, :, :, :, pl.ds(pl.multiple_of(low, 128), size)].reshape(self.width, size)

    def put(self, a, low, value):
        size = value.shape[1]
        shape = self.g.shape[1:4] + (size,)
        self.g[a, :, :, :, pl.ds(pl.multiple_of(low, 128), size)] = value.astype(BF16).reshape(shape)

    def gain(self, row):
        return self.tab[pl.ds(row, 1), :]

    def blk(self, i):
        return pl.ds(pl.multiple_of(i * 128, 128), 128)

    def seq_of(self, i):
        return (self.rows * self.p.m + 128 * i) // self.length

    def each_seq(self, run):
        for s in range(self.window):
            if s == 0:
                run(s)
            else:
                pl.when(self.s0 + s <= self.s1)(functools.partial(run, s))

    def masks(self):
        n = self.length
        for i in range(self.blocks):
            s = self.seq_of(i)
            at = lax.rem(self.rows * self.p.m + 128 * i, n)
            seg = self.seg[pl.ds(s, 1), :]
            grp = self.grp[pl.ds(s, 1), :]
            ans = self.ans[pl.ds(s, 1), :]
            seg_q = pick(at // 128, [seg[:, k : k + 128] for k in range(0, n, 128)])
            grp_q = pick(at // 128, [grp[:, k : k + 128] for k in range(0, n, 128)])
            code = jnp.where(seg_q == 0, -1, grp_q).astype(F32)
            code = jnp.transpose(jnp.broadcast_to(code, (8, 128)))[:, :1]
            open_key = (seg == 0) | (ans == 1)
            rule = (code == grp.astype(F32)) | (code < 0.0) | open_key
            position = lax.broadcasted_iota(jnp.int32, (1, n), 1)
            seen = rule & (position < self.pad[s])
            self.bias[i] = jnp.where(seen, 0.0, mask_fill)

    def project(self):
        c = self.cols

        @pl.loop(0, 4)
        def _(b):
            row = self.tab[pl.ds(6 + b, 1), :]
            lanes = lax.broadcasted_iota(jnp.int32, (1, 256), 1) < c // 4
            q = nn(self.tok[...], self.w(ATT, b * c, 256)) + row[:, :256]
            self.q[b] = jnp.where(lanes, q * score_scale, 0.0).astype(BF16)
            wkv = self.w(ATT, b * c + c // 2, c // 2)

            def one(s):
                kv = nn(self.tokw[s], wkv) + row[:, c // 2 :]
                self.kv[b, s] = kv.astype(BF16)

            self.each_seq(one)

    def heads(self, b, i):
        s = self.seq_of(i) - self.s0
        q0 = self.q[b, self.blk(i), :128]
        q2 = self.q[b, self.blk(i), 128:]
        return s, keep(q0, True), keep(q0, False), q2

    def attend(self):
        @pl.loop(0, 4 * self.blocks)
        def _(k):
            b, i = k // self.blocks, lax.rem(k, self.blocks)
            s, q0, q1, q2 = self.heads(b, i)
            bias = self.bias[i]

            def softmax(scores):
                scores = scores + bias
                e = jnp.exp(scores - jnp.max(scores, -1, keepdims=True))
                return (e * (1.0 / jnp.sum(e, -1, keepdims=True))).astype(BF16)

            t0, t1, t2 = (self.kv[b, s, :, 128 * t : 128 * t + 128] for t in range(3))
            s01 = nt(jnp.concatenate([q0, q1], 0), t0)
            p0, p1, p2 = softmax(s01[:128]), softmax(s01[128:]), softmax(nt(q2, t1))
            self.shares[b, i, 0] = p0
            self.shares[b, i, 1] = p1
            self.shares[b, i, 2] = p2
            o12 = nn(jnp.concatenate([p1, p2], 0), t2)
            self.o[b, self.blk(i), :128] = keep(nn(p0, t1), False).astype(BF16)
            self.o[b, self.blk(i), 128:] = jnp.where(even_lanes((128, 128)), o12[:128], o12[128:]).astype(BF16)

    def row_loop(self, step, sums):
        n = 48

        def run(k, carry):
            at = pl.ds(pl.multiple_of(k * n, n), n)
            return step(at, carry)

        zero = tuple(jnp.zeros((1, self.width), F32) for _ in range(sums))
        return lax.fori_loop(0, self.rows // n, run, zero)

    def first_norm(self):
        self.acc[...] = jnp.zeros_like(self.acc)

        @pl.loop(0, 4)
        def _(b):
            self.acc[...] += nt(self.o[b], self.w(ATT, b * self.cols + 128, 256))

        g1, b1, co = self.gain(0), self.gain(1), self.gain(2)

        def step(at, carry):
            r = self.tok[at, :].astype(F32) + (self.acc[at, :] + co)
            r = r - jnp.mean(r, -1, keepdims=True)
            rs = lax.rsqrt(jnp.mean(r * r, -1, keepdims=True) + norm_epsilon)
            xh = r * rs
            self.xh[at, :] = xh
            self.rs[at, :] = rs
            self.hb[at, :] = (xh * g1 + b1).astype(BF16)
            return carry

        self.row_loop(step, 0)

    def up(self):
        n = 256

        def part(b, k):
            low = pl.multiple_of(b * self.cols + k, n)
            u = nn(self.hb[...], self.w(UP, low, n)) + self.tab[pl.ds(10 + b, 1), k : k + n]
            share = 0.5 + 0.5 * lax.erf(u * np.float32(np.sqrt(0.5)))
            slope = share + u * (jnp.exp(-0.5 * (u * u)) * np.float32(1 / np.sqrt(2 * np.pi)))
            self.act[:, pl.ds(low, n)] = (u * share).astype(BF16)
            self.slope[:, pl.ds(low, n)] = slope.astype(BF16)

        self.hidden_loop(part, n)

    def hidden_loop(self, part, n):
        @pl.loop(0, 4)
        def _(b):
            for k in range(0, self.cols, n):
                part(b, k)

    def long_nt(self, left, a):
        n = 512

        @pl.loop(0, self.hidden // n)
        def _(j):
            low = pl.multiple_of(j * n, n)
            self.acc[...] += nt(left[:, pl.ds(low, n)], self.w(a, low, n))

    def second_norm(self):
        self.acc[...] = jnp.zeros_like(self.acc)
        self.long_nt(self.act, DOWN)
        g1, b1, g2, b2, cd = self.gain(0), self.gain(1), self.gain(3), self.gain(4), self.gain(5)

        def step(at, carry):
            r = (self.xh[at, :] * g1 + b1) + (self.acc[at, :] + cd)
            r = r - jnp.mean(r, -1, keepdims=True)
            rs = lax.rsqrt(jnp.mean(r * r, -1, keepdims=True) + norm_epsilon)
            xh = r * rs
            self.block_out[at, :] = (xh * g2 + b2).astype(BF16)
            grad = self.out_grad[at, :].astype(F32)
            inner = grad * g2
            back = rs * (inner - jnp.mean(inner, -1, keepdims=True) - xh * jnp.mean(inner * xh, -1, keepdims=True))
            self.acc[at, :] = back
            low = back.astype(BF16)
            self.dz[at, :] = low
            return carry[0] + col_sum(grad * xh), carry[1] + col_sum(grad), carry[2] + col_sum(low.astype(F32))

        dg, db, dc = self.row_loop(step, 3)
        self.sums[3:4, :] = dg
        self.sums[4:5, :] = db
        self.sums[5:6, :] = dc

    def hidden_back(self):
        n = 256

        def part(b, k):
            low = pl.multiple_of(b * self.cols + k, n)
            at = pl.ds(low, n)
            du = (nn(self.dz[...], self.w(DOWN, low, n)) * self.slope[:, at].astype(F32)).astype(BF16)
            self.slope[:, at] = du
            self.sums[pl.ds(10 + b, 1), k : k + n] = col_sum(du.astype(F32))

        self.hidden_loop(part, n)

    def weight_grad(self, a, left, right):
        n = 256
        self.turned[...] = left[...].T

        @pl.loop(0, self.hidden // n)
        def _(j):
            low = pl.multiple_of(j * n, n)
            self.put(a, low, nn(self.turned[...], right[:, pl.ds(low, n)]))

    def first_back(self):
        self.long_nt(self.slope, UP)
        g1 = self.gain(0)

        def step(at, carry):
            grad = self.acc[at, :]
            xh = self.xh[at, :]
            inner = grad * g1
            back = self.rs[at, :] * (
                inner - jnp.mean(inner, -1, keepdims=True) - xh * jnp.mean(inner * xh, -1, keepdims=True)
            )
            self.acc[at, :] = back
            low = back.astype(BF16)
            self.dz[at, :] = low
            return carry[0] + col_sum(grad * xh), carry[1] + col_sum(grad), carry[2] + col_sum(low.astype(F32))

        dg, db, dc = self.row_loop(step, 3)
        self.sums[0:1, :] = dg
        self.sums[1:2, :] = db
        self.sums[2:3, :] = dc

    def attend_back(self):
        c = self.cols

        @pl.loop(0, 4)
        def _(b):
            do = nn(self.dz[...], self.w(ATT, b * c + 128, 256))
            lanes = lax.broadcasted_iota(jnp.int32, (1, 256), 1) >= HD
            self.do[...] = jnp.where(lanes, do, 0.0).astype(BF16)
            self.dkv_acc[...] = jnp.zeros_like(self.dkv_acc)

            @pl.loop(0, self.blocks)
            def _(i):
                s, q0, q1, q2 = self.heads(b, i)
                t0, t1, t2 = (self.kv[b, s, :, 128 * t : 128 * t + 128] for t in range(3))
                do0 = self.do[self.blk(i), :128]
                do12 = self.do[self.blk(i), 128:]
                do1, do2 = keep(do12, True), keep(do12, False)
                dp12 = nt(jnp.concatenate([do1, do2], 0), t2)

                def back(h, dp):
                    low = self.shares[b, i, h]
                    p = low.astype(F32)
                    scaled = p * dp
                    return low, (scaled - p * jnp.sum(scaled, -1, keepdims=True)).astype(BF16)

                p0, ds0 = back(0, nt(do0, t1))
                p1, ds1 = back(1, dp12[:128])
                p2, ds2 = back(2, dp12[128:])
                dq01 = nn(jnp.concatenate([ds0, ds1], 0), t0)
                dq0 = jnp.where(even_lanes((128, 128)), dq01[:128], dq01[128:])
                dq2 = keep(nn(ds2, t1), True)
                self.q[b, self.blk(i), :128] = (dq0 * score_scale).astype(BF16)
                self.q[b, self.blk(i), 128:] = (dq2 * score_scale).astype(BF16)
                rows = jnp.concatenate
                self.dkv_acc[s, :, :128] += tn(rows([ds0, ds1], 0), rows([q0, q1], 0))
                self.dkv_acc[s, :, 128:256] += tn(rows([ds2, p0], 0), rows([q2, do0], 0))
                self.dkv_acc[s, :, 256:] += tn(rows([p1, p2], 0), rows([do1, do2], 0))

            total = jnp.zeros((1, c // 2), F32)
            for s in range(self.window):
                low = self.dkv_acc[s].astype(BF16)
                self.kv[b, s] = low
                total = total + col_sum(low.astype(F32))
            first = col_sum(self.q[b].astype(F32))
            gap = jnp.zeros((1, c // 2 - 256), F32)
            self.sums[pl.ds(6 + b, 1), :] = jnp.concatenate([first, gap, total], 1)

    def input_back(self):
        c, half = self.cols, self.width // 2

        @pl.loop(0, 4)
        def _(b):
            self.acc[...] += nt(self.q[b], self.w(ATT, b * c, 256))

        def one(s):
            self.dkv_acc[...] = jnp.zeros_like(self.dkv_acc)

            @pl.loop(0, 4)
            def _(b):
                w = self.w(ATT, b * c + c // 2, c // 2)
                for k in range(2):
                    self.dkv_acc[k] += nt(self.kv[b, s], w[k * half : k * half + half])

            for k in range(2):
                self.xw[s, :, k * half : k * half + half] = self.dkv_acc[k].astype(BF16)

        self.each_seq(one)

    def attention_grads(self):
        c = self.cols
        self.turned[...] = self.tok[...].T
        self.turned2[...] = self.dz[...].T

        def turn(s):
            self.turnedw[s] = self.tokw[s].T

        self.each_seq(turn)

        @pl.loop(0, 4)
        def _(b):
            dq = nn(self.turned[...], self.q[b])
            do = nn(self.turned2[...], self.o[b])
            self.put(ATT, b * c, dq[:, :128])
            self.put(ATT, b * c + 128, dq[:, 128:] + do[:, :128])
            self.put(ATT, b * c + 256, do[:, 128:])

            def finish(count):
                total = nn(self.turnedw[0], self.kv[b, 0])
                for s in range(1, count):
                    total = total + nn(self.turnedw[s], self.kv[b, s])
                self.put(ATT, b * c + c // 2, total)

            for count in range(1, self.window + 1):
                pl.when(self.s1 - self.s0 + 1 == count)(functools.partial(finish, count))


CHUNKS = 2


def gather_chunks(cols):
    w = cols // CHUNKS
    return [(a, k * w, w) for a in (ATT, UP, DOWN) for k in range(CHUNKS)]


def scatter_chunks(cols):
    w = cols // CHUNKS
    return [(a, k * w, w) for a in (DOWN, UP, ATT) for k in range(CHUNKS)]


INPUTS = ("shard", "small", "tok", "out_grad", "seg", "grp", "ans", "pad")
OUTPUTS = ("block_out", "input_grad", "owned", "total")


def kernel(names, chunks, back_chunks, pairs, *refs):
    r = dict(zip(names, refs))
    pc = Place()
    gather = Gather(pc, r["g"], chunks, [r["gs%d" % k] for k in range(8)])
    r["table"][...] = r["small"][...]
    for j, (a, low, w) in enumerate(chunks):
        ref = gather.piece(j, pc.z, 0, 0)
        ref[...] = r["shard"][a, :, low : low + w]
    layer = Layer(r, pc)
    rows = layer.rows
    greet(pc, True)
    tok, tokw = r["tok"], r["tokw"]

    share = Share(
        pc,
        pairs,
        lambda low, high, target: tok.at[pl.ds(low % rows, high - low)],
        lambda low, high, target: tokw.at[in_window(low, high, target, rows, layer.length)],
        r["share_sems"],
    )
    spread = Sum5(pc, r["table"], r["table_slots"], r["table_sems"])
    spread.start(0)
    share.start()
    for m in range(4):

        def own_tokens(m=m):
            for at, where in own_parts(m, rows, layer.length):
                tokw[where[0], where[1], :] = tok[at, :]

        pl.when(pc.m == m)(own_tokens)
    layer.masks()
    n = len(chunks)
    gather.own(0)
    gather.own(1)
    for j in range(n + 1):
        if j < n:
            gather.front(j)
            if j + 2 < n:
                gather.own(j + 2)
        if j < 5:
            spread.end(j)
            if j < 4:
                spread.start(j + 1)
        if j >= 1:
            gather.t_step(j - 1, 0)
            gather.t_step(j - 1, 1)
        if j >= 2:
            gather.core_wait(j - 2)
    gather.core_wait(n - 1)
    share.wait_recv()
    gather.finish()
    share.wait_send()
    spread.finish()

    r["tab"][...] = r["table"][...].astype(F32)
    layer.project()
    layer.attend()
    layer.first_norm()
    layer.up()
    layer.second_norm()
    layer.hidden_back()
    layer.weight_grad(DOWN, r["dz"], r["act"])
    layer.first_back()
    layer.weight_grad(UP, r["hb"], r["slope"])
    layer.attend_back()
    layer.input_back()

    window = r["xw"]

    xr = r["xrecv"]
    homes = [(t, s, low, high) for s, t, low, high in pairs]

    def home_copy(pair):
        k = 0 if pair[0] < pair[1] else 1
        size = pair[3] - pair[2]
        return remote(
            window.at[in_window(pair[2], pair[3], pair[0], rows, layer.length)],
            xr.at[k, pl.ds(0, size)],
            r["home_sems"].at[k],
            r["home_sems"].at[2 + k],
            pc.mate(pair[1]),
        )

    for pair in homes:
        pl.when(pc.m == pair[0])(home_copy(pair).start)
    layer.attention_grads()

    owned = r["owned"]

    def emit(j, value, first):
        a, low, w = back_chunks[j]
        if first:
            owned[a, :, low : low + w] = value
        else:
            owned[a, :, low : low + w] += value

    sc = Scatter(pc, r["g"], back_chunks, r["rc"], r["r3"], r["r2"], r["ru"], r["rd"], [r["ss%d" % k] for k in range(10)], emit)
    pipeline(
        [sc.core_start, sc.core_end, sc.third_end, sc.second_end, lambda j: sc.z_step(j, 0), lambda j: sc.z_step(j, 1), sc.last],
        len(back_chunks),
    )

    for m in range(4):

        def own_rows(m=m):
            for at, where in own_parts(m, rows, layer.length):
                r["acc"][at, :] += window[where[0], where[1], :].astype(F32)

        pl.when(pc.m == m)(own_rows)
    for pair in homes:

        def take(pair=pair):
            home_copy(pair).wait_recv()
            k = 0 if pair[0] < pair[1] else 1
            low, high = pair[2] - pair[1] * rows, pair[3] - pair[1] * rows
            r["acc"][low:high, :] += xr[k, : high - low, :].astype(F32)

        pl.when(pc.m == pair[1])(take)
    r["input_grad"][...] = r["acc"][...].astype(BF16)

    sums = r["sums"]
    squares = jnp.zeros((1, owned.shape[2]), F32)
    for a in range(3):
        squares = squares + col_sum(owned[a] * owned[a])
    sums[14:15, :] = squares
    sums[15:16, :] = jnp.zeros_like(squares)
    total = Sum5(pc, sums, r["sum_slots"], r["sum_sems"])
    for k in range(5):
        total.start(k)
        total.end(k)
    r["total"][...] = sums[...]
    for pair in homes:
        pl.when(pc.m == pair[0])(home_copy(pair).wait_send)
    sc.finish()
    total.finish()


def in_window(low, high, m, rows, length):
    return low // length - m * rows // length, pl.ds(low % length, high - low)


def own_parts(m, rows, length):
    parts, low = [], m * rows
    while low < (m + 1) * rows:
        high = min((m + 1) * rows, (low // length + 1) * length)
        parts.append((slice(low - m * rows, high - m * rows), in_window(low, high, m, rows, length)))
        low = high
    return parts


def run_layer(shard, small, tok, out_grad, seg, grp, ans, pad):
    _, per, cols = shard.shape
    rows, width = tok.shape
    length = seg.shape[1]
    hidden = 4 * cols
    window = max((m * rows + rows - 1) // length - m * rows // length + 1 for m in range(4))
    blocks = rows // 128
    pairs = overlaps(rows, length)
    chunks, back_chunks = gather_chunks(cols), scatter_chunks(cols)
    most = max(high - low for _, _, low, high in pairs)
    bufs, sems = scatter_scratch(back_chunks, per)
    scratch = {
        "g": pltpu.VMEM((3, 4, 2, per, hidden), BF16),
        "table": pltpu.VMEM((16, width), BF16),
        "tab": pltpu.VMEM((16, width), F32),
        "table_slots": pltpu.VMEM((10, 16, width), BF16),
        "tokw": pltpu.VMEM((window, length, width), BF16),
        "bias": pltpu.VMEM((blocks, 128, length), F32),
        "q": pltpu.VMEM((4, rows, 256), BF16),
        "kv": pltpu.VMEM((4, window, length, cols // 2), BF16),
        "shares": pltpu.VMEM((4, blocks, 3, 128, length), BF16),
        "o": pltpu.VMEM((4, rows, 256), BF16),
        "do": pltpu.VMEM((rows, 256), BF16),
        "dkv_acc": pltpu.VMEM((window, length, cols // 2), F32),
        "acc": pltpu.VMEM((rows, width), F32),
        "xh": pltpu.VMEM((rows, width), F32),
        "rs": pltpu.VMEM((rows, 1), F32),
        "hb": pltpu.VMEM((rows, width), BF16),
        "dz": pltpu.VMEM((rows, width), BF16),
        "act": pltpu.VMEM((rows, hidden), BF16),
        "slope": pltpu.VMEM((rows, hidden), BF16),
        "turned": pltpu.VMEM((width, rows), BF16),
        "turned2": pltpu.VMEM((width, rows), BF16),
        "turnedw": pltpu.VMEM((window, width, length), BF16),
        "xw": pltpu.VMEM((window, length, width), BF16),
        "xrecv": pltpu.VMEM((2, most, width), BF16),
        "sums": pltpu.VMEM((16, width), F32),
        "sum_slots": pltpu.VMEM((10, 16, width), F32),
        "share_sems": pltpu.SemaphoreType.DMA((4,)),
        "home_sems": pltpu.SemaphoreType.DMA((4,)),
        "table_sems": pltpu.SemaphoreType.DMA((10,)),
        "sum_sems": pltpu.SemaphoreType.DMA((10,)),
    }
    scratch.update(zip(("rc", "r3", "r2", "ru", "rd"), bufs))
    scratch.update(("gs%d" % k, s) for k, s in enumerate(gather_sems(len(chunks))))
    scratch.update(("ss%d" % k, s) for k, s in enumerate(sems))
    names = INPUTS + OUTPUTS + tuple(scratch)
    vmem = pl.BlockSpec(memory_space=pltpu.VMEM)
    return pl.pallas_call(
        functools.partial(kernel, names, chunks, back_chunks, pairs),
        out_shape=[
            jax.ShapeDtypeStruct((rows, width), BF16),
            jax.ShapeDtypeStruct((rows, width), BF16),
            jax.ShapeDtypeStruct((3, per, cols), F32),
            jax.ShapeDtypeStruct((16, width), F32),
        ],
        in_specs=[vmem] * 7 + [pl.BlockSpec(memory_space=pltpu.SMEM)],
        out_specs=[vmem] * 4,
        scratch_shapes=list(scratch.values()),
        compiler_params=pltpu.CompilerParams(collective_id=0, has_side_effects=True, vmem_limit_bytes=62 * 2**20),
        name="layer",
    )(shard, small, tok, out_grad, seg, grp, ans, pad)


def adam_update(weight, grad, first, second, factor, decayed, rate):
    clipped = grad * factor
    first_new = beta_first * first + (1.0 - beta_first) * clipped
    second_new = beta_second * second + (1.0 - beta_second) * clipped * clipped
    ratio = (
        first_new
        / (1.0 - beta_first**STEP)
        / (jnp.sqrt(second_new / (1.0 - beta_second**STEP)) + adam_epsilon)
    )
    if decayed:
        ratio = ratio + decay_rate * weight
    return (weight - rate * ratio, first_new, second_new)


def body(tokens, out_grad, segment_ids, group_ids, answer_ids, pad_lengths, *states):
    masters, firsts, seconds = states[:6], states[6:12], states[12:]
    qkv, out, up, down, norm, bias = [m.astype(BF16) for m in masters]
    inner = lax.axis_size("inner")
    place = lax.axis_index("outer") * inner + lax.axis_index("inner")
    mp = lax.axis_index("mp")
    width = tokens.shape[1]
    local = qkv.shape[2]
    attention = jnp.concatenate([qkv[0], out.T, qkv[1], qkv[2]], 1)
    shard = jnp.stack([attention, up, down.T])
    part = norm.shape[2]
    norm_rows = lax.dynamic_update_slice(jnp.zeros((6, width), BF16), norm[:, 0], (0, mp * local + place * part))
    columns = bias.shape[1] * inner * lax.axis_size("outer")
    line = lax.dynamic_update_slice(jnp.zeros((columns,), BF16), bias[0], (place * bias.shape[1],))
    line_att = jnp.concatenate([line[:local], jnp.zeros((2 * local,), BF16), line[local : 2 * local]])
    spread = jnp.arange(4)[:, None] == mp
    zero = jnp.zeros((), BF16)
    small = jnp.concatenate(
        [norm_rows, jnp.where(spread, line_att, zero), jnp.where(spread, line[2 * local :], zero), jnp.zeros((2, width), BF16)]
    )
    if inner > 1:
        shard = lax.all_gather(shard, "inner", axis=1, tiled=True)
        small = lax.psum(small, "inner")
    block_out, input_grad, owned, total = run_layer(
        shard, small, tokens, out_grad, segment_ids, group_ids, answer_ids, pad_lengths
    )
    squares = total[14]
    if inner > 1:
        owned = lax.psum_scatter(owned, "inner", scatter_dimension=1, tiled=True)
        total = lax.psum(total, "inner")
        squares = lax.psum(jnp.sum(owned * owned), ("outer", "inner", "mp"))
    small_rows = total[:14]
    table_sum = small_rows[:6]
    query_sum = small_rows[6:10, :local]
    value_sum = small_rows[6:10, 3 * local :]
    up_sum = small_rows[10:14]
    small_squares = sum(jnp.sum(v * v) for v in (table_sum, query_sum, value_sum, up_sum))
    grad_norm = jnp.sqrt(jnp.sum(squares) + small_squares)
    factor = jnp.minimum(1.0, clip_limit / grad_norm)
    line = jnp.concatenate([query_sum, value_sum, up_sum], 1)
    grads = [
        jnp.stack([owned[0, :, :local], owned[0, :, 2 * local : 3 * local], owned[0, :, 3 * local :]]),
        owned[0, :, local : 2 * local].T,
        owned[1],
        owned[2].T,
        lax.dynamic_slice(table_sum, (0, mp * local + place * part), (6, part))[:, None],
        lax.dynamic_slice(line, (mp, place * bias.shape[1]), (1, bias.shape[1])),
    ]
    updated = [
        adam_update(masters[k], grads[k], firsts[k], seconds[k], factor, k < 4, learn_rates[k]) for k in range(6)
    ]
    return (block_out, input_grad, grad_norm) + tuple(updated[k][part] for part in range(3) for k in range(6))


def solution(mesh):
    dp = mesh.shape["dp"]
    outer = 8
    grid = Mesh(mesh.devices.reshape(outer, dp // outer, mesh.shape["mp"]), ("outer", "inner", "mp"))
    d = ("outer", "inner")
    both = P(d + ("mp",), None)
    states = (P(None, d, "mp"), P("mp", d), P(d, "mp"), P("mp", d), P(None, "mp", d), P("mp", d))
    in_specs = (both, both, P(d, None), P(d, None), P(d, None), P(d)) + states * 3
    out_specs = (both, both, P()) + states * 3
    return jax.shard_map(body, mesh=grid, in_specs=in_specs, out_specs=out_specs, check_vma=False)
```

```python
import functools
import jax
import jax.numpy as jnp
import numpy as np
from jax import lax
from jax.sharding import Mesh, PartitionSpec as P
from jax.experimental import pallas as pl
from jax.experimental.pallas import tpu as pltpu

MESH = pl.DeviceIdType.MESH
F32 = jnp.float32
BF16 = jnp.bfloat16
HD = 64
STEP = 5

norm_epsilon = 1e-06
adam_epsilon = 1e-08
learn_rates = (0.02, 0.1, 0.02, 0.02, 0.5, 0.5)
beta_first = 0.5
beta_second = 0.5
decay_rate = 0.01
clip_limit = 0.05
mask_fill = -1000000000.0
score_scale = 0.125

ATT, UP, DOWN = 0, 1, 2


def pick(index, values):
    out = values[-1]
    for k in range(len(values) - 1):
        out = jnp.where(index == k, values[k], out)
    return out


class Place:
    def __init__(self):
        outer = lax.axis_index("outer")
        self.sub = lax.axis_index("inner")
        self.m = lax.axis_index("mp")
        self.z = outer // 2
        self.x = lax.rem(outer, 2)
        self.y = self.m // 2
        self.c = lax.rem(self.m, 2)
        self.first = self.c == 0
        self.sib = self.at(c=1 - self.c)
        x, y = self.line(1, 0)
        self.second = self.at(x=x, y=y)
        x, y = self.line(0, 1)
        self.third = self.at(x=x, y=y)

    def at(self, z=None, x=None, y=None, c=None):
        z = self.z if z is None else z
        x = self.x if x is None else x
        y = self.y if y is None else y
        c = self.c if c is None else c
        return (z * 2 + x, self.sub, y * 2 + c)

    def mate(self, m):
        return (self.z * 2 + self.x, self.sub, m)

    def line(self, side, far, other_core=False):
        first = (1 - self.c if other_core else self.c) == 0
        x = jnp.where(first, side, far)
        y = jnp.where(first, far, side)
        return self.x + x - 2 * self.x * x, self.y + y - 2 * self.y * y

    def order(self, t):
        return pick(self.z, [(0, 1, 2, 3), (1, 0, 3, 2), (2, 2, 1, 1), (3, 3, 0, 0)][t])


def remote(src, dst, send, recv, device):
    return pltpu.make_async_remote_copy(
        src_ref=src, dst_ref=dst, send_sem=send, recv_sem=recv, device_id=device, device_id_type=MESH
    )


def greet(place, mids):
    barrier = pltpu.get_barrier_semaphore()

    def hello(device):
        pl.semaphore_signal(barrier, inc=1, device_id=device, device_id_type=MESH)

    z = place.z
    hello(place.sib)
    hello(place.second)
    hello(place.third)
    hello(place.at(z=z + 2 - 4 * (z // 2)))
    pl.when(z > 0)(lambda: hello(place.at(z=z - 1)))
    pl.when(z < 3)(lambda: hello(place.at(z=z + 1)))
    count = 4 + jnp.where(z > 0, 1, 0) + jnp.where(z < 3, 1, 0)
    if mids:
        inside = (place.m == 1) | (place.m == 2)
        pl.when(inside)(lambda: hello((place.z * 2 + place.x, place.sub, 3 - place.m)))
        count = count + jnp.where(inside, 1, 0)
    pl.semaphore_wait(barrier, count)


class Gather:
    def __init__(self, place, g, chunks, sems):
        self.p, self.g, self.chunks = place, g, chunks
        self.zs, self.zr, self.ps, self.pr, self.ts, self.tr, self.cs, self.cr = sems
        self.width = g.shape[4] // 4
        self.sent = []

    def piece(self, j, z, side, far, core=False):
        x, y = self.p.line(side, far, core)
        c = 1 - self.p.c if core else self.p.c
        a, low, w, _ = self.chunks[j]
        cols = pl.ds(pl.multiple_of((y * 2 + c) * self.width + low, 128), w)
        if z is None:
            return self.g.at[a, :, x, :, cols]
        return self.g.at[a, z, x, :, cols]

    def go(self, ref, send, recv, device, when=None):
        copy = remote(ref, ref, send, recv, device)
        if when is None:
            copy.start()
        else:
            pl.when(when)(copy.start)
        self.sent.append((copy, when))

    def arrived(self, ref, recv):
        remote(ref, ref, recv, recv, self.p.sib).wait_recv()

    def z_send(self, j, side, src, index, to, when):
        self.go(self.piece(j, src, side, 0), self.zs.at[j, side, index], self.zr.at[j, side, src], self.p.at(z=to), when)

    def z_both(self, j, side):
        z = self.p.z
        self.z_send(j, side, z, z, z + 1, z < 3)
        self.z_send(j, side, z, 4, z - 1, z > 0)

    def third(self, j, side, src):
        k = side * 4 + src
        self.go(self.piece(j, src, side, 0), self.ts.at[j, k], self.tr.at[j, k], self.p.third)

    def second(self, j, src):
        self.go(self.piece(j, src, 0, 0), self.ps.at[j, src], self.pr.at[j, src], self.p.second)

    def to_sibling(self, j, side, far):
        k = side + 2 * far
        self.go(self.piece(j, None, side, far), self.cs.at[j, k], self.cr.at[j, k], self.p.sib)

    def own(self, j):
        self.second(j, self.p.z)
        self.z_both(j, 0)
        self.third(j, 0, self.p.z)

    def z_step(self, j, t, side=0):
        z = self.p.z
        src = self.p.order(t)
        self.arrived(self.piece(j, src, side, 0), self.zr.at[j, side, src])
        to = jnp.where(z > src, z + 1, z - 1)
        self.z_send(j, side, src, src, to, (to >= 0) & (to <= 3))
        if not self.chunks[j][3]:
            self.second(j, src)
        self.third(j, side, src)
        if t == 3:
            self.to_sibling(j, side, 0)

    def p_step(self, j, t):
        src = self.p.order(t)
        self.arrived(self.piece(j, src, 1, 0), self.pr.at[j, src])
        if self.chunks[j][3]:
            self.z_both(j, 1)
        self.third(j, 1, src)
        if t == 3:
            self.to_sibling(j, 1, 0)

    def t_step(self, j, side):
        for t in range(4):
            src = self.p.order(t)
            self.arrived(self.piece(j, src, side, 1), self.tr.at[j, side * 4 + src])
        self.to_sibling(j, side, 1)

    def core_wait(self, j):
        for k, (side, far) in enumerate(((0, 0), (1, 0), (0, 1), (1, 1))):
            self.arrived(self.piece(j, None, side, far, True), self.cr.at[j, k])

    def finish(self):
        for copy, when in self.sent:
            if when is None:
                copy.wait_send()
            else:
                pl.when(when)(copy.wait_send)
        self.sent = []


def gather_sems(chunks):
    sizes = ((2, 5), (2, 4), (4,), (4,), (8,), (8,), (4,), (4,))
    return [pltpu.SemaphoreType.DMA((chunks,) + n) for n in sizes]


def overlaps(rows, length):
    pairs = []
    for m in range(3):
        edge = (m + 1) * rows
        low = edge // length * length
        if low == edge:
            continue
        pairs.append((m, m + 1, max(low, m * rows), edge))
        pairs.append((m + 1, m, edge, min(low + length, edge + rows)))
    return pairs


class Share:
    def __init__(self, place, pairs, src, dst, sems):
        self.p, self.pairs, self.src, self.dst, self.sems = place, pairs, src, dst, sems

    def copy(self, pair):
        source, target, low, high = pair
        k = 0 if source < target else 1
        return remote(self.src(low, high, target), self.dst(low, high, target), self.sems.at[k], self.sems.at[2 + k], self.p.mate(target))

    def start(self):
        for pair in self.pairs:
            pl.when(self.p.m == pair[0])(self.copy(pair).start)

    def wait_recv(self):
        for pair in self.pairs:
            pl.when(self.p.m == pair[1])(self.copy(pair).wait_recv)

    def wait_send(self):
        for pair in self.pairs:
            pl.when(self.p.m == pair[0])(self.copy(pair).wait_send)


class Sum5:
    def __init__(self, place, table, slots, sems):
        self.p, self.table, self.slots, self.sems = place, table, slots, sems
        z = place.z
        self.peers = [
            place.at(z=z + 1 - 2 * lax.rem(z, 2)),
            place.at(z=z + 2 - 4 * (z // 2)),
            place.at(x=1 - place.x),
            place.at(y=1 - place.y),
            place.sib,
        ]

    def copy(self, k):
        return remote(self.slots.at[5 + k], self.slots.at[k], self.sems.at[k], self.sems.at[5 + k], self.peers[k])

    def start(self, k):
        self.slots[5 + k] = self.table[...]
        self.copy(k).start()

    def end(self, k):
        self.copy(k).wait_recv()
        self.table[...] = self.table[...] + self.slots[k]

    def finish(self):
        for k in range(5):
            self.copy(k).wait_send()


class Scatter:
    def __init__(self, place, grads, chunks, rc, r3, r2, rz, sems, emit):
        self.p, self.grads, self.chunks = place, grads, chunks
        self.rc, self.r3, self.r2, self.rz = rc, r3, r2, rz
        self.cs, self.cr, self.ts, self.tr, self.ps, self.pr, self.us, self.ds, self.zr = sems
        self.emit = emit
        self.width = grads[0].shape[3] // 4
        self.sent = []
        self.seconds, self.lines, _, _ = scatter_slots(chunks)

    def region(self, j, side, far, core=False):
        x, y = self.p.line(side, far, core)
        c = 1 - self.p.c if core else self.p.c
        a, low, w, _ = self.chunks[j]
        return a, x, pl.ds(pl.multiple_of((y * 2 + c) * self.width + low, 128), w)

    def block(self, j, side, far, core=False):
        a, x, cols = self.region(j, side, far, core)
        return self.grads[a].at[:, x, :, cols]

    def shard(self, j, side, z):
        a, x, cols = self.region(j, side, 0)
        return self.grads[a].at[z, x, :, cols]

    def go(self, src, dst, send, recv, device, when=None):
        copy = remote(src, dst, send, recv, device)
        if when is None:
            copy.start()
        else:
            pl.when(when)(copy.start)
        self.sent.append((copy, when))

    def arrived(self, ref, recv):
        remote(ref, ref, recv, recv, self.p.sib).wait_recv()

    def core_start(self, j):
        for far in (1, 0):
            for side in (1, 0):
                k = far * 2 + side
                self.go(self.block(j, side, far, True), self.rc.at[j, k], self.cs.at[j, k], self.cr.at[j, k], self.p.sib)

    def add(self, j, side, far, other):
        a, x, cols = self.region(j, side, far)

        def step(k):
            here = self.grads[a].at[k, x, :, cols]
            here[...] = (here[...].astype(F32) + other[k].astype(F32)).astype(BF16)

        pl.loop(0, 4)(step)

    def core_end(self, j, far):
        for side in (1, 0):
            k = far * 2 + side
            self.arrived(self.rc.at[j, k], self.cr.at[j, k])
            self.add(j, side, far, self.rc.at[j, k])
            if far == 1:
                self.go(self.block(j, side, 1), self.r3.at[j, side], self.ts.at[j, side], self.tr.at[j, side], self.p.third)

    def third_end(self, j, side):
        self.arrived(self.r3.at[j, side], self.tr.at[j, side])
        self.add(j, side, 0, self.r3.at[j, side])
        if self.chunks[j][3]:
            self.line_start(j, side)
        elif side == 1:
            slot = self.r2.at[pl.ds(self.seconds[j], 4)]
            self.go(self.block(j, 1, 0), slot, self.ps.at[j], self.pr.at[j], self.p.second)

    def second_end(self, j):
        slot = self.r2.at[pl.ds(self.seconds[j], 4)]
        self.arrived(slot, self.pr.at[j])
        self.add(j, 0, 0, slot)
        self.line_start(j, 0)

    def up(self, j, side, d, when):
        n = self.lines[j] + side
        self.go(self.shard(j, side, d), self.rz.at[n, d], self.us.at[n, d], self.zr.at[n, d], self.p.at(z=self.p.z + 1), when)

    def down(self, j, side, d, when):
        n = self.lines[j] + side
        slot = jnp.where(d == self.p.z - 1, 4, d)
        self.go(self.shard(j, side, d), self.rz.at[n, slot], self.ds.at[n, d], self.zr.at[n, slot], self.p.at(z=self.p.z - 1), when)

    def line_start(self, j, side):
        z = self.p.z
        for d in range(3):
            self.up(j, side, 3 - d, z == 0)
            self.down(j, side, d, z == 3)

    def fold(self, j, side, d, slot):
        n = self.lines[j] + side
        self.arrived(self.rz.at[n, slot], self.zr.at[n, slot])
        ref = self.shard(j, side, d)
        ref[...] = (ref[...].astype(F32) + self.rz[n, slot].astype(F32)).astype(BF16)

    def relay(self, j, side, d, send, when):
        pl.when(when)(lambda: self.fold(j, side, d, d))
        send(j, side, d, when)

    def z_step(self, j, side, t):
        z = self.p.z
        if t < 2:
            self.relay(j, side, 3 - t, self.up, z == 1)
            self.relay(j, side, t, self.down, z == 2)
        else:
            self.relay(j, side, 3, self.up, z == 2)
            self.relay(j, side, 0, self.down, z == 1)

    def z_last(self, j, side):
        z = self.p.z
        pl.when(z > 0)(lambda: self.fold(j, side, z, z))
        pl.when(z < 3)(lambda: self.fold(j, side, z, 4))
        if side == 1:
            slot = self.r2.at[self.seconds[j]]
            self.go(self.shard(j, 1, z), slot, self.ps.at[j], self.pr.at[j], self.p.second)

    def last(self, j):
        z = self.p.z
        if self.chunks[j][3]:
            slot = self.r2.at[self.seconds[j]]
            self.arrived(slot, self.pr.at[j])
            self.emit(j, self.shard(j, 0, z)[...].astype(F32) + slot[...].astype(F32))
        else:
            self.z_last(j, 0)
            self.emit(j, self.shard(j, 0, z)[...].astype(F32))

    def finish(self):
        for copy, when in self.sent:
            if when is None:
                copy.wait_send()
            else:
                pl.when(when)(copy.wait_send)
        self.sent = []


def scatter_slots(chunks):
    seconds, lines, n, m = [], [], 0, 0
    for chunk in chunks:
        seconds.append(n)
        lines.append(m)
        n += 1 if chunk[3] else 4
        m += 2 if chunk[3] else 1
    return seconds, lines, n, m


def scatter_scratch(chunks, rows):
    n, w = len(chunks), chunks[0][2]
    _, _, seconds, lines = scatter_slots(chunks)
    shapes = ((n, 4, 4), (n, 2, 4), (seconds,), (lines, 5))
    sems = ((n, 4), (n, 4), (n, 2), (n, 2), (n,), (n,), (lines, 4), (lines, 4), (lines, 5))
    return [pltpu.VMEM(s + (rows, w), BF16) for s in shapes], [pltpu.SemaphoreType.DMA(s) for s in sems]


def nt(a, b):
    return lax.dot_general(a, b, (((1,), (1,)), ((), ())), preferred_element_type=F32)


def tn(a, b):
    return lax.dot_general(a, b, (((0,), (0,)), ((), ())), preferred_element_type=F32)


def nn(a, b):
    return jnp.dot(a, b, preferred_element_type=F32)


def even_lanes(shape):
    return lax.broadcasted_iota(jnp.int32, shape, 1) < HD


def keep(values, even):
    mask = even_lanes(values.shape)
    zero = jnp.zeros_like(values)
    return jnp.where(mask, values, zero) if even else jnp.where(mask, zero, values)


def col_sum(values):
    return jnp.sum(values, 0, keepdims=True)


class Layer:
    def __init__(self, refs, place):
        self.__dict__.update(refs)
        self.p = place
        self.rows, self.width = self.tok.shape
        self.length = self.seg.shape[1]
        self.blocks = self.rows // 128
        self.cols = self.g.shape[4] // 4
        self.hidden = self.g.shape[4]
        self.s0 = self.rows * place.m // self.length
        self.s1 = (self.rows * place.m + self.rows - 1) // self.length
        self.window = self.kv.shape[1]

    def w(self, a, low, size):
        return self.g[a, :, :, :, low : low + size].reshape(self.width, size)

    def put(self, ref, low, value):
        size = value.shape[1]
        ref[:, :, :, low : low + size] = value.astype(BF16).reshape(ref.shape[:3] + (size,))

    def gain(self, row):
        return self.tab[pl.ds(row, 1), :]

    def blk(self, i):
        return pl.ds(pl.multiple_of(i * 128, 128), 128)

    def seq_of(self, i):
        return (self.rows * self.p.m + 128 * i) // self.length

    def each_seq(self, run):
        for s in range(self.window):
            if s == 0:
                run(s)
            else:
                pl.when(self.s0 + s <= self.s1)(functools.partial(run, s))

    def masks(self):
        n = self.length
        for i in range(self.blocks):
            s = self.seq_of(i)
            at = lax.rem(self.rows * self.p.m + 128 * i, n)
            seg = self.seg[pl.ds(s, 1), :]
            grp = self.grp[pl.ds(s, 1), :]
            ans = self.ans[pl.ds(s, 1), :]
            seg_q = pick(at // 128, [seg[:, k : k + 128] for k in range(0, n, 128)])
            grp_q = pick(at // 128, [grp[:, k : k + 128] for k in range(0, n, 128)])
            code = jnp.where(seg_q == 0, -1, grp_q).astype(F32)
            code = jnp.transpose(jnp.broadcast_to(code, (8, 128)))[:, :1]
            open_key = (seg == 0) | (ans == 1)
            rule = (code == grp.astype(F32)) | (code < 0.0) | open_key
            position = lax.broadcasted_iota(jnp.int32, (1, n), 1)
            seen = rule & (position < self.pad[s])
            self.bias[i] = jnp.where(seen, 0.0, mask_fill)

    def queries(self, b):
        c = self.cols
        lanes = lax.broadcasted_iota(jnp.int32, (1, 256), 1) < c // 4
        q = nn(self.tok[...], self.w(ATT, b * c, 256)) + self.tab[6 + b : 7 + b, :256]
        self.q[b] = jnp.where(lanes, q * score_scale, 0.0).astype(BF16)

    def keys_values(self, b):
        c = self.cols
        wkv = self.w(ATT, b * c + c // 2, c // 2)

        def one(s):
            self.kv[b, s] = (nn(self.tokw[s], wkv) + self.tab[6 + b : 7 + b, c // 2 :]).astype(BF16)

        self.each_seq(one)

    def heads(self, b, i):
        s = self.seq_of(i) - self.s0
        q0 = self.q[b, self.blk(i), :128]
        q2 = self.q[b, self.blk(i), 128:]
        return s, keep(q0, True), keep(q0, False), q2

    def attend(self, b):
        @pl.loop(0, self.blocks)
        def _(i):
            s, q0, q1, q2 = self.heads(b, i)
            bias = self.bias[i]

            def softmax(scores):
                scores = scores + bias
                e = jnp.exp(scores - jnp.max(scores, -1, keepdims=True))
                return (e * (1.0 / jnp.sum(e, -1, keepdims=True))).astype(BF16)

            t0, t1, t2 = (self.kv[b, s, :, 128 * t : 128 * t + 128] for t in range(3))
            s01 = nt(jnp.concatenate([q0, q1], 0), t0)
            p0, p1, p2 = softmax(s01[:128]), softmax(s01[128:]), softmax(nt(q2, t1))
            self.shares[b, i, 0] = p0
            self.shares[b, i, 1] = p1
            self.shares[b, i, 2] = p2
            o12 = nn(jnp.concatenate([p1, p2], 0), t2)
            self.o[b, self.blk(i), :128] = keep(nn(p0, t1), False).astype(BF16)
            self.o[b, self.blk(i), 128:] = jnp.where(even_lanes((128, 128)), o12[:128], o12[128:]).astype(BF16)

    def row_loop(self, step, sums):
        n = 48

        def run(k, carry):
            at = pl.ds(pl.multiple_of(k * n, n), n)
            return step(at, carry)

        zero = tuple(jnp.zeros((1, self.width), F32) for _ in range(sums))
        return lax.fori_loop(0, self.rows // n, run, zero)

    def accumulate(self, value, first):
        self.acc[...] = value if first else self.acc[...] + value

    def branch(self, b):
        self.accumulate(nt(self.o[b], self.w(ATT, b * self.cols + 128, 256)), b == 0)

    def first_norm(self):
        g1, b1, co = self.gain(0), self.gain(1), self.gain(2)

        def step(at, carry):
            r = self.tok[at, :].astype(F32) + (self.acc[at, :] + co)
            r = r - jnp.mean(r, -1, keepdims=True)
            rs = lax.rsqrt(jnp.mean(r * r, -1, keepdims=True) + norm_epsilon)
            xh = r * rs
            self.xh[at, :] = xh
            self.rs[at, :] = rs
            self.hb[at, :] = (xh * g1 + b1).astype(BF16)
            return carry

        self.row_loop(step, 0)

    def half(self, b, k):
        n = self.cols // 2
        return b * self.cols + k * n, n

    def hidden_ref(self, which):
        return self.hid.at[2 * which : 2 * which + 2]

    def get_hidden(self, which, low, n):
        return self.hidden_ref(which)[:, :, :, low : low + n].reshape(self.rows, n)

    def set_hidden(self, which, low, value):
        ref = self.hidden_ref(which)
        ref[:, :, :, low : low + value.shape[1]] = value.astype(BF16).reshape(ref.shape[:3] + value.shape[1:])

    def up(self, b, k):
        low, n = self.half(b, k)
        u = nn(self.hb[...], self.w(UP, low, n)) + self.tab[10 + b : 11 + b, k * n : k * n + n]
        share = 0.5 + 0.5 * lax.erf(u * np.float32(np.sqrt(0.5)))
        self.set_hidden(0, low, u * share)
        self.set_hidden(1, low, share + u * (jnp.exp(-0.5 * (u * u)) * np.float32(1 / np.sqrt(2 * np.pi))))

    def down(self, b, k):
        low, n = self.half(b, k)
        self.accumulate(nt(self.get_hidden(0, low, n), self.w(DOWN, low, n)), b == 0 and k == 0)

    def second_norm(self):
        g1, b1, g2, b2, cd = self.gain(0), self.gain(1), self.gain(3), self.gain(4), self.gain(5)

        def step(at, carry):
            r = (self.xh[at, :] * g1 + b1) + (self.acc[at, :] + cd)
            r = r - jnp.mean(r, -1, keepdims=True)
            rs = lax.rsqrt(jnp.mean(r * r, -1, keepdims=True) + norm_epsilon)
            xh = r * rs
            self.block_out[at, :] = (xh * g2 + b2).astype(BF16)
            grad = self.out_grad[at, :].astype(F32)
            inner = grad * g2
            back = rs * (inner - jnp.mean(inner, -1, keepdims=True) - xh * jnp.mean(inner * xh, -1, keepdims=True))
            self.acc[at, :] = back
            low = back.astype(BF16)
            self.dz[at, :] = low
            return carry[0] + col_sum(grad * xh), carry[1] + col_sum(grad), carry[2] + col_sum(low.astype(F32))

        dg, db, dc = self.row_loop(step, 3)
        self.sums[3:4, :] = dg
        self.sums[4:5, :] = db
        self.sums[5:6, :] = dc

    def hidden_back(self, b, k):
        if b == 0 and k == 0:
            self.turned[...] = self.dz[...].T
        low, n = self.half(b, k)
        du = nn(self.dz[...], self.w(DOWN, low, n)) * self.get_hidden(1, low, n).astype(F32)
        du = du.astype(BF16)
        self.set_hidden(1, low, du)
        self.sums[10 + b : 11 + b, k * n : k * n + n] = col_sum(du.astype(F32))
        self.put(self.g.at[DOWN], low, nn(self.turned[...], self.get_hidden(0, low, n)))

    def up_back(self, b):
        low = b * self.cols
        self.acc[...] += nt(self.get_hidden(1, low, self.cols), self.w(UP, low, self.cols))

    def up_grad(self, b, k):
        if b == 0 and k == 0:
            self.turned[...] = self.hb[...].T
        low, n = self.half(b, k)
        self.put(self.g.at[UP], low, nn(self.turned[...], self.get_hidden(1, low, n)))

    def first_back(self):
        g1 = self.gain(0)

        def step(at, carry):
            grad = self.acc[at, :]
            xh = self.xh[at, :]
            inner = grad * g1
            back = self.rs[at, :] * (
                inner - jnp.mean(inner, -1, keepdims=True) - xh * jnp.mean(inner * xh, -1, keepdims=True)
            )
            self.acc[at, :] = back
            low = back.astype(BF16)
            self.dz[at, :] = low
            return carry[0] + col_sum(grad * xh), carry[1] + col_sum(grad), carry[2] + col_sum(low.astype(F32))

        dg, db, dc = self.row_loop(step, 3)
        self.sums[0:1, :] = dg
        self.sums[1:2, :] = db
        self.sums[2:3, :] = dc

    def mixed_back(self, b):
        do = nn(self.dz[...], self.w(ATT, b * self.cols + 128, 256))
        lanes = lax.broadcasted_iota(jnp.int32, (1, 256), 1) >= HD
        self.do[...] = jnp.where(lanes, do, 0.0).astype(BF16)
        self.dkv_acc[...] = jnp.zeros_like(self.dkv_acc)

    def attend_back(self, b, i):
        s, q0, q1, q2 = self.heads(b, i)
        t0, t1, t2 = (self.kv[b, s, :, 128 * t : 128 * t + 128] for t in range(3))
        do0 = self.do[self.blk(i), :128]
        do12 = self.do[self.blk(i), 128:]
        do1, do2 = keep(do12, True), keep(do12, False)
        dp12 = nt(jnp.concatenate([do1, do2], 0), t2)

        def back(h, dp):
            low = self.shares[b, i, h]
            p = low.astype(F32)
            scaled = p * dp
            return low, (scaled - p * jnp.sum(scaled, -1, keepdims=True)).astype(BF16)

        p0, ds0 = back(0, nt(do0, t1))
        p1, ds1 = back(1, dp12[:128])
        p2, ds2 = back(2, dp12[128:])
        dq01 = nn(jnp.concatenate([ds0, ds1], 0), t0)
        dq0 = jnp.where(even_lanes((128, 128)), dq01[:128], dq01[128:])
        dq2 = keep(nn(ds2, t1), True)
        self.q[b, self.blk(i), :128] = (dq0 * score_scale).astype(BF16)
        self.q[b, self.blk(i), 128:] = (dq2 * score_scale).astype(BF16)
        rows = jnp.concatenate
        self.dkv_acc[s, :, :128] += tn(rows([ds0, ds1], 0), rows([q0, q1], 0))
        self.dkv_acc[s, :, 128:256] += tn(rows([ds2, p0], 0), rows([q2, do0], 0))
        self.dkv_acc[s, :, 256:] += tn(rows([p1, p2], 0), rows([do1, do2], 0))

    def keys_back(self, b):
        c = self.cols
        total = jnp.zeros((1, c // 2), F32)
        for s in range(self.window):
            low = self.dkv_acc[s].astype(BF16)
            self.kv[b, s] = low
            total = total + col_sum(low.astype(F32))
        first = col_sum(self.q[b].astype(F32))
        gap = jnp.zeros((1, c // 2 - 256), F32)
        self.sums[6 + b : 7 + b, :] = jnp.concatenate([first, gap, total], 1)

    def turn(self):
        self.turned[...] = self.tok[...].T
        self.turned2[...] = self.dz[...].T

        def one(s):
            self.turnedw[s] = self.tokw[s].T

        self.each_seq(one)

    def attention_grad(self, b):
        c = self.cols
        dq = nn(self.turned[...], self.q[b])
        do = nn(self.turned2[...], self.o[b])
        self.put(self.hid, b * c, dq[:, :128])
        self.put(self.hid, b * c + 128, dq[:, 128:] + do[:, :128])
        self.put(self.hid, b * c + 256, do[:, 128:])

        def finish(count):
            total = nn(self.turnedw[0], self.kv[b, 0])
            for s in range(1, count):
                total = total + nn(self.turnedw[s], self.kv[b, s])
            self.put(self.hid, b * c + c // 2, total)

        for count in range(1, self.window + 1):
            pl.when(self.s1 - self.s0 + 1 == count)(functools.partial(finish, count))

    def query_input(self, b):
        self.acc[...] += nt(self.q[b], self.w(ATT, b * self.cols, 256))

    def window_input(self, s):
        c, half = self.cols, self.width // 2

        def run():
            for k in range(2):
                for b in range(4):
                    w = self.g[ATT, 2 * k : 2 * k + 2, :, :, b * c + c // 2 : b * c + c].reshape(half, c // 2)
                    part = nt(self.kv[b, s], w)
                    self.dkv_acc[k] = part if b == 0 else self.dkv_acc[k] + part
                self.xw[s, :, k * half : k * half + half] = self.dkv_acc[k].astype(BF16)

        if s == 0:
            run()
        else:
            pl.when(self.s0 + s <= self.s1)(run)


LONG = (False, True, True, False, True, True)
BACK_LONG = (False, False, False, False, False, True)


def chunks_of(order, cols, long):
    w = cols // 2
    return [(order[k // 2], k % 2 * w, w, long[k]) for k in range(6)]


ORDER = (
    ("own", 0), ("own", 1), ("share",), ("z", 0, 1, 0), ("own", 2), ("start",), ("masks",), ("sp", 0),
    ("sp", 1), ("p", 1, 0), ("z", 0, 2, 0), ("z", 2, 1, 0), ("z", 1, 1, 0), ("z", 1, 2, 0), ("z", 0, 3, 0),
    ("sp", 2), ("z", 1, 3, 0), ("z", 1, 1, 1), ("z", 1, 2, 1), ("z", 1, 3, 1), ("p", 0, 0), ("p", 0, 1),
    ("shared",), ("t", 0, 0), ("own", 3), ("p", 0, 2), ("p", 0, 3), ("p", 2, 0), ("own", 4), ("z", 2, 1, 1),
    ("z", 2, 2, 0), ("z", 2, 2, 1), ("sp", 3), ("sp", 4), ("z", 2, 3, 1), ("z", 2, 3, 0), ("own", 5),
    ("t", 0, 1), ("t", 1, 0), ("t", 1, 1), ("z", 3, 1, 0), ("z", 3, 2, 0), ("cw", 0), ("q", 0), ("q", 1),
    ("q", 2), ("z", 4, 1, 0), ("q", 3), ("cw", 1), ("kv", 0), ("kv", 1), ("kv", 2), ("z", 3, 3, 0), ("p", 4, 0),
    ("kv", 3), ("t", 2, 0), ("t", 2, 1), ("att", 0), ("p", 3, 0), ("p", 3, 1), ("z", 4, 2, 0), ("p", 3, 2),
    ("att", 1), ("z", 5, 1, 0), ("z", 5, 2, 0), ("att", 2), ("p", 5, 0), ("att", 3), ("p", 3, 3), ("br", 0),
    ("z", 4, 1, 1), ("z", 4, 2, 1), ("z", 4, 3, 0), ("br", 1), ("br", 2), ("br", 3), ("n1",), ("t", 3, 0),
    ("t", 3, 1), ("z", 5, 3, 0), ("z", 5, 1, 1), ("z", 5, 2, 1), ("z", 4, 3, 1), ("cw", 2), ("up", 0, 0),
    ("up", 1, 0), ("up", 2, 0), ("up", 3, 0), ("t", 4, 0), ("cw", 3), ("up", 0, 1), ("up", 1, 1), ("up", 2, 1),
    ("up", 3, 1), ("t", 4, 1), ("z", 5, 3, 1), ("t", 5, 0), ("t", 5, 1), ("cw", 4), ("dn", 0, 0), ("dn", 1, 0),
    ("dn", 2, 0), ("dn", 3, 0), ("cw", 5), ("dn", 0, 1), ("dn", 1, 1), ("dn", 2, 1), ("dn", 3, 1), ("n2",),
    ("sent",), ("hb", 0, 0), ("hb", 1, 0), ("hb", 2, 0), ("hb", 3, 0), ("cs", 0), ("hb", 0, 1), ("hb", 1, 1),
    ("hb", 2, 1), ("hb", 3, 1), ("cs", 1), ("ub", 0), ("ce", 0, 1), ("ce", 0, 0), ("ub", 1), ("ub", 2),
    ("ub", 3), ("n1b",), ("ce", 1, 1), ("gu", 0, 0), ("gu", 1, 0), ("gu", 2, 0), ("gu", 3, 0), ("cs", 2),
    ("gu", 0, 1), ("gu", 1, 1), ("te", 0, 1), ("gu", 2, 1), ("gu", 3, 1), ("cs", 3), ("mb", 0), ("ab", 0, 0),
    ("ab", 0, 1), ("ab", 0, 2), ("ce", 3, 1), ("ce", 2, 1), ("kb", 0), ("mb", 1), ("ab", 1, 0), ("ab", 1, 1),
    ("ab", 1, 2), ("te", 0, 0), ("kb", 1), ("ce", 2, 0), ("mb", 2), ("ab", 2, 0), ("ab", 2, 1), ("ab", 2, 2),
    ("ce", 1, 0), ("te", 1, 1), ("kb", 2), ("mb", 3), ("ab", 3, 0), ("ab", 3, 1), ("ab", 3, 2), ("kb", 3),
    ("turn",), ("ce", 3, 0), ("ag", 0), ("te", 3, 1), ("ag", 1), ("ag", 2), ("te", 1, 0), ("ag", 3), ("se", 0),
    ("zs", 0, 0, 0), ("zs", 0, 0, 1), ("zs", 0, 0, 2), ("cs", 4), ("te", 2, 1), ("te", 2, 0), ("cs", 5),
    ("wi", 0), ("wi", 1), ("home",), ("qi", 0), ("se", 1), ("zs", 1, 0, 0), ("zs", 1, 0, 1), ("zs", 1, 0, 2),
    ("ce", 4, 1), ("ce", 4, 0), ("qi", 1), ("qi", 2), ("qi", 3), ("own_in",), ("te", 3, 0), ("ce", 5, 1),
    ("se", 2), ("zs", 2, 0, 0), ("zs", 2, 0, 1), ("zs", 2, 0, 2), ("take",), ("ce", 5, 0), ("te", 4, 1),
    ("se", 3), ("zs", 3, 0, 0), ("zs", 3, 0, 1), ("zs", 3, 0, 2), ("te", 4, 0), ("te", 5, 1), ("zs", 5, 1, 0),
    ("zs", 5, 1, 1), ("zs", 5, 1, 2), ("te", 5, 0), ("zs", 5, 0, 0), ("zs", 5, 0, 1), ("zs", 5, 0, 2),
    ("la", 0), ("se", 4), ("zs", 4, 0, 0), ("zs", 4, 0, 1), ("zs", 4, 0, 2), ("zl", 5, 1), ("zl", 5, 0),
    ("la", 1), ("la", 3), ("la", 2), ("la", 4), ("la", 5),
)

INPUTS = ("m_qkv", "m_out", "m_up", "m_down", "m_norm", "m_bias", "tok", "out_grad", "seg", "grp", "ans")
OUTPUTS = ("block_out", "input_grad", "owned", "sums")


def kernel(names, chunks, back_chunks, pairs, *refs):
    r = dict(zip(names, refs))
    pc = Place()
    loads = {n: pltpu.make_async_copy(r["hbm_" + n], r[n], r["load_sems"].at[k]) for k, n in enumerate(INPUTS)}
    stores = {n: pltpu.make_async_copy(r[n], r["hbm_" + n], r["store_sems"].at[k]) for k, n in enumerate(OUTPUTS)}
    for copy in loads.values():
        copy.start()
    greet(pc, True)
    for n in INPUTS[:6]:
        loads[n].wait()
    gather = Gather(pc, r["g"], chunks, [r["gs%d" % k] for k in range(8)])
    lower_masters(r, pc, chunks, gather)
    layer = Layer(r, pc)
    rows, length = layer.rows, layer.length
    tok, tokw, window, xr, owned = r["tok"], r["tokw"], r["xw"], r["xrecv"], r["owned"]
    share = Share(
        pc,
        pairs,
        lambda low, high, target: tok.at[pl.ds(low % rows, high - low)],
        lambda low, high, target: tokw.at[in_window(low, high, target, rows, length)],
        r["share_sems"],
    )
    home = Share(
        pc,
        [(t, s, low, high) for s, t, low, high in pairs],
        lambda low, high, target: window.at[in_window(low, high, other_end(pairs, target, low), rows, length)],
        lambda low, high, target: xr.at[1 if low % rows == 0 else 0, pl.ds(0, high - low)],
        r["home_sems"],
    )
    spread = Sum5(pc, r["table"], r["table_slots"], r["table_sems"])
    total = Sum5(pc, r["sums"], r["sum_slots"], r["sum_sems"])

    def emit(j, value):
        a, low, w, _ = back_chunks[j]
        owned[a, :, low : low + w] = value

    grads = (r["hid"], r["g"].at[UP], r["g"].at[DOWN])
    back = Scatter(
        pc, grads, back_chunks, r["rc"], r["r3"], r["r2"], r["rz"], [r["ss%d" % k] for k in range(9)], emit
    )

    def start():
        for m in range(4):

            def own_tokens(m=m):
                for at, where in own_parts(m, rows, length):
                    tokw[where[0], where[1], :] = tok[at, :]

            pl.when(pc.m == m)(own_tokens)

    def share_start():
        loads["tok"].wait()
        share.start()

    def masks():
        for n in ("seg", "grp", "ans"):
            loads[n].wait()
        layer.masks()

    def second_norm():
        loads["out_grad"].wait()
        layer.second_norm()
        stores["block_out"].start()

    def table_step(k):
        spread.end(k)
        if k < 4:
            spread.start(k + 1)
        else:
            r["tab"][...] = r["table"][...].astype(F32)

    def sent():
        gather.finish()
        share.wait_send()
        spread.finish()

    def homeward():
        for m in range(4):

            def own_rows(m=m):
                for at, where in own_parts(m, rows, length):
                    r["acc"][at, :] += window[where[0], where[1], :].astype(F32)

            pl.when(pc.m == m)(own_rows)

    def take():
        home.wait_recv()
        for source, target, low, high in home.pairs:

            def add(source=source, target=target, low=low, high=high):
                at = slice(low - target * rows, high - target * rows)
                k = 1 if low % rows == 0 else 0
                r["acc"][at, :] += xr[k, : high - low, :].astype(F32)

            pl.when(pc.m == target)(add)
        r["input_grad"][...] = r["acc"][...].astype(BF16)
        stores["input_grad"].start()

    steps = {
        "own": gather.own,
        "z": gather.z_step,
        "p": gather.p_step,
        "t": gather.t_step,
        "cw": gather.core_wait,
        "share": share_start,
        "shared": share.wait_recv,
        "sp": table_step,
        "sent": sent,
        "start": start,
        "masks": masks,
        "q": layer.queries,
        "kv": layer.keys_values,
        "att": layer.attend,
        "br": layer.branch,
        "n1": layer.first_norm,
        "up": layer.up,
        "dn": layer.down,
        "n2": second_norm,
        "hb": layer.hidden_back,
        "ub": layer.up_back,
        "n1b": layer.first_back,
        "gu": layer.up_grad,
        "mb": layer.mixed_back,
        "ab": layer.attend_back,
        "kb": layer.keys_back,
        "turn": layer.turn,
        "ag": layer.attention_grad,
        "qi": layer.query_input,
        "wi": layer.window_input,
        "home": home.start,
        "own_in": homeward,
        "take": take,
        "cs": back.core_start,
        "ce": back.core_end,
        "te": back.third_end,
        "se": back.second_end,
        "zs": back.z_step,
        "zl": back.z_last,
        "la": back.last,
    }
    spread.start(0)
    for name, *at in ORDER:
        steps[name](*at)

    stores["owned"].start()
    sums = r["sums"]
    squares = jnp.zeros((1, owned.shape[2]), F32)
    for a in range(3):
        squares = squares + col_sum(owned[a] * owned[a])
    sums[14:15, :] = squares
    sums[15:16, :] = jnp.zeros_like(squares)
    for k in range(5):
        total.start(k)
        total.end(k)
    stores["sums"].start()
    home.wait_send()
    back.finish()
    total.finish()
    for copy in stores.values():
        copy.wait()


def lower_masters(r, pc, chunks, gather):
    qkv, table = r["m_qkv"], r["table"]
    local = qkv.shape[2]
    for j, (a, low, w, _) in enumerate(chunks):
        ref = gather.piece(j, pc.z, 0, 0)
        if a == ATT:
            pair = (qkv[0], r["m_out"][...].T) if low == 0 else (qkv[1], qkv[2])
            ref[...] = jnp.concatenate(pair, 1).astype(BF16)
        else:
            ref[...] = r["m_up" if a == UP else "m_down"][:, low : low + w].astype(BF16)
    outer = pc.z * 2 + pc.x
    norm, bias = r["m_norm"], r["m_bias"]
    part, piece = norm.shape[2], bias.shape[1]
    width, columns = table.shape[1], 8 * piece
    wide = r["norm_wide"]
    wide[...] = jnp.zeros_like(wide)
    for k in range(6):
        wide[k : k + 1, :part] = norm[k]
    rows = pltpu.roll(wide[...], pc.m * local + outer * part, 1)
    line = r["bias_wide"]
    line[...] = jnp.zeros_like(line)
    line[0:1, :piece] = bias[...]
    line = pltpu.roll(line[...], outer * piece, 1)[0:1]
    head = line[:, : 2 * local]
    early = lax.broadcasted_iota(jnp.int32, head.shape, 1) < local
    attention = jnp.concatenate([jnp.where(early, head, 0.0), jnp.where(early, 0.0, head)], 1)
    hidden = line[:, 2 * local :]
    row = lax.broadcasted_iota(jnp.int32, (8, width), 0)
    top = jnp.where(row < 6, rows, 0.0)
    top = jnp.where(row == 6 + pc.m, attention, top)
    top = jnp.where(row == 10 + pc.m, hidden, top)
    low = jnp.where(row + 8 == 6 + pc.m, attention, 0.0)
    low = jnp.where(row + 8 == 10 + pc.m, hidden, low)
    table[...] = jnp.concatenate([top, low], 0).astype(BF16)


def other_end(pairs, owner, low):
    return [t for s, t, first, _ in pairs if s == owner and first == low][0]


def in_window(low, high, m, rows, length):
    return low // length - m * rows // length, pl.ds(low % length, high - low)


def own_parts(m, rows, length):
    parts, low = [], m * rows
    while low < (m + 1) * rows:
        high = min((m + 1) * rows, (low // length + 1) * length)
        parts.append((slice(low - m * rows, high - m * rows), in_window(low, high, m, rows, length)))
        low = high
    return parts


def run_layer(masters, tok, out_grad, seg, grp, ans, pad):
    per, cols = masters[2].shape
    rows, width = tok.shape
    length = seg.shape[1]
    hidden = 4 * cols
    window = max((m * rows + rows - 1) // length - m * rows // length + 1 for m in range(4))
    blocks = rows // 128
    pairs = overlaps(rows, length)
    chunks = chunks_of((ATT, UP, DOWN), cols, LONG)
    back_chunks = chunks_of((DOWN, UP, ATT), cols, BACK_LONG)
    most = max(high - low for _, _, low, high in pairs)
    bufs, sems = scatter_scratch(back_chunks, per)
    scratch = {
        "g": pltpu.VMEM((3, 4, 2, per, hidden), BF16),
        "table": pltpu.VMEM((16, width), BF16),
        "norm_wide": pltpu.VMEM((8, width), F32),
        "bias_wide": pltpu.VMEM((8, 8 * masters[5].shape[1]), F32),
        "tab": pltpu.VMEM((16, width), F32),
        "table_slots": pltpu.VMEM((10, 16, width), BF16),
        "tokw": pltpu.VMEM((window, length, width), BF16),
        "bias": pltpu.VMEM((blocks, 128, length), F32),
        "q": pltpu.VMEM((4, rows, 256), BF16),
        "kv": pltpu.VMEM((4, window, length, cols // 2), BF16),
        "shares": pltpu.VMEM((4, blocks, 3, 128, length), BF16),
        "o": pltpu.VMEM((4, rows, 256), BF16),
        "do": pltpu.VMEM((rows, 256), BF16),
        "dkv_acc": pltpu.VMEM((window, length, cols // 2), F32),
        "acc": pltpu.VMEM((rows, width), F32),
        "xh": pltpu.VMEM((rows, width), F32),
        "rs": pltpu.VMEM((rows, 1), F32),
        "hb": pltpu.VMEM((rows, width), BF16),
        "dz": pltpu.VMEM((rows, width), BF16),
        "hid": pltpu.VMEM((4, 2, per, hidden), BF16),
        "turned": pltpu.VMEM((width, rows), BF16),
        "turned2": pltpu.VMEM((width, rows), BF16),
        "turnedw": pltpu.VMEM((window, width, length), BF16),
        "xw": pltpu.VMEM((window, length, width), BF16),
        "xrecv": pltpu.VMEM((2, most, width), BF16),
        "sum_slots": pltpu.VMEM((10, 16, width), F32),
        "share_sems": pltpu.SemaphoreType.DMA((4,)),
        "home_sems": pltpu.SemaphoreType.DMA((4,)),
        "table_sems": pltpu.SemaphoreType.DMA((10,)),
        "sum_sems": pltpu.SemaphoreType.DMA((10,)),
    }
    scratch.update(zip(("rc", "r3", "r2", "rz"), bufs))
    scratch.update(("gs%d" % k, s) for k, s in enumerate(gather_sems(len(chunks))))
    scratch.update(("ss%d" % k, s) for k, s in enumerate(sems))
    given = dict(zip(INPUTS, list(masters) + [tok, out_grad, seg, grp, ans]))
    scratch.update((n, pltpu.VMEM(v.shape, v.dtype)) for n, v in given.items())
    made = dict(
        block_out=jax.ShapeDtypeStruct((rows, width), BF16),
        input_grad=jax.ShapeDtypeStruct((rows, width), BF16),
        owned=jax.ShapeDtypeStruct((3, per, cols), F32),
        sums=jax.ShapeDtypeStruct((16, width), F32),
    )
    scratch.update((n, pltpu.VMEM(v.shape, v.dtype)) for n, v in made.items())
    scratch["load_sems"] = pltpu.SemaphoreType.DMA((len(INPUTS),))
    scratch["store_sems"] = pltpu.SemaphoreType.DMA((len(OUTPUTS),))
    names = tuple("hbm_" + n for n in INPUTS) + ("pad",) + tuple("hbm_" + n for n in OUTPUTS) + tuple(scratch)
    anywhere = pl.BlockSpec(memory_space=pl.ANY)
    return pl.pallas_call(
        functools.partial(kernel, names, chunks, back_chunks, pairs),
        out_shape=list(made.values()),
        in_specs=[anywhere] * len(INPUTS) + [pl.BlockSpec(memory_space=pltpu.SMEM)],
        out_specs=[anywhere] * len(OUTPUTS),
        scratch_shapes=list(scratch.values()),
        compiler_params=pltpu.CompilerParams(collective_id=0, has_side_effects=True, vmem_limit_bytes=62 * 2**20),
        name="layer",
    )(*masters, tok, out_grad, seg, grp, ans, pad)


def adam_update(weight, grad, first, second, factor, decayed, rate):
    clipped = grad * factor
    first_new = beta_first * first + (1.0 - beta_first) * clipped
    second_new = beta_second * second + (1.0 - beta_second) * clipped * clipped
    ratio = (
        first_new
        / (1.0 - beta_first**STEP)
        / (jnp.sqrt(second_new / (1.0 - beta_second**STEP)) + adam_epsilon)
    )
    if decayed:
        ratio = ratio + decay_rate * weight
    return (weight - rate * ratio, first_new, second_new)


def update_kernel(*refs):
    given, (block_out, input_grad, norm_out), made = refs[:22], refs[22:25], refs[25:43]
    held, (grad_norm, load_sems, store_sems) = refs[43:65], refs[65:]
    loads = [pltpu.make_async_copy(a, b, load_sems.at[k]) for k, (a, b) in enumerate(zip(given, held))]
    outs = [held[2 + n * 6 + k] for n in range(3) for k in range(6)]
    stores = [pltpu.make_async_copy(a, b, store_sems.at[k]) for k, (a, b) in enumerate(zip(outs, made))]
    order = [1, 0] + [2 + n * 6 + k for k in (2, 3, 0, 1, 4, 5) for n in range(3)] + [20, 21]
    for k in order:
        loads[k].start()
    passed = [
        pltpu.make_async_copy(held[20], block_out, store_sems.at[18]),
        pltpu.make_async_copy(held[21], input_grad, store_sems.at[19]),
        pltpu.make_async_copy(grad_norm, norm_out, store_sems.at[20]),
    ]
    owned, total = held[:2]
    masters, firsts, seconds = held[2:8], held[8:14], held[14:20]
    loads[1].wait()
    place = lax.axis_index("outer") * lax.axis_size("inner") + lax.axis_index("inner")
    mp = lax.axis_index("mp")
    local = masters[0].shape[2]
    width = total.shape[1]
    lane = lax.broadcasted_iota(jnp.int32, (4, width), 1)
    head, hidden = total[6:10, :], total[10:14, :]
    head = jnp.where((lane < local) | (lane >= 3 * local), head, 0.0)

    def square(v):
        return jnp.sum(jnp.sum(v * v, 0, keepdims=True), 1, keepdims=True)

    squares = jnp.sum(total[14:15, :], 1, keepdims=True) + square(total[0:6, :]) + square(head) + square(hidden)
    norm = jnp.sqrt(squares)
    grad_norm[...] = norm
    passed[2].start()
    factor = jnp.minimum(1.0, clip_limit / norm)
    mine = lax.broadcasted_iota(jnp.int32, (4, width), 0) == mp
    head = jnp.sum(jnp.where(mine, head, 0.0), 0, keepdims=True)
    hidden = jnp.sum(jnp.where(mine, hidden, 0.0), 0, keepdims=True)
    line = jnp.concatenate([head[:, : 2 * local] + head[:, 2 * local :], hidden], 1)
    part, piece = masters[4].shape[2], masters[5].shape[1]
    line = jnp.broadcast_to(line, (8, line.shape[1]))
    line = pltpu.roll(line, lax.rem(line.shape[1] - place * piece, line.shape[1]), 1)[0:1, :piece]
    norms = pltpu.roll(total[0:8, :], lax.rem(width - (mp * local + place * part), width), 1)

    def update(k, at, grad):
        values = adam_update(masters[k][at], grad, firsts[k][at], seconds[k][at], factor, k < 4, learn_rates[k])
        for n, value in enumerate(values):
            outs[n * 6 + k][at] = value

    def ready(k):
        for n in range(3):
            loads[2 + n * 6 + k].wait()

    def done(k):
        for n in range(3):
            stores[n * 6 + k].start()

    loads[0].wait()
    everything = (slice(None), slice(None))
    for k, grad in ((2, owned[1]), (3, owned[2])):
        ready(k)
        update(k, everything, grad)
        done(k)
    attention = owned[0]
    ready(0)
    update(0, 0, attention[:, :local])
    update(0, 1, attention[:, 2 * local : 3 * local])
    update(0, 2, attention[:, 3 * local :])
    done(0)
    ready(1)
    update(1, everything, attention[:, local : 2 * local].T)
    done(1)
    ready(4)
    for k in range(6):
        update(4, k, norms[k : k + 1, :part])
    done(4)
    ready(5)
    update(5, everything, line)
    done(5)
    for k in range(2):
        loads[20 + k].wait()
        passed[k].start()
    for copy in stores + passed:
        copy.wait()


def update(owned, total, block_out, input_grad, masters, firsts, seconds):
    anywhere = pl.BlockSpec(memory_space=pl.ANY)
    given = [owned, total, *masters, *firsts, *seconds, block_out, input_grad]

    def like(v):
        return jax.ShapeDtypeStruct(v.shape, v.dtype)

    return pl.pallas_call(
        update_kernel,
        out_shape=[like(block_out), like(input_grad), jax.ShapeDtypeStruct((1, 1), F32)] + [like(m) for m in masters] * 3,
        in_specs=[anywhere] * 22,
        out_specs=[anywhere] * 21,
        scratch_shapes=[pltpu.VMEM(v.shape, v.dtype) for v in given]
        + [pltpu.VMEM((1, 1), F32), pltpu.SemaphoreType.DMA((22,)), pltpu.SemaphoreType.DMA((21,))],
        compiler_params=pltpu.CompilerParams(vmem_limit_bytes=62 * 2**20),
        name="update",
    )(*given)


def body(tokens, out_grad, segment_ids, group_ids, answer_ids, pad_lengths, *states):
    def turned(values):
        return [v.T if k == 3 else v for k, v in enumerate(values)]

    masters, firsts, seconds = turned(states[:6]), turned(states[6:12]), turned(states[12:])
    inner = lax.axis_size("inner")
    shared = masters
    if inner > 1:
        shared = [lax.all_gather(v, "inner", axis=d, tiled=True) for v, d in zip(masters, (1, 1, 0, 0, 2, 1))]
    block_out, input_grad, owned, total = run_layer(
        shared, tokens, out_grad, segment_ids, group_ids, answer_ids, pad_lengths
    )
    if inner > 1:
        owned = lax.psum_scatter(owned, "inner", scatter_dimension=1, tiled=True)
        total = lax.psum(total, "inner")
        squares = lax.psum(jnp.sum(owned * owned), ("outer", "inner", "mp"))
        total = total.at[14].set(squares / total.shape[1])
    results = update(owned, total, block_out, input_grad, masters, firsts, seconds)
    updated = [v for n in range(3) for v in turned(results[3 + 6 * n : 9 + 6 * n])]
    return (results[0], results[1], results[2][0, 0]) + tuple(updated)


def solution(mesh):
    dp = mesh.shape["dp"]
    outer = 8
    grid = Mesh(mesh.devices.reshape(outer, dp // outer, mesh.shape["mp"]), ("outer", "inner", "mp"))
    d = ("outer", "inner")
    both = P(d + ("mp",), None)
    states = (P(None, d, "mp"), P("mp", d), P(d, "mp"), P("mp", d), P(None, "mp", d), P("mp", d))
    in_specs = (both, both, P(d, None), P(d, None), P(d, None), P(d)) + states * 3
    out_specs = (both, both, P()) + states * 3
    return jax.shard_map(body, mesh=grid, in_specs=in_specs, out_specs=out_specs, check_vma=False)
```

```python
import functools
import jax
import jax.numpy as jnp
import numpy as np
from jax import lax
from jax.sharding import Mesh, PartitionSpec as P
from jax.experimental import pallas as pl
from jax.experimental.pallas import tpu as pltpu

MESH = pl.DeviceIdType.MESH
F32 = jnp.float32
BF16 = jnp.bfloat16
HD = 64
STEP = 5

norm_epsilon = 1e-06
adam_epsilon = 1e-08
learn_rates = (0.02, 0.1, 0.02, 0.02, 0.5, 0.5)
beta_first = 0.5
beta_second = 0.5
decay_rate = 0.01
clip_limit = 0.05
mask_fill = -1000000000.0
score_scale = 0.125

ATT, UP, DOWN = 0, 1, 2
NEAR, LONG, DIRECT = 0, 1, 2


def pick(index, values):
    out = values[-1]
    for k in range(len(values) - 1):
        out = jnp.where(index == k, values[k], out)
    return out


class Place:
    def __init__(self):
        outer = lax.axis_index("outer")
        self.sub = lax.axis_index("inner")
        self.m = lax.axis_index("mp")
        self.z = outer // 2
        self.x = lax.rem(outer, 2)
        self.y = self.m // 2
        self.c = lax.rem(self.m, 2)
        self.first = self.c == 0
        self.sib = self.at(c=1 - self.c)
        x, y = self.line(1, 0)
        self.second = self.at(x=x, y=y)
        x, y = self.line(0, 1)
        self.third = self.at(x=x, y=y)

    def at(self, z=None, x=None, y=None, c=None):
        z = self.z if z is None else z
        x = self.x if x is None else x
        y = self.y if y is None else y
        c = self.c if c is None else c
        return (z * 2 + x, self.sub, y * 2 + c)

    def mate(self, m):
        return (self.z * 2 + self.x, self.sub, m)

    def line(self, side, far, other_core=False):
        first = (1 - self.c if other_core else self.c) == 0
        x = jnp.where(first, side, far)
        y = jnp.where(first, far, side)
        return self.x + x - 2 * self.x * x, self.y + y - 2 * self.y * y

    def order(self, t):
        return pick(self.z, [(0, 1, 2, 3), (1, 0, 3, 2), (2, 2, 1, 1), (3, 3, 0, 0)][t])


def remote(src, dst, send, recv, device):
    return pltpu.make_async_remote_copy(
        src_ref=src, dst_ref=dst, send_sem=send, recv_sem=recv, device_id=device, device_id_type=MESH
    )


def peers(place):
    z, x, y, c = place.z, place.x, place.y, place.c

    def other(v, bit):
        return 1 - v if bit else v

    plane = [place.at(x=other(x, k & 4), y=other(y, k & 2), c=other(c, k & 1)) for k in range(1, 8)]
    return plane + [place.at(z=across(z, k)) for k in range(1, 4)]


def across(z, k):
    low, high = lax.rem(z, 2), z // 2
    return (1 - high if k & 2 else high) * 2 + (1 - low if k & 1 else low)


def greet(place):
    barrier = pltpu.get_barrier_semaphore()
    for device in peers(place):
        pl.semaphore_signal(barrier, inc=1, device_id=device, device_id_type=MESH)
    return lambda: pl.semaphore_wait(barrier, 10)


class Gather:
    def __init__(self, place, g, chunks, sems):
        self.p, self.g, self.chunks = place, g, chunks
        self.zs, self.zr, self.ps, self.pr, self.ts, self.tr, self.cs, self.cr = sems
        self.width = g.shape[4] // 4
        self.sent = []

    def piece(self, j, z, side, far, core=False):
        x, y = self.p.line(side, far, core)
        c = 1 - self.p.c if core else self.p.c
        a, low, w, _ = self.chunks[j]
        cols = pl.ds(pl.multiple_of((y * 2 + c) * self.width + low, 128), w)
        if z is None:
            return self.g.at[a, :, x, :, cols]
        return self.g.at[a, z, x, :, cols]

    def go(self, ref, send, recv, device, when=None):
        copy = remote(ref, ref, send, recv, device)
        if when is None:
            copy.start()
        else:
            pl.when(when)(copy.start)
        self.sent.append((copy, when))

    def arrived(self, ref, recv):
        remote(ref, ref, recv, recv, self.p.sib).wait_recv()

    def z_send(self, j, side, src, index, to, when):
        self.go(self.piece(j, src, side, 0), self.zs.at[j, side, index], self.zr.at[j, side, src], self.p.at(z=to), when)

    def z_both(self, j, side):
        z = self.p.z
        self.z_send(j, side, z, z, z + 1, z < 3)
        self.z_send(j, side, z, 4, z - 1, z > 0)

    def third(self, j, side, src):
        k = side * 4 + src
        self.go(self.piece(j, src, side, 0), self.ts.at[j, k], self.tr.at[j, k], self.p.third)

    def second(self, j, src):
        self.go(self.piece(j, src, 0, 0), self.ps.at[j, src], self.pr.at[j, src], self.p.second)

    def to_sibling(self, j, side, far):
        k = side + 2 * far
        self.go(self.piece(j, None, side, far), self.cs.at[j, k], self.cr.at[j, k], self.p.sib)

    def own(self, j):
        self.second(j, self.p.z)
        self.z_both(j, 0)
        self.third(j, 0, self.p.z)

    def z_step(self, j, t, side=0):
        z = self.p.z
        src = self.p.order(t)
        self.arrived(self.piece(j, src, side, 0), self.zr.at[j, side, src])
        to = jnp.where(z > src, z + 1, z - 1)
        self.z_send(j, side, src, src, to, (to >= 0) & (to <= 3))
        if self.chunks[j][3] != LONG:
            self.second(j, src)
        self.third(j, side, src)
        if t == 3:
            self.to_sibling(j, side, 0)

    def p_step(self, j, t):
        src = self.p.order(t)
        self.arrived(self.piece(j, src, 1, 0), self.pr.at[j, src])
        if self.chunks[j][3] == LONG:
            self.z_both(j, 1)
        self.third(j, 1, src)
        if t == 3:
            self.to_sibling(j, 1, 0)

    def t_step(self, j, side):
        for t in range(4):
            src = self.p.order(t)
            self.arrived(self.piece(j, src, side, 1), self.tr.at[j, side * 4 + src])
        self.to_sibling(j, side, 1)

    def core_wait(self, j):
        for k, (side, far) in enumerate(((0, 0), (1, 0), (0, 1), (1, 1))):
            self.arrived(self.piece(j, None, side, far, True), self.cr.at[j, k])

    def finish(self):
        for copy, when in self.sent:
            if when is None:
                copy.wait_send()
            else:
                pl.when(when)(copy.wait_send)
        self.sent = []


def gather_sems(chunks):
    sizes = ((2, 5), (2, 4), (4,), (4,), (8,), (8,), (4,), (4,))
    return [pltpu.SemaphoreType.DMA((chunks,) + n) for n in sizes]


def overlaps(rows, length):
    pairs = []
    for m in range(3):
        edge = (m + 1) * rows
        low = edge // length * length
        if low == edge:
            continue
        pairs.append((m, m + 1, max(low, m * rows), edge))
        pairs.append((m + 1, m, edge, min(low + length, edge + rows)))
    return pairs


class Share:
    def __init__(self, place, pairs, src, dst, sems):
        self.p, self.pairs, self.src, self.dst, self.sems = place, pairs, src, dst, sems

    def copy(self, pair):
        source, target, low, high = pair
        k = 0 if source < target else 1
        return remote(self.src(low, high, target), self.dst(low, high, target), self.sems.at[k], self.sems.at[2 + k], self.p.mate(target))

    def start(self):
        for pair in self.pairs:
            pl.when(self.p.m == pair[0])(self.copy(pair).start)

    def wait_recv(self):
        for pair in self.pairs:
            pl.when(self.p.m == pair[1])(self.copy(pair).wait_recv)

    def wait_send(self):
        for pair in self.pairs:
            pl.when(self.p.m == pair[0])(self.copy(pair).wait_send)


class Sum5:
    def __init__(self, place, table, slots, sems):
        self.p, self.table, self.slots, self.sems = place, table, slots, sems
        z = place.z
        self.peers = [
            place.at(z=z + 1 - 2 * lax.rem(z, 2)),
            place.at(z=z + 2 - 4 * (z // 2)),
            place.at(x=1 - place.x),
            place.at(y=1 - place.y),
            place.sib,
        ]

    def copy(self, k):
        return remote(self.slots.at[5 + k], self.slots.at[k], self.sems.at[k], self.sems.at[5 + k], self.peers[k])

    def start(self, k):
        self.slots[5 + k] = self.table[...]
        self.copy(k).start()

    def end(self, k):
        self.copy(k).wait_recv()
        self.table[...] = self.table[...] + self.slots[k]

    def finish(self):
        for k in range(5):
            self.copy(k).wait_send()


class Total:
    def __init__(self, place, tile, slots, sems):
        self.p, self.tile, self.slots, self.sems = place, tile, slots, sems
        self.copies = [remote(slots.at[0 if k < 7 else 11], slots.at[1 + k], sems.at[k], sems.at[10 + k], d) for k, d in enumerate(peers(place))]

    def run(self):
        for first, ks in ((0, range(7)), (11, range(7, 10))):
            self.slots[first] = self.tile[...]
            for k in ks:
                self.copies[k].start()
            total = self.tile[...]
            for k in ks:
                self.copies[k].wait_recv()
                total = total + self.slots[1 + k]
            self.tile[...] = total

    def finish(self):
        for copy in self.copies:
            copy.wait_send()


class Scatter:
    def __init__(self, place, grads, chunks, rc, r3, r2, rz, sems, emit):
        self.p, self.grads, self.chunks = place, grads, chunks
        self.rc, self.r3, self.r2, self.rz = rc, r3, r2, rz
        self.cs, self.cr, self.ts, self.tr, self.ps, self.pr, self.us, self.ds, self.zr = sems
        self.emit = emit
        self.width = grads[0].shape[3] // 4
        self.sent = []
        self.seconds, self.lines, _, _ = scatter_slots(chunks)

    def region(self, j, side, far, core=False):
        x, y = self.p.line(side, far, core)
        c = 1 - self.p.c if core else self.p.c
        a, low, w, _ = self.chunks[j]
        return a, x, pl.ds(pl.multiple_of((y * 2 + c) * self.width + low, 128), w)

    def block(self, j, side, far, core=False):
        a, x, cols = self.region(j, side, far, core)
        return self.grads[a].at[:, x, :, cols]

    def shard(self, j, side, z):
        a, x, cols = self.region(j, side, 0)
        return self.grads[a].at[z, x, :, cols]

    def go(self, src, dst, send, recv, device, when=None):
        copy = remote(src, dst, send, recv, device)
        if when is None:
            copy.start()
        else:
            pl.when(when)(copy.start)
        self.sent.append((copy, when))

    def arrived(self, ref, recv):
        remote(ref, ref, recv, recv, self.p.sib).wait_recv()

    def core_start(self, j):
        for far in (1, 0):
            for side in (1, 0):
                k = far * 2 + side
                self.go(self.block(j, side, far, True), self.rc.at[j, k], self.cs.at[j, k], self.cr.at[j, k], self.p.sib)

    def add(self, j, side, far, other):
        a, x, cols = self.region(j, side, far)

        def step(k):
            here = self.grads[a].at[k, x, :, cols]
            here[...] = (here[...].astype(F32) + other[k].astype(F32)).astype(BF16)

        pl.loop(0, 4)(step)

    def core_end(self, j, far):
        for side in (1, 0):
            k = far * 2 + side
            self.arrived(self.rc.at[j, k], self.cr.at[j, k])
            self.add(j, side, far, self.rc.at[j, k])
            if far == 1:
                self.go(self.block(j, side, 1), self.r3.at[j, side], self.ts.at[j, side], self.tr.at[j, side], self.p.third)

    def third_end(self, j, side):
        self.arrived(self.r3.at[j, side], self.tr.at[j, side])
        self.add(j, side, 0, self.r3.at[j, side])
        if self.chunks[j][3] == LONG:
            self.line_start(j, side)
        elif side == 1:
            slot = self.r2.at[pl.ds(self.seconds[j], 4)]
            self.go(self.block(j, 1, 0), slot, self.ps.at[j], self.pr.at[j], self.p.second)

    def second_end(self, j):
        slot = self.r2.at[pl.ds(self.seconds[j], 4)]
        self.arrived(slot, self.pr.at[j])
        self.add(j, 0, 0, slot)
        if self.chunks[j][3] != DIRECT:
            self.line_start(j, 0)
            return
        n = self.lines[j]
        for k in (3, 2, 1):
            to = across(self.p.z, k)
            self.go(self.shard(j, 0, to), self.rz.at[n, k], self.us.at[n, k], self.zr.at[n, k], self.p.at(z=to))

    def up(self, j, side, d, when):
        n = self.lines[j] + side
        self.go(self.shard(j, side, d), self.rz.at[n, d], self.us.at[n, d], self.zr.at[n, d], self.p.at(z=self.p.z + 1), when)

    def down(self, j, side, d, when):
        n = self.lines[j] + side
        slot = jnp.where(d == self.p.z - 1, 4, d)
        self.go(self.shard(j, side, d), self.rz.at[n, slot], self.ds.at[n, d], self.zr.at[n, slot], self.p.at(z=self.p.z - 1), when)

    def line_start(self, j, side):
        z = self.p.z
        for d in range(3):
            self.up(j, side, 3 - d, z == 0)
            self.down(j, side, d, z == 3)

    def fold(self, j, side, d, slot):
        n = self.lines[j] + side
        self.arrived(self.rz.at[n, slot], self.zr.at[n, slot])
        ref = self.shard(j, side, d)
        ref[...] = (ref[...].astype(F32) + self.rz[n, slot].astype(F32)).astype(BF16)

    def relay(self, j, side, d, send, when):
        pl.when(when)(lambda: self.fold(j, side, d, d))
        send(j, side, d, when)

    def z_step(self, j, side, t):
        z = self.p.z
        if t < 2:
            self.relay(j, side, 3 - t, self.up, z == 1)
            self.relay(j, side, t, self.down, z == 2)
        else:
            self.relay(j, side, 3, self.up, z == 2)
            self.relay(j, side, 0, self.down, z == 1)

    def z_last(self, j, side):
        z = self.p.z
        pl.when(z > 0)(lambda: self.fold(j, side, z, z))
        pl.when(z < 3)(lambda: self.fold(j, side, z, 4))
        if side == 1:
            slot = self.r2.at[self.seconds[j]]
            self.go(self.shard(j, 1, z), slot, self.ps.at[j], self.pr.at[j], self.p.second)

    def last(self, j):
        z = self.p.z
        if self.chunks[j][3] == DIRECT:
            n = self.lines[j]
            total = self.shard(j, 0, z)[...].astype(F32)
            for k in (1, 2, 3):
                self.arrived(self.rz.at[n, k], self.zr.at[n, k])
                total = total + self.rz[n, k].astype(F32)
            self.emit(j, total)
        elif self.chunks[j][3] == LONG:
            slot = self.r2.at[self.seconds[j]]
            self.arrived(slot, self.pr.at[j])
            self.emit(j, self.shard(j, 0, z)[...].astype(F32) + slot[...].astype(F32))
        else:
            self.z_last(j, 0)
            self.emit(j, self.shard(j, 0, z)[...].astype(F32))

    def finish(self):
        for copy, when in self.sent:
            if when is None:
                copy.wait_send()
            else:
                pl.when(when)(copy.wait_send)
        self.sent = []


def scatter_slots(chunks):
    seconds, lines, n, m = [], [], 0, 0
    for chunk in chunks:
        seconds.append(n)
        lines.append(m)
        n += 1 if chunk[3] == LONG else 4
        m += 2 if chunk[3] == LONG else 1
    return seconds, lines, n, m


def scatter_scratch(chunks, rows):
    n, w = len(chunks), chunks[0][2]
    _, _, seconds, lines = scatter_slots(chunks)
    shapes = ((n, 4, 4), (n, 2, 4), (seconds,), (lines, 5))
    sems = ((n, 4), (n, 4), (n, 2), (n, 2), (n,), (n,), (lines, 4), (lines, 4), (lines, 5))
    return [pltpu.VMEM(s + (rows, w), BF16) for s in shapes], [pltpu.SemaphoreType.DMA(s) for s in sems]


def nt(a, b):
    return lax.dot_general(a, b, (((1,), (1,)), ((), ())), preferred_element_type=F32)


def tn(a, b):
    return lax.dot_general(a, b, (((0,), (0,)), ((), ())), preferred_element_type=F32)


def nn(a, b):
    return jnp.dot(a, b, preferred_element_type=F32)


def even_lanes(shape):
    return lax.broadcasted_iota(jnp.int32, shape, 1) < HD


def keep(values, even):
    mask = even_lanes(values.shape)
    zero = jnp.zeros_like(values)
    return jnp.where(mask, values, zero) if even else jnp.where(mask, zero, values)


def col_sum(values):
    return jnp.sum(values, 0, keepdims=True)


class Layer:
    def __init__(self, refs, place):
        self.__dict__.update(refs)
        self.p = place
        self.rows, self.width = self.tok.shape
        self.length = self.seg.shape[1]
        self.blocks = self.rows // 128
        self.cols = self.g.shape[4] // 4
        self.hidden = self.g.shape[4]
        self.s0 = self.rows * place.m // self.length
        self.s1 = (self.rows * place.m + self.rows - 1) // self.length
        self.window = self.kv.shape[1]

    def w(self, a, low, size):
        return self.g[a, :, :, :, low : low + size].reshape(self.width, size)

    def put(self, ref, low, value):
        size = value.shape[1]
        ref[:, :, :, low : low + size] = value.astype(BF16).reshape(ref.shape[:3] + (size,))

    def gain(self, row):
        return self.tab[pl.ds(row, 1), :]

    def blk(self, i):
        return pl.ds(pl.multiple_of(i * 128, 128), 128)

    def seq_of(self, i):
        return (self.rows * self.p.m + 128 * i) // self.length

    def each_seq(self, run):
        for s in range(self.window):
            if s == 0:
                run(s)
            else:
                pl.when(self.s0 + s <= self.s1)(functools.partial(run, s))

    def masks(self):
        n = self.length
        for i in range(self.blocks):
            s = self.seq_of(i)
            at = lax.rem(self.rows * self.p.m + 128 * i, n)
            seg = self.seg[pl.ds(s, 1), :]
            grp = self.grp[pl.ds(s, 1), :]
            ans = self.ans[pl.ds(s, 1), :]
            seg_q = pick(at // 128, [seg[:, k : k + 128] for k in range(0, n, 128)])
            grp_q = pick(at // 128, [grp[:, k : k + 128] for k in range(0, n, 128)])
            code = jnp.where(seg_q == 0, -1, grp_q).astype(F32)
            code = jnp.transpose(jnp.broadcast_to(code, (8, 128)))[:, :1]
            open_key = (seg == 0) | (ans == 1)
            rule = (code == grp.astype(F32)) | (code < 0.0) | open_key
            position = lax.broadcasted_iota(jnp.int32, (1, n), 1)
            seen = rule & (position < self.pad[s])
            self.bias[i] = jnp.where(seen, 0.0, mask_fill)

    def queries(self, b):
        c = self.cols
        lanes = lax.broadcasted_iota(jnp.int32, (1, 256), 1) < c // 4
        q = nn(self.tok[...], self.w(ATT, b * c, 256)) + self.tab[6 + b : 7 + b, :256]
        self.q[b] = jnp.where(lanes, q * score_scale, 0.0).astype(BF16)

    def keys_values(self, b):
        c = self.cols
        wkv = self.w(ATT, b * c + c // 2, c // 2)

        def one(s):
            self.kv[b, s] = (nn(self.tokw[s], wkv) + self.tab[6 + b : 7 + b, c // 2 :]).astype(BF16)

        self.each_seq(one)

    def heads(self, b, i):
        s = self.seq_of(i) - self.s0
        q0 = self.q[b, self.blk(i), :128]
        q2 = self.q[b, self.blk(i), 128:]
        return s, keep(q0, True), keep(q0, False), q2

    def attend(self, b):
        @pl.loop(0, self.blocks)
        def _(i):
            s, q0, q1, q2 = self.heads(b, i)
            bias = self.bias[i]

            def softmax(scores):
                scores = scores + bias
                e = jnp.exp(scores - jnp.max(scores, -1, keepdims=True))
                return (e * (1.0 / jnp.sum(e, -1, keepdims=True))).astype(BF16)

            t0, t1, t2 = (self.kv[b, s, :, 128 * t : 128 * t + 128] for t in range(3))
            s01 = nt(jnp.concatenate([q0, q1], 0), t0)
            p0, p1, p2 = softmax(s01[:128]), softmax(s01[128:]), softmax(nt(q2, t1))
            self.shares[b, i, 0] = p0
            self.shares[b, i, 1] = p1
            self.shares[b, i, 2] = p2
            o12 = nn(jnp.concatenate([p1, p2], 0), t2)
            self.o[b, self.blk(i), :128] = keep(nn(p0, t1), False).astype(BF16)
            self.o[b, self.blk(i), 128:] = jnp.where(even_lanes((128, 128)), o12[:128], o12[128:]).astype(BF16)

    def row_loop(self, step, sums):
        n = 48

        def run(k, carry):
            at = pl.ds(pl.multiple_of(k * n, n), n)
            return step(at, carry)

        zero = tuple(jnp.zeros((1, self.width), F32) for _ in range(sums))
        return lax.fori_loop(0, self.rows // n, run, zero)

    def accumulate(self, value, first):
        self.acc[...] = value if first else self.acc[...] + value

    def branch(self, b):
        self.accumulate(nt(self.o[b], self.w(ATT, b * self.cols + 128, 256)), b == 0)

    def first_norm(self):
        g1, b1, co = self.gain(0), self.gain(1), self.gain(2)

        def step(at, carry):
            r = self.tok[at, :].astype(F32) + (self.acc[at, :] + co)
            r = r - jnp.mean(r, -1, keepdims=True)
            rs = lax.rsqrt(jnp.mean(r * r, -1, keepdims=True) + norm_epsilon)
            xh = r * rs
            self.xh[at, :] = xh
            self.rs[at, :] = rs
            self.hb[at, :] = (xh * g1 + b1).astype(BF16)
            return carry

        self.row_loop(step, 0)

    def half(self, b, k):
        n = self.cols // 2
        return b * self.cols + k * n, n

    def hidden_ref(self, which):
        return self.hid.at[2 * which : 2 * which + 2]

    def get_hidden(self, which, low, n):
        return self.hidden_ref(which)[:, :, :, low : low + n].reshape(self.rows, n)

    def set_hidden(self, which, low, value):
        ref = self.hidden_ref(which)
        ref[:, :, :, low : low + value.shape[1]] = value.astype(BF16).reshape(ref.shape[:3] + value.shape[1:])

    def up(self, b, k):
        low, n = self.half(b, k)
        u = nn(self.hb[...], self.w(UP, low, n)) + self.tab[10 + b : 11 + b, k * n : k * n + n]
        share = 0.5 + 0.5 * lax.erf(u * np.float32(np.sqrt(0.5)))
        self.set_hidden(0, low, u * share)
        self.set_hidden(1, low, share + u * (jnp.exp(-0.5 * (u * u)) * np.float32(1 / np.sqrt(2 * np.pi))))

    def down(self, b, k):
        low, n = self.half(b, k)
        self.accumulate(nt(self.get_hidden(0, low, n), self.w(DOWN, low, n)), b == 0 and k == 0)

    def second_norm(self):
        g1, b1, g2, b2, cd = self.gain(0), self.gain(1), self.gain(3), self.gain(4), self.gain(5)

        def step(at, carry):
            r = (self.xh[at, :] * g1 + b1) + (self.acc[at, :] + cd)
            r = r - jnp.mean(r, -1, keepdims=True)
            rs = lax.rsqrt(jnp.mean(r * r, -1, keepdims=True) + norm_epsilon)
            xh = r * rs
            self.block_out[at, :] = (xh * g2 + b2).astype(BF16)
            grad = self.out_grad[at, :].astype(F32)
            inner = grad * g2
            back = rs * (inner - jnp.mean(inner, -1, keepdims=True) - xh * jnp.mean(inner * xh, -1, keepdims=True))
            self.acc[at, :] = back
            low = back.astype(BF16)
            self.dz[at, :] = low
            return carry[0] + col_sum(grad * xh), carry[1] + col_sum(grad), carry[2] + col_sum(low.astype(F32))

        dg, db, dc = self.row_loop(step, 3)
        self.sums[3:4, :] = dg
        self.sums[4:5, :] = db
        self.sums[5:6, :] = dc

    def hidden_back(self, b, k):
        if b == 0 and k == 0:
            self.turned[...] = self.dz[...].T
        low, n = self.half(b, k)
        du = nn(self.dz[...], self.w(DOWN, low, n)) * self.get_hidden(1, low, n).astype(F32)
        du = du.astype(BF16)
        self.set_hidden(1, low, du)
        self.sums[10 + b : 11 + b, k * n : k * n + n] = col_sum(du.astype(F32))
        self.put(self.g.at[DOWN], low, nn(self.turned[...], self.get_hidden(0, low, n)))

    def up_back(self, b):
        low = b * self.cols
        self.acc[...] += nt(self.get_hidden(1, low, self.cols), self.w(UP, low, self.cols))

    def up_grad(self, b, k):
        if b == 0 and k == 0:
            self.turned[...] = self.hb[...].T
        low, n = self.half(b, k)
        self.put(self.g.at[UP], low, nn(self.turned[...], self.get_hidden(1, low, n)))

    def first_back(self):
        g1 = self.gain(0)

        def step(at, carry):
            grad = self.acc[at, :]
            xh = self.xh[at, :]
            inner = grad * g1
            back = self.rs[at, :] * (
                inner - jnp.mean(inner, -1, keepdims=True) - xh * jnp.mean(inner * xh, -1, keepdims=True)
            )
            self.acc[at, :] = back
            low = back.astype(BF16)
            self.dz[at, :] = low
            return carry[0] + col_sum(grad * xh), carry[1] + col_sum(grad), carry[2] + col_sum(low.astype(F32))

        dg, db, dc = self.row_loop(step, 3)
        self.sums[0:1, :] = dg
        self.sums[1:2, :] = db
        self.sums[2:3, :] = dc

    def mixed_back(self, b):
        do = nn(self.dz[...], self.w(ATT, b * self.cols + 128, 256))
        lanes = lax.broadcasted_iota(jnp.int32, (1, 256), 1) >= HD
        self.do[...] = jnp.where(lanes, do, 0.0).astype(BF16)
        self.dkv_acc[...] = jnp.zeros_like(self.dkv_acc)

    def attend_back(self, b, i):
        s, q0, q1, q2 = self.heads(b, i)
        t0, t1, t2 = (self.kv[b, s, :, 128 * t : 128 * t + 128] for t in range(3))
        do0 = self.do[self.blk(i), :128]
        do12 = self.do[self.blk(i), 128:]
        do1, do2 = keep(do12, True), keep(do12, False)
        dp12 = nt(jnp.concatenate([do1, do2], 0), t2)

        def back(h, dp):
            low = self.shares[b, i, h]
            p = low.astype(F32)
            scaled = p * dp
            return low, (scaled - p * jnp.sum(scaled, -1, keepdims=True)).astype(BF16)

        p0, ds0 = back(0, nt(do0, t1))
        p1, ds1 = back(1, dp12[:128])
        p2, ds2 = back(2, dp12[128:])
        dq01 = nn(jnp.concatenate([ds0, ds1], 0), t0)
        dq0 = jnp.where(even_lanes((128, 128)), dq01[:128], dq01[128:])
        dq2 = keep(nn(ds2, t1), True)
        self.q[b, self.blk(i), :128] = (dq0 * score_scale).astype(BF16)
        self.q[b, self.blk(i), 128:] = (dq2 * score_scale).astype(BF16)
        rows = jnp.concatenate
        self.dkv_acc[s, :, :128] += tn(rows([ds0, ds1], 0), rows([q0, q1], 0))
        self.dkv_acc[s, :, 128:256] += tn(rows([ds2, p0], 0), rows([q2, do0], 0))
        self.dkv_acc[s, :, 256:] += tn(rows([p1, p2], 0), rows([do1, do2], 0))

    def keys_back(self, b):
        c = self.cols
        total = jnp.zeros((1, c // 2), F32)
        for s in range(self.window):
            low = self.dkv_acc[s].astype(BF16)
            self.kv[b, s] = low
            total = total + col_sum(low.astype(F32))
        first = col_sum(self.q[b].astype(F32))
        gap = jnp.zeros((1, c // 2 - 256), F32)
        self.sums[6 + b : 7 + b, :] = jnp.concatenate([first, gap, total], 1)

    def turn(self):
        self.turned[...] = self.tok[...].T
        self.turned2[...] = self.dz[...].T

        def one(s):
            self.turnedw[s] = self.tokw[s].T

        self.each_seq(one)

    def query_grad(self, b):
        c = self.cols
        dq = nn(self.turned[...], self.q[b])
        do = nn(self.turned2[...], self.o[b])
        self.put(self.hid, b * c, dq[:, :128])
        self.put(self.hid, b * c + 128, dq[:, 128:] + do[:, :128])
        self.put(self.hid, b * c + 256, do[:, 128:])

    def keys_grad(self, b):
        c = self.cols

        def finish(count):
            total = nn(self.turnedw[0], self.kv[b, 0])
            for s in range(1, count):
                total = total + nn(self.turnedw[s], self.kv[b, s])
            self.put(self.hid, b * c + c // 2, total)

        for count in range(1, self.window + 1):
            pl.when(self.s1 - self.s0 + 1 == count)(functools.partial(finish, count))

    def query_input(self, b):
        self.acc[...] += nt(self.q[b], self.w(ATT, b * self.cols, 256))

    def window_input(self, s):
        c, half = self.cols, self.width // 2

        def run():
            for k in range(2):
                for b in range(4):
                    w = self.g[ATT, 2 * k : 2 * k + 2, :, :, b * c + c // 2 : b * c + c].reshape(half, c // 2)
                    part = nt(self.kv[b, s], w)
                    self.dkv_acc[k] = part if b == 0 else self.dkv_acc[k] + part
                self.xw[s, :, k * half : k * half + half] = self.dkv_acc[k].astype(BF16)

        if s == 0:
            run()
        else:
            pl.when(self.s0 + s <= self.s1)(run)


WAYS = (NEAR, LONG, LONG, NEAR, LONG, LONG)
BACK_WAYS = (DIRECT, DIRECT, DIRECT, DIRECT, LONG, DIRECT)


def chunks_of(order, cols, ways):
    w = cols // 2
    return [(order[k // 2], k % 2 * w, w, ways[k]) for k in range(6)]


ORDER = (
    ("own", 0), ("own", 1), ("share",), ("p", 0, 0), ("sp", 0), ("start",), ("masks",), ("z", 0, 1, 0),
    ("z", 0, 2, 0), ("p", 1, 0), ("sp", 1), ("z", 1, 1, 0), ("z", 1, 2, 0), ("own", 2), ("sp", 2),
    ("z", 1, 1, 1), ("z", 1, 2, 1), ("z", 0, 3, 0), ("p", 2, 0), ("own", 3), ("z", 2, 1, 0), ("z", 1, 3, 0),
    ("p", 0, 1), ("p", 0, 2), ("p", 0, 3), ("z", 1, 3, 1), ("z", 2, 2, 0), ("z", 2, 3, 0), ("shared",),
    ("z", 3, 1, 0), ("own", 4), ("sp", 3), ("z", 3, 2, 0), ("sp", 4), ("t", 0, 0), ("z", 2, 1, 1),
    ("z", 2, 2, 1), ("t", 0, 1), ("t", 1, 0), ("t", 1, 1), ("t", 2, 0), ("cw", 0), ("z", 2, 3, 1), ("own", 5),
    ("q", 0), ("q", 1), ("q", 2), ("q", 3), ("cw", 1), ("kv", 0), ("kv", 1), ("z", 3, 3, 0), ("kv", 2),
    ("p", 4, 0), ("kv", 3), ("att", 0), ("p", 3, 0), ("p", 3, 1), ("p", 3, 2), ("att", 1), ("z", 5, 1, 0),
    ("z", 5, 2, 0), ("z", 4, 1, 0), ("z", 4, 2, 0), ("t", 2, 1), ("att", 2), ("p", 5, 0), ("att", 3),
    ("p", 3, 3), ("z", 4, 3, 0), ("br", 0), ("br", 1), ("z", 4, 1, 1), ("z", 4, 2, 1), ("br", 2), ("br", 3),
    ("n1",), ("z", 5, 3, 0), ("cw", 2), ("up", 0, 0), ("up", 1, 0), ("up", 2, 0), ("up", 3, 0), ("z", 4, 3, 1),
    ("t", 3, 0), ("t", 3, 1), ("z", 5, 1, 1), ("z", 5, 2, 1), ("t", 5, 0), ("t", 4, 0), ("t", 4, 1),
    ("z", 5, 3, 1), ("cw", 3), ("up", 0, 1), ("up", 1, 1), ("up", 2, 1), ("up", 3, 1), ("t", 5, 1), ("cw", 4),
    ("dn", 0, 0), ("dn", 1, 0), ("dn", 2, 0), ("dn", 3, 0), ("cw", 5), ("dn", 0, 1), ("dn", 1, 1), ("dn", 2, 1),
    ("dn", 3, 1), ("n2",), ("sent",), ("hb", 0, 0), ("hb", 1, 0), ("hb", 2, 0), ("hb", 3, 0), ("cs", 0),
    ("hb", 0, 1), ("hb", 1, 1), ("hb", 2, 1), ("ce", 0, 1), ("hb", 3, 1), ("cs", 1), ("ce", 0, 0), ("ub", 0),
    ("ub", 1), ("ce", 1, 1), ("ub", 2), ("ub", 3), ("n1b",), ("gu", 0, 0), ("gu", 1, 0), ("gu", 2, 0),
    ("gu", 3, 0), ("cs", 2), ("gu", 0, 1), ("gu", 1, 1), ("gu", 2, 1), ("gu", 3, 1), ("cs", 3), ("mb", 0),
    ("ab", 0, 0), ("te", 0, 1), ("ab", 0, 1), ("ab", 0, 2), ("kb", 0), ("ce", 2, 1), ("te", 0, 0), ("mb", 1),
    ("ab", 1, 0), ("ab", 1, 1), ("ce", 2, 0), ("ce", 1, 0), ("ab", 1, 2), ("kb", 1), ("mb", 2), ("te", 1, 1),
    ("ab", 2, 0), ("se", 0), ("ab", 2, 1), ("ab", 2, 2), ("kb", 2), ("mb", 3), ("ab", 3, 0), ("ab", 3, 1),
    ("ab", 3, 2), ("ce", 3, 1), ("kb", 3), ("ce", 3, 0), ("te", 2, 1), ("sm0",), ("turn",), ("aq", 0),
    ("ak", 0), ("aq", 1), ("ak", 1), ("te", 1, 0), ("se", 1), ("aq", 2), ("sm", 0), ("ak", 2), ("te", 3, 1),
    ("aq", 3), ("ak", 3), ("te", 2, 0), ("cs", 4), ("cs", 5), ("wi", 0), ("wi", 1), ("se", 2), ("home",),
    ("qi", 0), ("la", 0), ("qi", 1), ("qi", 2), ("qi", 3), ("own_in",), ("te", 3, 0), ("sm", 1), ("ce", 4, 1),
    ("ce", 5, 1), ("ce", 4, 0), ("ce", 5, 0), ("se", 3), ("take",), ("te", 4, 1), ("zs", 4, 1, 0),
    ("zs", 4, 1, 1), ("zs", 4, 1, 2), ("sm", 2), ("te", 5, 1), ("te", 4, 0), ("zs", 4, 0, 0), ("zs", 4, 0, 1),
    ("zs", 4, 0, 2), ("la", 1), ("te", 5, 0), ("zl", 4, 1), ("se", 5), ("la", 2), ("sm", 3), ("sm", 4),
    ("zl", 4, 0), ("la", 4), ("la", 3), ("la", 5),
)

INPUTS = ("m_qkv", "m_out", "m_up", "m_down", "m_norm", "m_bias", "tok", "out_grad", "seg", "grp", "ans")
OUTPUTS = ("block_out", "input_grad", "owned", "sums", "squares")


def kernel(names, chunks, back_chunks, pairs, *refs):
    r = dict(zip(names, refs))
    pc = Place()
    loads = {n: pltpu.make_async_copy(r["hbm_" + n], r[n], r["load_sems"].at[k]) for k, n in enumerate(INPUTS)}
    stores = {n: pltpu.make_async_copy(r[n], r["hbm_" + n], r["store_sems"].at[k]) for k, n in enumerate(OUTPUTS)}
    for copy in loads.values():
        copy.start()
    all_here = greet(pc)
    r["squares"][...] = jnp.zeros_like(r["squares"])
    for n in INPUTS[:6]:
        loads[n].wait()
    gather = Gather(pc, r["g"], chunks, [r["gs%d" % k] for k in range(8)])
    lower_masters(r, pc, chunks, gather)
    layer = Layer(r, pc)
    rows, length = layer.rows, layer.length
    tok, tokw, window, xr, owned = r["tok"], r["tokw"], r["xw"], r["xrecv"], r["owned"]
    share = Share(
        pc,
        pairs,
        lambda low, high, target: tok.at[pl.ds(low % rows, high - low)],
        lambda low, high, target: tokw.at[in_window(low, high, target, rows, length)],
        r["share_sems"],
    )
    home = Share(
        pc,
        [(t, s, low, high) for s, t, low, high in pairs],
        lambda low, high, target: window.at[in_window(low, high, other_end(pairs, target, low), rows, length)],
        lambda low, high, target: xr.at[1 if low % rows == 0 else 0, pl.ds(0, high - low)],
        r["home_sems"],
    )
    spread = Sum5(pc, r["table"], r["table_slots"], r["table_sems"])
    total = Sum5(pc, r["sums"], r["sum_slots"], r["sum_sems"])

    def emit(j, value):
        a, low, w, _ = back_chunks[j]
        owned[a, :, low : low + w] = value
        line = col_sum(value * value)
        r["squares"][...] += sum(line[:, k : k + 128] for k in range(0, w, 128))

    grads = (r["hid"], r["g"].at[UP], r["g"].at[DOWN])
    back = Scatter(
        pc, grads, back_chunks, r["rc"], r["r3"], r["r2"], r["rz"], [r["ss%d" % k] for k in range(9)], emit
    )

    def start():
        for m in range(4):

            def own_tokens(m=m):
                for at, where in own_parts(m, rows, length):
                    tokw[where[0], where[1], :] = tok[at, :]

            pl.when(pc.m == m)(own_tokens)

    def share_start():
        loads["tok"].wait()
        share.start()

    def masks():
        for n in ("seg", "grp", "ans"):
            loads[n].wait()
        layer.masks()

    def second_norm():
        loads["out_grad"].wait()
        layer.second_norm()
        stores["block_out"].start()

    def table_step(k):
        spread.end(k)
        if k < 4:
            spread.start(k + 1)
        else:
            r["tab"][...] = r["table"][...].astype(F32)

    def sums_start():
        r["sums"][14:16, :] = jnp.zeros_like(r["sums"][14:16, :])
        total.start(0)

    def sums_step(k):
        total.end(k)
        if k < 4:
            total.start(k + 1)
        else:
            stores["sums"].start()

    def sent():
        gather.finish()
        share.wait_send()
        spread.finish()

    def homeward():
        for m in range(4):

            def own_rows(m=m):
                for at, where in own_parts(m, rows, length):
                    r["acc"][at, :] += window[where[0], where[1], :].astype(F32)

            pl.when(pc.m == m)(own_rows)

    def take():
        home.wait_recv()
        for source, target, low, high in home.pairs:

            def add(source=source, target=target, low=low, high=high):
                at = slice(low - target * rows, high - target * rows)
                k = 1 if low % rows == 0 else 0
                r["acc"][at, :] += xr[k, : high - low, :].astype(F32)

            pl.when(pc.m == target)(add)
        r["input_grad"][...] = r["acc"][...].astype(BF16)
        stores["input_grad"].start()

    steps = {
        "own": gather.own,
        "z": gather.z_step,
        "p": gather.p_step,
        "t": gather.t_step,
        "cw": gather.core_wait,
        "share": share_start,
        "shared": share.wait_recv,
        "sp": table_step,
        "sent": sent,
        "start": start,
        "masks": masks,
        "q": layer.queries,
        "kv": layer.keys_values,
        "att": layer.attend,
        "br": layer.branch,
        "n1": layer.first_norm,
        "up": layer.up,
        "dn": layer.down,
        "n2": second_norm,
        "hb": layer.hidden_back,
        "ub": layer.up_back,
        "n1b": layer.first_back,
        "gu": layer.up_grad,
        "mb": layer.mixed_back,
        "ab": layer.attend_back,
        "kb": layer.keys_back,
        "sm0": sums_start,
        "sm": sums_step,
        "turn": layer.turn,
        "aq": layer.query_grad,
        "ak": layer.keys_grad,
        "qi": layer.query_input,
        "wi": layer.window_input,
        "home": home.start,
        "own_in": homeward,
        "take": take,
        "cs": back.core_start,
        "ce": back.core_end,
        "te": back.third_end,
        "se": back.second_end,
        "zs": back.z_step,
        "zl": back.z_last,
        "la": back.last,
    }
    all_here()
    spread.start(0)
    for name, *at in ORDER:
        steps[name](*at)

    stores["owned"].start()
    norm = Total(pc, r["squares"], r["norm_slots"], r["norm_sems"])
    norm.run()
    stores["squares"].start()
    home.wait_send()
    back.finish()
    total.finish()
    norm.finish()
    for copy in stores.values():
        copy.wait()


def lower_masters(r, pc, chunks, gather):
    qkv, table = r["m_qkv"], r["table"]
    local = qkv.shape[2]
    for j, (a, low, w, _) in enumerate(chunks):
        ref = gather.piece(j, pc.z, 0, 0)
        if a == ATT:
            pair = (qkv[0], r["m_out"][...].T) if low == 0 else (qkv[1], qkv[2])
            ref[...] = jnp.concatenate(pair, 1).astype(BF16)
        else:
            ref[...] = r["m_up" if a == UP else "m_down"][:, low : low + w].astype(BF16)
    outer = pc.z * 2 + pc.x
    norm, bias = r["m_norm"], r["m_bias"]
    part, piece = norm.shape[2], bias.shape[1]
    width, columns = table.shape[1], 8 * piece
    wide = r["norm_wide"]
    wide[...] = jnp.zeros_like(wide)
    for k in range(6):
        wide[k : k + 1, :part] = norm[k]
    rows = pltpu.roll(wide[...], pc.m * local + outer * part, 1)
    line = r["bias_wide"]
    line[...] = jnp.zeros_like(line)
    line[0:1, :piece] = bias[...]
    line = pltpu.roll(line[...], outer * piece, 1)[0:1]
    head = line[:, : 2 * local]
    early = lax.broadcasted_iota(jnp.int32, head.shape, 1) < local
    attention = jnp.concatenate([jnp.where(early, head, 0.0), jnp.where(early, 0.0, head)], 1)
    hidden = line[:, 2 * local :]
    row = lax.broadcasted_iota(jnp.int32, (8, width), 0)
    top = jnp.where(row < 6, rows, 0.0)
    top = jnp.where(row == 6 + pc.m, attention, top)
    top = jnp.where(row == 10 + pc.m, hidden, top)
    low = jnp.where(row + 8 == 6 + pc.m, attention, 0.0)
    low = jnp.where(row + 8 == 10 + pc.m, hidden, low)
    table[...] = jnp.concatenate([top, low], 0).astype(BF16)


def other_end(pairs, owner, low):
    return [t for s, t, first, _ in pairs if s == owner and first == low][0]


def in_window(low, high, m, rows, length):
    return low // length - m * rows // length, pl.ds(low % length, high - low)


def own_parts(m, rows, length):
    parts, low = [], m * rows
    while low < (m + 1) * rows:
        high = min((m + 1) * rows, (low // length + 1) * length)
        parts.append((slice(low - m * rows, high - m * rows), in_window(low, high, m, rows, length)))
        low = high
    return parts


def run_layer(masters, tok, out_grad, seg, grp, ans, pad):
    per, cols = masters[2].shape
    rows, width = tok.shape
    length = seg.shape[1]
    hidden = 4 * cols
    window = max((m * rows + rows - 1) // length - m * rows // length + 1 for m in range(4))
    blocks = rows // 128
    pairs = overlaps(rows, length)
    chunks = chunks_of((ATT, UP, DOWN), cols, WAYS)
    back_chunks = chunks_of((DOWN, UP, ATT), cols, BACK_WAYS)
    most = max(high - low for _, _, low, high in pairs)
    bufs, sems = scatter_scratch(back_chunks, per)
    scratch = {
        "g": pltpu.VMEM((3, 4, 2, per, hidden), BF16),
        "table": pltpu.VMEM((16, width), BF16),
        "norm_wide": pltpu.VMEM((8, width), F32),
        "bias_wide": pltpu.VMEM((8, 8 * masters[5].shape[1]), F32),
        "tab": pltpu.VMEM((16, width), F32),
        "table_slots": pltpu.VMEM((10, 16, width), BF16),
        "tokw": pltpu.VMEM((window, length, width), BF16),
        "bias": pltpu.VMEM((blocks, 128, length), F32),
        "q": pltpu.VMEM((4, rows, 256), BF16),
        "kv": pltpu.VMEM((4, window, length, cols // 2), BF16),
        "shares": pltpu.VMEM((4, blocks, 3, 128, length), BF16),
        "o": pltpu.VMEM((4, rows, 256), BF16),
        "do": pltpu.VMEM((rows, 256), BF16),
        "dkv_acc": pltpu.VMEM((window, length, cols // 2), F32),
        "acc": pltpu.VMEM((rows, width), F32),
        "xh": pltpu.VMEM((rows, width), F32),
        "rs": pltpu.VMEM((rows, 1), F32),
        "hb": pltpu.VMEM((rows, width), BF16),
        "dz": pltpu.VMEM((rows, width), BF16),
        "hid": pltpu.VMEM((4, 2, per, hidden), BF16),
        "turned": pltpu.VMEM((width, rows), BF16),
        "turned2": pltpu.VMEM((width, rows), BF16),
        "turnedw": pltpu.VMEM((window, width, length), BF16),
        "xw": pltpu.VMEM((window, length, width), BF16),
        "xrecv": pltpu.VMEM((2, most, width), BF16),
        "sum_slots": pltpu.VMEM((10, 16, width), F32),
        "share_sems": pltpu.SemaphoreType.DMA((4,)),
        "home_sems": pltpu.SemaphoreType.DMA((4,)),
        "table_sems": pltpu.SemaphoreType.DMA((10,)),
        "norm_slots": pltpu.VMEM((12, 8, 128), F32),
        "norm_sems": pltpu.SemaphoreType.DMA((20,)),
        "sum_sems": pltpu.SemaphoreType.DMA((10,)),
    }
    scratch.update(zip(("rc", "r3", "r2", "rz"), bufs))
    scratch.update(("gs%d" % k, s) for k, s in enumerate(gather_sems(len(chunks))))
    scratch.update(("ss%d" % k, s) for k, s in enumerate(sems))
    given = dict(zip(INPUTS, list(masters) + [tok, out_grad, seg, grp, ans]))
    scratch.update((n, pltpu.VMEM(v.shape, v.dtype)) for n, v in given.items())
    made = dict(
        block_out=jax.ShapeDtypeStruct((rows, width), BF16),
        input_grad=jax.ShapeDtypeStruct((rows, width), BF16),
        owned=jax.ShapeDtypeStruct((3, per, cols), F32),
        sums=jax.ShapeDtypeStruct((16, width), F32),
        squares=jax.ShapeDtypeStruct((8, 128), F32),
    )
    scratch.update((n, pltpu.VMEM(v.shape, v.dtype)) for n, v in made.items())
    scratch["load_sems"] = pltpu.SemaphoreType.DMA((len(INPUTS),))
    scratch["store_sems"] = pltpu.SemaphoreType.DMA((len(OUTPUTS),))
    names = tuple("hbm_" + n for n in INPUTS) + ("pad",) + tuple("hbm_" + n for n in OUTPUTS) + tuple(scratch)
    anywhere = pl.BlockSpec(memory_space=pl.ANY)
    return pl.pallas_call(
        functools.partial(kernel, names, chunks, back_chunks, pairs),
        out_shape=list(made.values()),
        in_specs=[anywhere] * len(INPUTS) + [pl.BlockSpec(memory_space=pltpu.SMEM)],
        out_specs=[anywhere] * len(OUTPUTS),
        scratch_shapes=list(scratch.values()),
        compiler_params=pltpu.CompilerParams(collective_id=0, has_side_effects=True, vmem_limit_bytes=62 * 2**20),
        name="layer",
    )(*masters, tok, out_grad, seg, grp, ans, pad)


def adam_update(weight, grad, first, second, factor, decayed, rate):
    clipped = grad * factor
    first_new = beta_first * first + (1.0 - beta_first) * clipped
    second_new = beta_second * second + (1.0 - beta_second) * clipped * clipped
    ratio = (
        first_new
        / (1.0 - beta_first**STEP)
        / (jnp.sqrt(second_new / (1.0 - beta_second**STEP)) + adam_epsilon)
    )
    if decayed:
        ratio = ratio + decay_rate * weight
    return (weight - rate * ratio, first_new, second_new)


def update_kernel(*refs):
    given, (block_out, input_grad, norm_out), made = refs[:23], refs[23:26], refs[26:44]
    held, (grad_norm, load_sems, store_sems) = refs[44:67], refs[67:]
    loads = [pltpu.make_async_copy(a, b, load_sems.at[k]) for k, (a, b) in enumerate(zip(given, held))]
    outs = [held[2 + n * 6 + k] for n in range(3) for k in range(6)]
    stores = [pltpu.make_async_copy(a, b, store_sems.at[k]) for k, (a, b) in enumerate(zip(outs, made))]
    order = [1, 22, 0] + [2 + n * 6 + k for k in (2, 3, 0, 1, 4, 5) for n in range(3)] + [20, 21]
    for k in order:
        loads[k].start()
    passed = [
        pltpu.make_async_copy(held[20], block_out, store_sems.at[18]),
        pltpu.make_async_copy(held[21], input_grad, store_sems.at[19]),
        pltpu.make_async_copy(grad_norm, norm_out, store_sems.at[20]),
    ]
    owned, total = held[:2]
    masters, firsts, seconds = held[2:8], held[8:14], held[14:20]
    loads[1].wait()
    loads[22].wait()
    place = lax.axis_index("outer") * lax.axis_size("inner") + lax.axis_index("inner")
    mp = lax.axis_index("mp")
    local = masters[0].shape[2]
    width = total.shape[1]
    lane = lax.broadcasted_iota(jnp.int32, (4, width), 1)
    head, hidden = total[6:10, :], total[10:14, :]
    head = jnp.where((lane < local) | (lane >= 3 * local), head, 0.0)

    def square(v):
        return jnp.sum(jnp.sum(v * v, 0, keepdims=True), 1, keepdims=True)

    squares = jnp.sum(held[22][0:1, :], 1, keepdims=True) + square(total[0:6, :]) + square(head) + square(hidden)
    norm = jnp.sqrt(squares)
    grad_norm[...] = norm
    passed[2].start()
    factor = jnp.minimum(1.0, clip_limit / norm)
    mine = lax.broadcasted_iota(jnp.int32, (4, width), 0) == mp
    head = jnp.sum(jnp.where(mine, head, 0.0), 0, keepdims=True)
    hidden = jnp.sum(jnp.where(mine, hidden, 0.0), 0, keepdims=True)
    line = jnp.concatenate([head[:, : 2 * local] + head[:, 2 * local :], hidden], 1)
    part, piece = masters[4].shape[2], masters[5].shape[1]
    line = jnp.broadcast_to(line, (8, line.shape[1]))
    line = pltpu.roll(line, lax.rem(line.shape[1] - place * piece, line.shape[1]), 1)[0:1, :piece]
    norms = pltpu.roll(total[0:8, :], lax.rem(width - (mp * local + place * part), width), 1)

    def update(k, at, grad):
        values = adam_update(masters[k][at], grad, firsts[k][at], seconds[k][at], factor, k < 4, learn_rates[k])
        for n, value in enumerate(values):
            outs[n * 6 + k][at] = value

    def ready(k):
        for n in range(3):
            loads[2 + n * 6 + k].wait()

    def done(k):
        for n in range(3):
            stores[n * 6 + k].start()

    loads[0].wait()
    everything = (slice(None), slice(None))
    for k, grad in ((2, owned[1]), (3, owned[2])):
        ready(k)
        update(k, everything, grad)
        done(k)
    attention = owned[0]
    ready(0)
    update(0, 0, attention[:, :local])
    update(0, 1, attention[:, 2 * local : 3 * local])
    update(0, 2, attention[:, 3 * local :])
    done(0)
    ready(1)
    update(1, everything, attention[:, local : 2 * local].T)
    done(1)
    ready(4)
    for k in range(6):
        update(4, k, norms[k : k + 1, :part])
    done(4)
    ready(5)
    update(5, everything, line)
    done(5)
    for k in range(2):
        loads[20 + k].wait()
        passed[k].start()
    for copy in stores + passed:
        copy.wait()


def update(owned, total, squares, block_out, input_grad, masters, firsts, seconds):
    anywhere = pl.BlockSpec(memory_space=pl.ANY)
    given = [owned, total, *masters, *firsts, *seconds, block_out, input_grad, squares]

    def like(v):
        return jax.ShapeDtypeStruct(v.shape, v.dtype)

    return pl.pallas_call(
        update_kernel,
        out_shape=[like(block_out), like(input_grad), jax.ShapeDtypeStruct((1, 1), F32)] + [like(m) for m in masters] * 3,
        in_specs=[anywhere] * len(given),
        out_specs=[anywhere] * 21,
        scratch_shapes=[pltpu.VMEM(v.shape, v.dtype) for v in given]
        + [pltpu.VMEM((1, 1), F32), pltpu.SemaphoreType.DMA((len(given),)), pltpu.SemaphoreType.DMA((21,))],
        compiler_params=pltpu.CompilerParams(vmem_limit_bytes=62 * 2**20),
        name="update",
    )(*given)


def body(tokens, out_grad, segment_ids, group_ids, answer_ids, pad_lengths, *states):
    def turned(values):
        return [v.T if k == 3 else v for k, v in enumerate(values)]

    masters, firsts, seconds = turned(states[:6]), turned(states[6:12]), turned(states[12:])
    inner = lax.axis_size("inner")
    shared = masters
    if inner > 1:
        shared = [lax.all_gather(v, "inner", axis=d, tiled=True) for v, d in zip(masters, (1, 1, 0, 0, 2, 1))]
    block_out, input_grad, owned, total, squares = run_layer(
        shared, tokens, out_grad, segment_ids, group_ids, answer_ids, pad_lengths
    )
    if inner > 1:
        owned = lax.psum_scatter(owned, "inner", scatter_dimension=1, tiled=True)
        total = lax.psum(total, "inner")
        squares = lax.psum(jnp.sum(owned * owned), ("outer", "inner", "mp"))
        squares = jnp.full((8, 128), squares / 128)
    results = update(owned, total, squares, block_out, input_grad, masters, firsts, seconds)
    updated = [v for n in range(3) for v in turned(results[3 + 6 * n : 9 + 6 * n])]
    return (results[0], results[1], results[2][0, 0]) + tuple(updated)


def solution(mesh):
    dp = mesh.shape["dp"]
    outer = 8
    grid = Mesh(mesh.devices.reshape(outer, dp // outer, mesh.shape["mp"]), ("outer", "inner", "mp"))
    d = ("outer", "inner")
    both = P(d + ("mp",), None)
    states = (P(None, d, "mp"), P("mp", d), P(d, "mp"), P("mp", d), P(None, "mp", d), P("mp", d))
    in_specs = (both, both, P(d, None), P(d, None), P(d, None), P(d)) + states * 3
    out_specs = (both, both, P()) + states * 3
    return jax.shard_map(body, mesh=grid, in_specs=in_specs, out_specs=out_specs, check_vma=False)
```

```python
import functools
import jax
import jax.numpy as jnp
import numpy as np
from jax import lax
from jax.sharding import Mesh, PartitionSpec as P
from jax.experimental import pallas as pl
from jax.experimental.pallas import tpu as pltpu

MESH = pl.DeviceIdType.MESH
F32 = jnp.float32
BF16 = jnp.bfloat16
HD = 64
STEP = 5

norm_epsilon = 1e-06
adam_epsilon = 1e-08
learn_rates = (0.02, 0.1, 0.02, 0.02, 0.5, 0.5)
beta_first = 0.5
beta_second = 0.5
decay_rate = 0.01
clip_limit = 0.05
mask_fill = -1000000000.0
score_scale = 0.125

ATT, UP, DOWN = 0, 1, 2
NEAR, LONG, DIRECT = 0, 1, 2


def pick(index, values):
    out = values[-1]
    for k in range(len(values) - 1):
        out = jnp.where(index == k, values[k], out)
    return out


class Place:
    def __init__(self):
        outer = lax.axis_index("outer")
        self.sub = lax.axis_index("inner")
        self.m = lax.axis_index("mp")
        self.z = outer // 2
        self.x = lax.rem(outer, 2)
        self.y = self.m // 2
        self.c = lax.rem(self.m, 2)
        self.first = self.c == 0
        self.sib = self.at(c=1 - self.c)
        x, y = self.line(1, 0)
        self.second = self.at(x=x, y=y)
        x, y = self.line(0, 1)
        self.third = self.at(x=x, y=y)

    def at(self, z=None, x=None, y=None, c=None):
        z = self.z if z is None else z
        x = self.x if x is None else x
        y = self.y if y is None else y
        c = self.c if c is None else c
        return (z * 2 + x, self.sub, y * 2 + c)

    def mate(self, m):
        return (self.z * 2 + self.x, self.sub, m)

    def line(self, side, far, other_core=False):
        first = (1 - self.c if other_core else self.c) == 0
        x = jnp.where(first, side, far)
        y = jnp.where(first, far, side)
        return self.x + x - 2 * self.x * x, self.y + y - 2 * self.y * y

    def order(self, t):
        return pick(self.z, [(0, 1, 2, 3), (1, 0, 3, 2), (2, 2, 1, 1), (3, 3, 0, 0)][t])


def remote(src, dst, send, recv, device):
    return pltpu.make_async_remote_copy(
        src_ref=src, dst_ref=dst, send_sem=send, recv_sem=recv, device_id=device, device_id_type=MESH
    )


def peers(place):
    z, x, y, c = place.z, place.x, place.y, place.c

    def other(v, bit):
        return 1 - v if bit else v

    plane = [place.at(x=other(x, k & 4), y=other(y, k & 2), c=other(c, k & 1)) for k in range(1, 8)]
    return plane + [place.at(z=across(z, k)) for k in range(1, 4)]


def across(z, k):
    low, high = lax.rem(z, 2), z // 2
    return (1 - high if k & 2 else high) * 2 + (1 - low if k & 1 else low)


def greet(place):
    barrier = pltpu.get_barrier_semaphore()
    for device in peers(place):
        pl.semaphore_signal(barrier, inc=1, device_id=device, device_id_type=MESH)
    return lambda: pl.semaphore_wait(barrier, 10)


class Gather:
    def __init__(self, place, g, chunks, sems):
        self.p, self.g, self.chunks = place, g, chunks
        self.zs, self.zr, self.ps, self.pr, self.ts, self.tr, self.cs, self.cr = sems
        self.width = g.shape[4] // 4
        self.sent = []

    def piece(self, j, z, side, far, core=False):
        x, y = self.p.line(side, far, core)
        c = 1 - self.p.c if core else self.p.c
        a, low, w, _ = self.chunks[j]
        cols = pl.ds(pl.multiple_of((y * 2 + c) * self.width + low, 128), w)
        if z is None:
            return self.g.at[a, :, x, :, cols]
        return self.g.at[a, z, x, :, cols]

    def go(self, ref, send, recv, device, when=None):
        copy = remote(ref, ref, send, recv, device)
        if when is None:
            copy.start()
        else:
            pl.when(when)(copy.start)
        self.sent.append((copy, when))

    def arrived(self, ref, recv):
        remote(ref, ref, recv, recv, self.p.sib).wait_recv()

    def z_send(self, j, side, src, index, to, when):
        self.go(self.piece(j, src, side, 0), self.zs.at[j, side, index], self.zr.at[j, side, src], self.p.at(z=to), when)

    def z_both(self, j, side):
        z = self.p.z
        self.z_send(j, side, z, z, z + 1, z < 3)
        self.z_send(j, side, z, 4, z - 1, z > 0)

    def third(self, j, side, src):
        k = side * 4 + src
        self.go(self.piece(j, src, side, 0), self.ts.at[j, k], self.tr.at[j, k], self.p.third)

    def second(self, j, src):
        self.go(self.piece(j, src, 0, 0), self.ps.at[j, src], self.pr.at[j, src], self.p.second)

    def to_sibling(self, j, side, far):
        k = side + 2 * far
        self.go(self.piece(j, None, side, far), self.cs.at[j, k], self.cr.at[j, k], self.p.sib)

    def own(self, j):
        self.second(j, self.p.z)
        self.z_both(j, 0)
        self.third(j, 0, self.p.z)

    def z_step(self, j, t, side=0):
        z = self.p.z
        src = self.p.order(t)
        self.arrived(self.piece(j, src, side, 0), self.zr.at[j, side, src])
        to = jnp.where(z > src, z + 1, z - 1)
        self.z_send(j, side, src, src, to, (to >= 0) & (to <= 3))
        if self.chunks[j][3] != LONG:
            self.second(j, src)
        self.third(j, side, src)
        if t == 3:
            self.to_sibling(j, side, 0)

    def p_step(self, j, t):
        src = self.p.order(t)
        self.arrived(self.piece(j, src, 1, 0), self.pr.at[j, src])
        if self.chunks[j][3] == LONG:
            self.z_both(j, 1)
        self.third(j, 1, src)
        if t == 3:
            self.to_sibling(j, 1, 0)

    def t_step(self, j, side):
        for t in range(4):
            src = self.p.order(t)
            self.arrived(self.piece(j, src, side, 1), self.tr.at[j, side * 4 + src])
        self.to_sibling(j, side, 1)

    def core_wait(self, j):
        for k, (side, far) in enumerate(((0, 0), (1, 0), (0, 1), (1, 1))):
            self.arrived(self.piece(j, None, side, far, True), self.cr.at[j, k])

    def finish(self):
        for copy, when in self.sent:
            if when is None:
                copy.wait_send()
            else:
                pl.when(when)(copy.wait_send)
        self.sent = []


def gather_sems(chunks):
    sizes = ((2, 5), (2, 4), (4,), (4,), (8,), (8,), (4,), (4,))
    return [pltpu.SemaphoreType.DMA((chunks,) + n) for n in sizes]


def overlaps(rows, length):
    pairs = []
    for m in range(3):
        edge = (m + 1) * rows
        low = edge // length * length
        if low == edge:
            continue
        pairs.append((m, m + 1, max(low, m * rows), edge))
        pairs.append((m + 1, m, edge, min(low + length, edge + rows)))
    return pairs


class Share:
    def __init__(self, place, pairs, src, dst, sems):
        self.p, self.pairs, self.src, self.dst, self.sems = place, pairs, src, dst, sems

    def copy(self, pair):
        source, target, low, high = pair
        k = 0 if source < target else 1
        return remote(self.src(low, high, target), self.dst(low, high, target), self.sems.at[k], self.sems.at[2 + k], self.p.mate(target))

    def start(self):
        for pair in self.pairs:
            pl.when(self.p.m == pair[0])(self.copy(pair).start)

    def wait_recv(self):
        for pair in self.pairs:
            pl.when(self.p.m == pair[1])(self.copy(pair).wait_recv)

    def wait_send(self):
        for pair in self.pairs:
            pl.when(self.p.m == pair[0])(self.copy(pair).wait_send)


class Sum5:
    def __init__(self, place, table, slots, sems):
        self.p, self.table, self.slots, self.sems = place, table, slots, sems
        z = place.z
        self.peers = [
            place.at(z=z + 1 - 2 * lax.rem(z, 2)),
            place.at(z=z + 2 - 4 * (z // 2)),
            place.at(x=1 - place.x),
            place.at(y=1 - place.y),
            place.sib,
        ]

    def copy(self, k):
        return remote(self.slots.at[5 + k], self.slots.at[k], self.sems.at[k], self.sems.at[5 + k], self.peers[k])

    def start(self, k):
        self.slots[5 + k] = self.table[...]
        self.copy(k).start()

    def end(self, k):
        self.copy(k).wait_recv()
        self.table[...] = self.table[...] + self.slots[k]

    def finish(self):
        for k in range(5):
            self.copy(k).wait_send()


class Total:
    def __init__(self, place, tile, slots, sems):
        self.p, self.tile, self.slots, self.sems = place, tile, slots, sems
        self.copies = [remote(slots.at[0 if k < 7 else 11], slots.at[1 + k], sems.at[k], sems.at[10 + k], d) for k, d in enumerate(peers(place))]

    def run(self):
        for first, ks in ((0, range(7)), (11, range(7, 10))):
            self.slots[first] = self.tile[...]
            for k in ks:
                self.copies[k].start()
            total = self.tile[...]
            for k in ks:
                self.copies[k].wait_recv()
                total = total + self.slots[1 + k]
            self.tile[...] = total

    def finish(self):
        for copy in self.copies:
            copy.wait_send()


class Scatter:
    def __init__(self, place, grads, chunks, rc, r3, r2, rz, sems, emit):
        self.p, self.grads, self.chunks = place, grads, chunks
        self.rc, self.r3, self.r2, self.rz = rc, r3, r2, rz
        self.cs, self.cr, self.ts, self.tr, self.ps, self.pr, self.us, self.ds, self.zr = sems
        self.emit = emit
        self.width = grads[0].shape[3] // 4
        self.sent = []
        self.seconds, self.lines, _, _ = scatter_slots(chunks)

    def region(self, j, side, far, core=False):
        x, y = self.p.line(side, far, core)
        c = 1 - self.p.c if core else self.p.c
        a, low, w, _ = self.chunks[j]
        return a, x, pl.ds(pl.multiple_of((y * 2 + c) * self.width + low, 128), w)

    def block(self, j, side, far, core=False):
        a, x, cols = self.region(j, side, far, core)
        return self.grads[a].at[:, x, :, cols]

    def shard(self, j, side, z):
        a, x, cols = self.region(j, side, 0)
        return self.grads[a].at[z, x, :, cols]

    def go(self, src, dst, send, recv, device, when=None):
        copy = remote(src, dst, send, recv, device)
        if when is None:
            copy.start()
        else:
            pl.when(when)(copy.start)
        self.sent.append((copy, when))

    def arrived(self, ref, recv):
        remote(ref, ref, recv, recv, self.p.sib).wait_recv()

    def core_start(self, j):
        for far in (1, 0):
            for side in (1, 0):
                k = far * 2 + side
                self.go(self.block(j, side, far, True), self.rc.at[j, k], self.cs.at[j, k], self.cr.at[j, k], self.p.sib)

    def add(self, j, side, far, other):
        a, x, cols = self.region(j, side, far)

        def step(k):
            here = self.grads[a].at[k, x, :, cols]
            here[...] = (here[...].astype(F32) + other[k].astype(F32)).astype(BF16)

        pl.loop(0, 4)(step)

    def core_end(self, j, far):
        for side in (1, 0):
            k = far * 2 + side
            self.arrived(self.rc.at[j, k], self.cr.at[j, k])
            self.add(j, side, far, self.rc.at[j, k])
            if far == 1:
                self.go(self.block(j, side, 1), self.r3.at[j, side], self.ts.at[j, side], self.tr.at[j, side], self.p.third)

    def third_end(self, j, side):
        self.arrived(self.r3.at[j, side], self.tr.at[j, side])
        self.add(j, side, 0, self.r3.at[j, side])
        if self.chunks[j][3] == LONG:
            self.line_start(j, side)
        elif side == 1:
            slot = self.r2.at[pl.ds(self.seconds[j], 4)]
            self.go(self.block(j, 1, 0), slot, self.ps.at[j], self.pr.at[j], self.p.second)

    def second_end(self, j):
        slot = self.r2.at[pl.ds(self.seconds[j], 4)]
        self.arrived(slot, self.pr.at[j])
        self.add(j, 0, 0, slot)
        if self.chunks[j][3] != DIRECT:
            self.line_start(j, 0)
            return
        n = self.lines[j]
        for k in (3, 2, 1):
            to = across(self.p.z, k)
            self.go(self.shard(j, 0, to), self.rz.at[n, k], self.us.at[n, k], self.zr.at[n, k], self.p.at(z=to))

    def up(self, j, side, d, when):
        n = self.lines[j] + side
        self.go(self.shard(j, side, d), self.rz.at[n, d], self.us.at[n, d], self.zr.at[n, d], self.p.at(z=self.p.z + 1), when)

    def down(self, j, side, d, when):
        n = self.lines[j] + side
        slot = jnp.where(d == self.p.z - 1, 4, d)
        self.go(self.shard(j, side, d), self.rz.at[n, slot], self.ds.at[n, d], self.zr.at[n, slot], self.p.at(z=self.p.z - 1), when)

    def line_start(self, j, side):
        z = self.p.z
        for d in range(3):
            self.up(j, side, 3 - d, z == 0)
            self.down(j, side, d, z == 3)

    def fold(self, j, side, d, slot):
        n = self.lines[j] + side
        self.arrived(self.rz.at[n, slot], self.zr.at[n, slot])
        ref = self.shard(j, side, d)
        ref[...] = (ref[...].astype(F32) + self.rz[n, slot].astype(F32)).astype(BF16)

    def relay(self, j, side, d, send, when):
        pl.when(when)(lambda: self.fold(j, side, d, d))
        send(j, side, d, when)

    def z_step(self, j, side, t):
        z = self.p.z
        if t < 2:
            self.relay(j, side, 3 - t, self.up, z == 1)
            self.relay(j, side, t, self.down, z == 2)
        else:
            self.relay(j, side, 3, self.up, z == 2)
            self.relay(j, side, 0, self.down, z == 1)

    def z_last(self, j, side):
        z = self.p.z
        pl.when(z > 0)(lambda: self.fold(j, side, z, z))
        pl.when(z < 3)(lambda: self.fold(j, side, z, 4))
        if side == 1:
            slot = self.r2.at[self.seconds[j]]
            self.go(self.shard(j, 1, z), slot, self.ps.at[j], self.pr.at[j], self.p.second)

    def last(self, j):
        z = self.p.z
        if self.chunks[j][3] == DIRECT:
            n = self.lines[j]
            total = self.shard(j, 0, z)[...].astype(F32)
            for k in (1, 2, 3):
                self.arrived(self.rz.at[n, k], self.zr.at[n, k])
                total = total + self.rz[n, k].astype(F32)
            self.emit(j, total)
        elif self.chunks[j][3] == LONG:
            slot = self.r2.at[self.seconds[j]]
            self.arrived(slot, self.pr.at[j])
            self.emit(j, self.shard(j, 0, z)[...].astype(F32) + slot[...].astype(F32))
        else:
            self.z_last(j, 0)
            self.emit(j, self.shard(j, 0, z)[...].astype(F32))

    def finish(self):
        for copy, when in self.sent:
            if when is None:
                copy.wait_send()
            else:
                pl.when(when)(copy.wait_send)
        self.sent = []


def scatter_slots(chunks):
    seconds, lines, n, m = [], [], 0, 0
    for chunk in chunks:
        seconds.append(n)
        lines.append(m)
        n += 1 if chunk[3] == LONG else 4
        m += 2 if chunk[3] == LONG else 1
    return seconds, lines, n, m


def scatter_scratch(chunks, rows):
    n, w = len(chunks), chunks[0][2]
    _, _, seconds, lines = scatter_slots(chunks)
    shapes = ((n, 4, 4), (n, 2, 4), (seconds,), (lines, 5))
    sems = ((n, 4), (n, 4), (n, 2), (n, 2), (n,), (n,), (lines, 4), (lines, 4), (lines, 5))
    return [pltpu.VMEM(s + (rows, w), BF16) for s in shapes], [pltpu.SemaphoreType.DMA(s) for s in sems]


def nt(a, b):
    return lax.dot_general(a, b, (((1,), (1,)), ((), ())), preferred_element_type=F32)


def tn(a, b):
    return lax.dot_general(a, b, (((0,), (0,)), ((), ())), preferred_element_type=F32)


def nn(a, b):
    return jnp.dot(a, b, preferred_element_type=F32)


def even_lanes(shape):
    return lax.broadcasted_iota(jnp.int32, shape, 1) < HD


def keep(values, even):
    mask = even_lanes(values.shape)
    zero = jnp.zeros_like(values)
    return jnp.where(mask, values, zero) if even else jnp.where(mask, zero, values)


def col_sum(values):
    return jnp.sum(values, 0, keepdims=True)


class Layer:
    def __init__(self, refs, place):
        self.__dict__.update(refs)
        self.p = place
        self.rows, self.width = self.tok.shape
        self.length = self.seg.shape[1]
        self.blocks = self.rows // 128
        self.cols = self.g.shape[4] // 4
        self.hidden = self.g.shape[4]
        self.s0 = self.rows * place.m // self.length
        self.s1 = (self.rows * place.m + self.rows - 1) // self.length
        self.window = self.kv.shape[1]

    def w(self, a, low, size):
        return self.g[a, :, :, :, low : low + size].reshape(self.width, size)

    def put(self, ref, low, value):
        size = value.shape[1]
        ref[:, :, :, low : low + size] = value.astype(BF16).reshape(ref.shape[:3] + (size,))

    def gain(self, row):
        return self.tab[pl.ds(row, 1), :]

    def blk(self, i):
        return pl.ds(pl.multiple_of(i * 128, 128), 128)

    def seq_of(self, i):
        return (self.rows * self.p.m + 128 * i) // self.length

    def each_seq(self, run):
        for s in range(self.window):
            if s == 0:
                run(s)
            else:
                pl.when(self.s0 + s <= self.s1)(functools.partial(run, s))

    def masks(self):
        n = self.length
        for i in range(self.blocks):
            s = self.seq_of(i)
            at = lax.rem(self.rows * self.p.m + 128 * i, n)
            seg = self.seg[pl.ds(s, 1), :]
            grp = self.grp[pl.ds(s, 1), :]
            ans = self.ans[pl.ds(s, 1), :]
            seg_q = pick(at // 128, [seg[:, k : k + 128] for k in range(0, n, 128)])
            grp_q = pick(at // 128, [grp[:, k : k + 128] for k in range(0, n, 128)])
            code = jnp.where(seg_q == 0, -1, grp_q).astype(F32)
            code = jnp.transpose(jnp.broadcast_to(code, (8, 128)))[:, :1]
            open_key = (seg == 0) | (ans == 1)
            rule = (code == grp.astype(F32)) | (code < 0.0) | open_key
            position = lax.broadcasted_iota(jnp.int32, (1, n), 1)
            seen = rule & (position < self.pad[s])
            self.bias[i] = jnp.where(seen, 0.0, mask_fill)

    def queries(self, b):
        c = self.cols
        lanes = lax.broadcasted_iota(jnp.int32, (1, 256), 1) < c // 4
        q = nn(self.tok[...], self.w(ATT, b * c, 256)) + self.tab[6 + b : 7 + b, :256]
        self.q[b] = jnp.where(lanes, q * score_scale, 0.0).astype(BF16)

    def keys_values(self, b):
        c = self.cols
        wkv = self.w(ATT, b * c + c // 2, c // 2)

        def one(s):
            self.kv[b, s] = (nn(self.tokw[s], wkv) + self.tab[6 + b : 7 + b, c // 2 :]).astype(BF16)

        self.each_seq(one)

    def heads(self, b, i):
        s = self.seq_of(i) - self.s0
        q0 = self.q[b, self.blk(i), :128]
        q2 = self.q[b, self.blk(i), 128:]
        return s, keep(q0, True), keep(q0, False), q2

    def attend(self, b):
        @pl.loop(0, self.blocks)
        def _(i):
            s, q0, q1, q2 = self.heads(b, i)
            bias = self.bias[i]

            def softmax(scores):
                scores = scores + bias
                e = jnp.exp(scores - jnp.max(scores, -1, keepdims=True))
                return (e * (1.0 / jnp.sum(e, -1, keepdims=True))).astype(BF16)

            t0, t1, t2 = (self.kv[b, s, :, 128 * t : 128 * t + 128] for t in range(3))
            s01 = nt(jnp.concatenate([q0, q1], 0), t0)
            p0, p1, p2 = softmax(s01[:128]), softmax(s01[128:]), softmax(nt(q2, t1))
            self.shares[b, i, 0] = p0
            self.shares[b, i, 1] = p1
            self.shares[b, i, 2] = p2
            o12 = nn(jnp.concatenate([p1, p2], 0), t2)
            self.o[b, self.blk(i), :128] = keep(nn(p0, t1), False).astype(BF16)
            self.o[b, self.blk(i), 128:] = jnp.where(even_lanes((128, 128)), o12[:128], o12[128:]).astype(BF16)

    def row_loop(self, step, sums):
        n = 48

        def run(k, carry):
            at = pl.ds(pl.multiple_of(k * n, n), n)
            return step(at, carry)

        zero = tuple(jnp.zeros((1, self.width), F32) for _ in range(sums))
        return lax.fori_loop(0, self.rows // n, run, zero)

    def accumulate(self, value, first):
        self.acc[...] = value if first else self.acc[...] + value

    def branch(self, b):
        self.accumulate(nt(self.o[b], self.w(ATT, b * self.cols + 128, 256)), b == 0)

    def first_norm(self):
        g1, b1, co = self.gain(0), self.gain(1), self.gain(2)

        def step(at, carry):
            r = self.tok[at, :].astype(F32) + (self.acc[at, :] + co)
            r = r - jnp.mean(r, -1, keepdims=True)
            rs = lax.rsqrt(jnp.mean(r * r, -1, keepdims=True) + norm_epsilon)
            xh = r * rs
            self.xh[at, :] = xh
            self.rs[at, :] = rs
            self.hb[at, :] = (xh * g1 + b1).astype(BF16)
            return carry

        self.row_loop(step, 0)

    def part(self, b, k):
        n = self.cols // PARTS
        return b * self.cols + k * n, n

    def hidden_ref(self, which):
        return self.hid.at[2 * which : 2 * which + 2]

    def get_hidden(self, which, low, n):
        return self.hidden_ref(which)[:, :, :, low : low + n].reshape(self.rows, n)

    def set_hidden(self, which, low, value):
        ref = self.hidden_ref(which)
        ref[:, :, :, low : low + value.shape[1]] = value.astype(BF16).reshape(ref.shape[:3] + value.shape[1:])

    def up(self, b, k):
        low, n = self.part(b, k)
        u = nn(self.hb[...], self.w(UP, low, n)) + self.tab[10 + b : 11 + b, k * n : k * n + n]
        share = 0.5 + 0.5 * lax.erf(u * np.float32(np.sqrt(0.5)))
        self.set_hidden(0, low, u * share)
        self.set_hidden(1, low, share + u * (jnp.exp(-0.5 * (u * u)) * np.float32(1 / np.sqrt(2 * np.pi))))

    def down(self, b, k):
        low, n = self.part(b, k)
        self.accumulate(nt(self.get_hidden(0, low, n), self.w(DOWN, low, n)), b == 0 and k == 0)

    def second_norm(self):
        g1, b1, g2, b2, cd = self.gain(0), self.gain(1), self.gain(3), self.gain(4), self.gain(5)

        def step(at, carry):
            r = (self.xh[at, :] * g1 + b1) + (self.acc[at, :] + cd)
            r = r - jnp.mean(r, -1, keepdims=True)
            rs = lax.rsqrt(jnp.mean(r * r, -1, keepdims=True) + norm_epsilon)
            xh = r * rs
            self.block_out[at, :] = (xh * g2 + b2).astype(BF16)
            grad = self.out_grad[at, :].astype(F32)
            inner = grad * g2
            back = rs * (inner - jnp.mean(inner, -1, keepdims=True) - xh * jnp.mean(inner * xh, -1, keepdims=True))
            self.acc[at, :] = back
            low = back.astype(BF16)
            self.dz[at, :] = low
            return carry[0] + col_sum(grad * xh), carry[1] + col_sum(grad), carry[2] + col_sum(low.astype(F32))

        dg, db, dc = self.row_loop(step, 3)
        self.sums[3:4, :] = dg
        self.sums[4:5, :] = db
        self.sums[5:6, :] = dc

    def hidden_back(self, b, k):
        if b == 0 and k == 0:
            self.turned[...] = self.dz[...].T
        low, n = self.part(b, k)
        du = nn(self.dz[...], self.w(DOWN, low, n)) * self.get_hidden(1, low, n).astype(F32)
        du = du.astype(BF16)
        self.set_hidden(1, low, du)
        self.sums[10 + b : 11 + b, k * n : k * n + n] = col_sum(du.astype(F32))
        self.put(self.g.at[DOWN], low, nn(self.turned[...], self.get_hidden(0, low, n)))

    def up_back(self, b):
        low = b * self.cols
        self.acc[...] += nt(self.get_hidden(1, low, self.cols), self.w(UP, low, self.cols))

    def up_grad(self, b, k):
        if b == 0 and k == 0:
            self.turned[...] = self.hb[...].T
        low, n = self.part(b, k)
        self.put(self.g.at[UP], low, nn(self.turned[...], self.get_hidden(1, low, n)))

    def first_back(self):
        g1 = self.gain(0)

        def step(at, carry):
            grad = self.acc[at, :]
            xh = self.xh[at, :]
            inner = grad * g1
            back = self.rs[at, :] * (
                inner - jnp.mean(inner, -1, keepdims=True) - xh * jnp.mean(inner * xh, -1, keepdims=True)
            )
            self.acc[at, :] = back
            low = back.astype(BF16)
            self.dz[at, :] = low
            return carry[0] + col_sum(grad * xh), carry[1] + col_sum(grad), carry[2] + col_sum(low.astype(F32))

        dg, db, dc = self.row_loop(step, 3)
        self.sums[0:1, :] = dg
        self.sums[1:2, :] = db
        self.sums[2:3, :] = dc

    def mixed_back(self, b):
        do = nn(self.dz[...], self.w(ATT, b * self.cols + 128, 256))
        lanes = lax.broadcasted_iota(jnp.int32, (1, 256), 1) >= HD
        self.do[...] = jnp.where(lanes, do, 0.0).astype(BF16)
        self.dkv_acc[...] = jnp.zeros_like(self.dkv_acc)

    def attend_back(self, b, i):
        s, q0, q1, q2 = self.heads(b, i)
        t0, t1, t2 = (self.kv[b, s, :, 128 * t : 128 * t + 128] for t in range(3))
        do0 = self.do[self.blk(i), :128]
        do12 = self.do[self.blk(i), 128:]
        do1, do2 = keep(do12, True), keep(do12, False)
        dp12 = nt(jnp.concatenate([do1, do2], 0), t2)

        def back(h, dp):
            low = self.shares[b, i, h]
            p = low.astype(F32)
            scaled = p * dp
            return low, (scaled - p * jnp.sum(scaled, -1, keepdims=True)).astype(BF16)

        p0, ds0 = back(0, nt(do0, t1))
        p1, ds1 = back(1, dp12[:128])
        p2, ds2 = back(2, dp12[128:])
        dq01 = nn(jnp.concatenate([ds0, ds1], 0), t0)
        dq0 = jnp.where(even_lanes((128, 128)), dq01[:128], dq01[128:])
        dq2 = keep(nn(ds2, t1), True)
        self.q[b, self.blk(i), :128] = (dq0 * score_scale).astype(BF16)
        self.q[b, self.blk(i), 128:] = (dq2 * score_scale).astype(BF16)
        rows = jnp.concatenate
        self.dkv_acc[s, :, :128] += tn(rows([ds0, ds1], 0), rows([q0, q1], 0))
        self.dkv_acc[s, :, 128:256] += tn(rows([ds2, p0], 0), rows([q2, do0], 0))
        self.dkv_acc[s, :, 256:] += tn(rows([p1, p2], 0), rows([do1, do2], 0))

    def keys_back(self, b):
        c = self.cols
        total = jnp.zeros((1, c // 2), F32)
        for s in range(self.window):
            low = self.dkv_acc[s].astype(BF16)
            self.kv[b, s] = low
            total = total + col_sum(low.astype(F32))
        first = col_sum(self.q[b].astype(F32))
        gap = jnp.zeros((1, c // 2 - 256), F32)
        self.sums[6 + b : 7 + b, :] = jnp.concatenate([first, gap, total], 1)

    def turn(self):
        self.turned[...] = self.tok[...].T
        self.turned2[...] = self.dz[...].T

        def one(s):
            self.turnedw[s] = self.tokw[s].T

        self.each_seq(one)

    def query_grad(self, b):
        c = self.cols
        dq = nn(self.turned[...], self.q[b])
        do = nn(self.turned2[...], self.o[b])
        self.put(self.hid, b * c, dq[:, :128])
        self.put(self.hid, b * c + 128, dq[:, 128:] + do[:, :128])
        self.put(self.hid, b * c + 256, do[:, 128:])

    def keys_grad(self, b):
        c = self.cols

        def finish(count):
            total = nn(self.turnedw[0], self.kv[b, 0])
            for s in range(1, count):
                total = total + nn(self.turnedw[s], self.kv[b, s])
            self.put(self.hid, b * c + c // 2, total)

        for count in range(1, self.window + 1):
            pl.when(self.s1 - self.s0 + 1 == count)(functools.partial(finish, count))

    def query_input(self, b):
        self.acc[...] += nt(self.q[b], self.w(ATT, b * self.cols, 256))

    def window_input(self, s):
        c, half = self.cols, self.width // 2

        def run():
            for k in range(2):
                for b in range(4):
                    w = self.g[ATT, 2 * k : 2 * k + 2, :, :, b * c + c // 2 : b * c + c].reshape(half, c // 2)
                    part = nt(self.kv[b, s], w)
                    self.dkv_acc[k] = part if b == 0 else self.dkv_acc[k] + part
                self.xw[s, :, k * half : k * half + half] = self.dkv_acc[k].astype(BF16)

        if s == 0:
            run()
        else:
            pl.when(self.s0 + s <= self.s1)(run)


PARTS = 2
WAYS = (NEAR, LONG, LONG, NEAR, LONG, LONG)
BACK_WAYS = (DIRECT, LONG, DIRECT, LONG, DIRECT, DIRECT)


def chunks_of(order, cols, ways):
    w = cols // PARTS
    return [(order[k // PARTS], k % PARTS * w, w, ways[k]) for k in range(3 * PARTS)]


ORDER = (
    ("own", 0), ("own", 1), ("share",), ("own", 2), ("z", 0, 1, 0), ("sp", 0), ("z", 0, 2, 0), ("sp", 1),
    ("p", 2, 0), ("own", 3), ("own", 4), ("sp", 2), ("p", 1, 0), ("p", 0, 0), ("start",), ("z", 1, 1, 0),
    ("z", 1, 2, 0), ("masks",), ("z", 0, 3, 0), ("z", 1, 3, 0), ("z", 1, 1, 1), ("p", 4, 0), ("p", 0, 1),
    ("p", 0, 2), ("p", 0, 3), ("z", 1, 2, 1), ("z", 1, 3, 1), ("z", 3, 1, 0), ("z", 3, 2, 0), ("t", 0, 0),
    ("sp", 3), ("z", 3, 3, 0), ("t", 0, 1), ("z", 4, 1, 0), ("z", 4, 2, 0), ("z", 2, 1, 0), ("t", 1, 0),
    ("t", 1, 1), ("z", 2, 2, 0), ("own", 5), ("z", 4, 1, 1), ("z", 2, 1, 1), ("cw", 0), ("sp", 4), ("shared",),
    ("q", 0), ("q", 1), ("q", 2), ("q", 3), ("p", 3, 0), ("cw", 1), ("kv", 0), ("z", 2, 2, 1), ("kv", 1),
    ("kv", 2), ("z", 2, 3, 0), ("t", 3, 0), ("kv", 3), ("att", 0), ("z", 2, 3, 1), ("z", 4, 3, 0), ("p", 3, 1),
    ("att", 1), ("p", 3, 2), ("p", 3, 3), ("z", 5, 1, 0), ("z", 5, 2, 0), ("p", 5, 0), ("att", 2),
    ("z", 4, 2, 1), ("att", 3), ("t", 2, 0), ("t", 2, 1), ("br", 0), ("z", 4, 3, 1), ("br", 1), ("br", 2),
    ("z", 5, 3, 0), ("br", 3), ("t", 3, 1), ("z", 5, 1, 1), ("n1",), ("z", 5, 2, 1), ("t", 4, 0), ("cw", 2),
    ("up", 0, 0), ("up", 1, 0), ("z", 5, 3, 1), ("t", 4, 1), ("up", 2, 0), ("up", 3, 0), ("cw", 3), ("t", 5, 0),
    ("up", 0, 1), ("up", 1, 1), ("up", 2, 1), ("up", 3, 1), ("t", 5, 1), ("cw", 4), ("dn", 0, 0), ("dn", 1, 0),
    ("dn", 2, 0), ("dn", 3, 0), ("cw", 5), ("dn", 0, 1), ("dn", 1, 1), ("dn", 2, 1), ("dn", 3, 1), ("n2",),
    ("sent",), ("hb", 0, 0), ("hb", 1, 0), ("hb", 2, 0), ("hb", 3, 0), ("cs", 0), ("hb", 0, 1), ("hb", 1, 1),
    ("hb", 2, 1), ("hb", 3, 1), ("ce", 0, 1), ("cs", 1), ("ub", 0), ("ub", 1), ("ub", 2), ("ub", 3), ("n1b",),
    ("gu", 0, 0), ("gu", 1, 0), ("ce", 1, 1), ("ce", 1, 0), ("gu", 2, 0), ("gu", 3, 0), ("cs", 2), ("gu", 0, 1),
    ("gu", 1, 1), ("gu", 2, 1), ("gu", 3, 1), ("ce", 0, 0), ("te", 0, 1), ("cs", 3), ("mb", 0), ("ab", 0, 0),
    ("ab", 0, 1), ("te", 1, 1), ("ce", 2, 1), ("ab", 0, 2), ("kb", 0), ("mb", 1), ("ab", 1, 0), ("ab", 1, 1),
    ("te", 0, 0), ("ab", 1, 2), ("kb", 1), ("mb", 2), ("ab", 2, 0), ("te", 1, 0), ("ab", 2, 1), ("ab", 2, 2),
    ("kb", 2), ("mb", 3), ("se", 0), ("zs", 1, 1, 0), ("ce", 2, 0), ("zs", 1, 1, 1), ("ce", 3, 1), ("ab", 3, 0),
    ("ab", 3, 1), ("ab", 3, 2), ("kb", 3), ("sm0",), ("turn",), ("aq", 0), ("ak", 0), ("te", 2, 1), ("aq", 1),
    ("ak", 1), ("aq", 2), ("ak", 2), ("zs", 1, 0, 0), ("zs", 1, 0, 1), ("aq", 3), ("ak", 3), ("cs", 4),
    ("ce", 3, 0), ("te", 3, 1), ("ce", 4, 1), ("cs", 5), ("zs", 3, 1, 0), ("zs", 3, 1, 1), ("ce", 4, 0),
    ("te", 2, 0), ("se", 2), ("te", 4, 1), ("te", 3, 0), ("te", 4, 0), ("ce", 5, 1), ("zs", 1, 0, 2),
    ("zs", 1, 1, 2), ("zl", 1, 1), ("sm", 0), ("zs", 3, 0, 0), ("se", 4), ("ce", 5, 0), ("te", 5, 1),
    ("zs", 3, 1, 2), ("wi", 0), ("wi", 1), ("home",), ("zs", 3, 0, 1), ("zs", 3, 0, 2), ("sm", 1), ("qi", 0),
    ("qi", 1), ("zl", 1, 0), ("te", 5, 0), ("se", 5), ("sm", 2), ("la", 0), ("la", 2), ("qi", 2), ("qi", 3),
    ("own_in",), ("zl", 3, 1), ("la", 4), ("la", 1), ("zl", 3, 0), ("sm", 3), ("take",), ("la", 3), ("la", 5),
    ("sm", 4),
)

INPUTS = ("m_qkv", "m_out", "m_up", "m_down", "m_norm", "m_bias", "tok", "out_grad", "seg", "grp", "ans")
OUTPUTS = ("block_out", "input_grad", "owned", "sums", "squares")


def kernel(names, chunks, back_chunks, pairs, *refs):
    r = dict(zip(names, refs))
    pc = Place()
    loads = {n: pltpu.make_async_copy(r["hbm_" + n], r[n], r["load_sems"].at[k]) for k, n in enumerate(INPUTS)}
    stores = {n: pltpu.make_async_copy(r[n], r["hbm_" + n], r["store_sems"].at[k]) for k, n in enumerate(OUTPUTS)}
    for copy in loads.values():
        copy.start()
    all_here = greet(pc)
    r["squares"][...] = jnp.zeros_like(r["squares"])
    for n in INPUTS[:6]:
        loads[n].wait()
    gather = Gather(pc, r["g"], chunks, [r["gs%d" % k] for k in range(8)])
    lower_masters(r, pc, chunks, gather)
    layer = Layer(r, pc)
    rows, length = layer.rows, layer.length
    tok, tokw, window, xr, owned = r["tok"], r["tokw"], r["xw"], r["xrecv"], r["owned"]
    share = Share(
        pc,
        pairs,
        lambda low, high, target: tok.at[pl.ds(low % rows, high - low)],
        lambda low, high, target: tokw.at[in_window(low, high, target, rows, length)],
        r["share_sems"],
    )
    home = Share(
        pc,
        [(t, s, low, high) for s, t, low, high in pairs],
        lambda low, high, target: window.at[in_window(low, high, other_end(pairs, target, low), rows, length)],
        lambda low, high, target: xr.at[1 if low % rows == 0 else 0, pl.ds(0, high - low)],
        r["home_sems"],
    )
    spread = Sum5(pc, r["table"], r["table_slots"], r["table_sems"])
    total = Sum5(pc, r["sums"], r["sum_slots"], r["sum_sems"])

    def emit(j, value):
        a, low, w, _ = back_chunks[j]
        owned[a, :, low : low + w] = value
        line = col_sum(value * value)
        r["squares"][...] += sum(line[:, k : k + 128] for k in range(0, w, 128))

    grads = (r["hid"], r["g"].at[UP], r["g"].at[DOWN])
    back = Scatter(
        pc, grads, back_chunks, r["rc"], r["r3"], r["r2"], r["rz"], [r["ss%d" % k] for k in range(9)], emit
    )

    def start():
        for m in range(4):

            def own_tokens(m=m):
                for at, where in own_parts(m, rows, length):
                    tokw[where[0], where[1], :] = tok[at, :]

            pl.when(pc.m == m)(own_tokens)

    def share_start():
        loads["tok"].wait()
        share.start()

    def masks():
        for n in ("seg", "grp", "ans"):
            loads[n].wait()
        layer.masks()

    def second_norm():
        loads["out_grad"].wait()
        layer.second_norm()
        stores["block_out"].start()

    def table_step(k):
        spread.end(k)
        if k < 4:
            spread.start(k + 1)
        else:
            r["tab"][...] = r["table"][...].astype(F32)

    def sums_start():
        r["sums"][14:16, :] = jnp.zeros_like(r["sums"][14:16, :])
        total.start(0)

    def sums_step(k):
        total.end(k)
        if k < 4:
            total.start(k + 1)
        else:
            stores["sums"].start()

    def sent():
        gather.finish()
        share.wait_send()
        spread.finish()

    def homeward():
        for m in range(4):

            def own_rows(m=m):
                for at, where in own_parts(m, rows, length):
                    r["acc"][at, :] += window[where[0], where[1], :].astype(F32)

            pl.when(pc.m == m)(own_rows)

    def take():
        home.wait_recv()
        for source, target, low, high in home.pairs:

            def add(source=source, target=target, low=low, high=high):
                at = slice(low - target * rows, high - target * rows)
                k = 1 if low % rows == 0 else 0
                r["acc"][at, :] += xr[k, : high - low, :].astype(F32)

            pl.when(pc.m == target)(add)
        r["input_grad"][...] = r["acc"][...].astype(BF16)
        stores["input_grad"].start()

    steps = {
        "own": gather.own,
        "z": gather.z_step,
        "p": gather.p_step,
        "t": gather.t_step,
        "cw": gather.core_wait,
        "share": share_start,
        "shared": share.wait_recv,
        "sp": table_step,
        "sent": sent,
        "start": start,
        "masks": masks,
        "q": layer.queries,
        "kv": layer.keys_values,
        "att": layer.attend,
        "br": layer.branch,
        "n1": layer.first_norm,
        "up": layer.up,
        "dn": layer.down,
        "n2": second_norm,
        "hb": layer.hidden_back,
        "ub": layer.up_back,
        "n1b": layer.first_back,
        "gu": layer.up_grad,
        "mb": layer.mixed_back,
        "ab": layer.attend_back,
        "kb": layer.keys_back,
        "sm0": sums_start,
        "sm": sums_step,
        "turn": layer.turn,
        "aq": layer.query_grad,
        "ak": layer.keys_grad,
        "qi": layer.query_input,
        "wi": layer.window_input,
        "home": home.start,
        "own_in": homeward,
        "take": take,
        "cs": back.core_start,
        "ce": back.core_end,
        "te": back.third_end,
        "se": back.second_end,
        "zs": back.z_step,
        "zl": back.z_last,
        "la": back.last,
    }
    all_here()
    spread.start(0)
    for name, *at in ORDER:
        steps[name](*at)

    stores["owned"].start()
    norm = Total(pc, r["squares"], r["norm_slots"], r["norm_sems"])
    norm.run()
    stores["squares"].start()
    home.wait_send()
    back.finish()
    total.finish()
    norm.finish()
    for copy in stores.values():
        copy.wait()


def lower_masters(r, pc, chunks, gather):
    qkv, table = r["m_qkv"], r["table"]
    local = qkv.shape[2]
    heads = jnp.concatenate([qkv[0], r["m_out"][...].T, qkv[1], qkv[2]], 1)
    for j, (a, low, w, _) in enumerate(chunks):
        ref = gather.piece(j, pc.z, 0, 0)
        if a == ATT:
            ref[...] = heads[:, low : low + w].astype(BF16)
        else:
            ref[...] = r["m_up" if a == UP else "m_down"][:, low : low + w].astype(BF16)
    outer = pc.z * 2 + pc.x
    norm, bias = r["m_norm"], r["m_bias"]
    part, piece = norm.shape[2], bias.shape[1]
    width, columns = table.shape[1], 8 * piece
    wide = r["norm_wide"]
    wide[...] = jnp.zeros_like(wide)
    for k in range(6):
        wide[k : k + 1, :part] = norm[k]
    rows = pltpu.roll(wide[...], pc.m * local + outer * part, 1)
    line = r["bias_wide"]
    line[...] = jnp.zeros_like(line)
    line[0:1, :piece] = bias[...]
    line = pltpu.roll(line[...], outer * piece, 1)[0:1]
    head = line[:, : 2 * local]
    early = lax.broadcasted_iota(jnp.int32, head.shape, 1) < local
    attention = jnp.concatenate([jnp.where(early, head, 0.0), jnp.where(early, 0.0, head)], 1)
    hidden = line[:, 2 * local :]
    row = lax.broadcasted_iota(jnp.int32, (8, width), 0)
    top = jnp.where(row < 6, rows, 0.0)
    top = jnp.where(row == 6 + pc.m, attention, top)
    top = jnp.where(row == 10 + pc.m, hidden, top)
    low = jnp.where(row + 8 == 6 + pc.m, attention, 0.0)
    low = jnp.where(row + 8 == 10 + pc.m, hidden, low)
    table[...] = jnp.concatenate([top, low], 0).astype(BF16)


def other_end(pairs, owner, low):
    return [t for s, t, first, _ in pairs if s == owner and first == low][0]


def in_window(low, high, m, rows, length):
    return low // length - m * rows // length, pl.ds(low % length, high - low)


def own_parts(m, rows, length):
    parts, low = [], m * rows
    while low < (m + 1) * rows:
        high = min((m + 1) * rows, (low // length + 1) * length)
        parts.append((slice(low - m * rows, high - m * rows), in_window(low, high, m, rows, length)))
        low = high
    return parts


def run_layer(masters, tok, out_grad, seg, grp, ans, pad):
    per, cols = masters[2].shape
    rows, width = tok.shape
    length = seg.shape[1]
    hidden = 4 * cols
    window = max((m * rows + rows - 1) // length - m * rows // length + 1 for m in range(4))
    blocks = rows // 128
    pairs = overlaps(rows, length)
    chunks = chunks_of((ATT, UP, DOWN), cols, WAYS)
    back_chunks = chunks_of((DOWN, UP, ATT), cols, BACK_WAYS)
    most = max(high - low for _, _, low, high in pairs)
    bufs, sems = scatter_scratch(back_chunks, per)
    scratch = {
        "g": pltpu.VMEM((3, 4, 2, per, hidden), BF16),
        "table": pltpu.VMEM((16, width), BF16),
        "norm_wide": pltpu.VMEM((8, width), F32),
        "bias_wide": pltpu.VMEM((8, 8 * masters[5].shape[1]), F32),
        "tab": pltpu.VMEM((16, width), F32),
        "table_slots": pltpu.VMEM((10, 16, width), BF16),
        "tokw": pltpu.VMEM((window, length, width), BF16),
        "bias": pltpu.VMEM((blocks, 128, length), F32),
        "q": pltpu.VMEM((4, rows, 256), BF16),
        "kv": pltpu.VMEM((4, window, length, cols // 2), BF16),
        "shares": pltpu.VMEM((4, blocks, 3, 128, length), BF16),
        "o": pltpu.VMEM((4, rows, 256), BF16),
        "do": pltpu.VMEM((rows, 256), BF16),
        "dkv_acc": pltpu.VMEM((window, length, cols // 2), F32),
        "acc": pltpu.VMEM((rows, width), F32),
        "xh": pltpu.VMEM((rows, width), F32),
        "rs": pltpu.VMEM((rows, 1), F32),
        "hb": pltpu.VMEM((rows, width), BF16),
        "dz": pltpu.VMEM((rows, width), BF16),
        "hid": pltpu.VMEM((4, 2, per, hidden), BF16),
        "turned": pltpu.VMEM((width, rows), BF16),
        "turned2": pltpu.VMEM((width, rows), BF16),
        "turnedw": pltpu.VMEM((window, width, length), BF16),
        "xw": pltpu.VMEM((window, length, width), BF16),
        "xrecv": pltpu.VMEM((2, most, width), BF16),
        "sum_slots": pltpu.VMEM((10, 16, width), F32),
        "share_sems": pltpu.SemaphoreType.DMA((4,)),
        "home_sems": pltpu.SemaphoreType.DMA((4,)),
        "table_sems": pltpu.SemaphoreType.DMA((10,)),
        "norm_slots": pltpu.VMEM((12, 8, 128), F32),
        "norm_sems": pltpu.SemaphoreType.DMA((20,)),
        "sum_sems": pltpu.SemaphoreType.DMA((10,)),
    }
    scratch.update(zip(("rc", "r3", "r2", "rz"), bufs))
    scratch.update(("gs%d" % k, s) for k, s in enumerate(gather_sems(len(chunks))))
    scratch.update(("ss%d" % k, s) for k, s in enumerate(sems))
    given = dict(zip(INPUTS, list(masters) + [tok, out_grad, seg, grp, ans]))
    scratch.update((n, pltpu.VMEM(v.shape, v.dtype)) for n, v in given.items())
    made = dict(
        block_out=jax.ShapeDtypeStruct((rows, width), BF16),
        input_grad=jax.ShapeDtypeStruct((rows, width), BF16),
        owned=jax.ShapeDtypeStruct((3, per, cols), F32),
        sums=jax.ShapeDtypeStruct((16, width), F32),
        squares=jax.ShapeDtypeStruct((8, 128), F32),
    )
    scratch.update((n, pltpu.VMEM(v.shape, v.dtype)) for n, v in made.items())
    scratch["load_sems"] = pltpu.SemaphoreType.DMA((len(INPUTS),))
    scratch["store_sems"] = pltpu.SemaphoreType.DMA((len(OUTPUTS),))
    names = tuple("hbm_" + n for n in INPUTS) + ("pad",) + tuple("hbm_" + n for n in OUTPUTS) + tuple(scratch)
    anywhere = pl.BlockSpec(memory_space=pl.ANY)
    return pl.pallas_call(
        functools.partial(kernel, names, chunks, back_chunks, pairs),
        out_shape=list(made.values()),
        in_specs=[anywhere] * len(INPUTS) + [pl.BlockSpec(memory_space=pltpu.SMEM)],
        out_specs=[anywhere] * len(OUTPUTS),
        scratch_shapes=list(scratch.values()),
        compiler_params=pltpu.CompilerParams(collective_id=0, has_side_effects=True, vmem_limit_bytes=62 * 2**20),
        name="layer",
    )(*masters, tok, out_grad, seg, grp, ans, pad)


def adam_update(weight, grad, first, second, factor, decayed, rate):
    clipped = grad * factor
    first_new = beta_first * first + (1.0 - beta_first) * clipped
    second_new = beta_second * second + (1.0 - beta_second) * clipped * clipped
    ratio = (
        first_new
        / (1.0 - beta_first**STEP)
        / (jnp.sqrt(second_new / (1.0 - beta_second**STEP)) + adam_epsilon)
    )
    if decayed:
        ratio = ratio + decay_rate * weight
    return (weight - rate * ratio, first_new, second_new)


def update_kernel(*refs):
    given, (block_out, input_grad, norm_out), made = refs[:23], refs[23:26], refs[26:44]
    held, (grad_norm, load_sems, store_sems) = refs[44:67], refs[67:]
    loads = [pltpu.make_async_copy(a, b, load_sems.at[k]) for k, (a, b) in enumerate(zip(given, held))]
    outs = [held[2 + n * 6 + k] for n in range(3) for k in range(6)]
    stores = [pltpu.make_async_copy(a, b, store_sems.at[k]) for k, (a, b) in enumerate(zip(outs, made))]
    order = [1, 22, 0] + [2 + n * 6 + k for k in (2, 3, 0, 1, 4, 5) for n in range(3)] + [20, 21]
    for k in order:
        loads[k].start()
    passed = [
        pltpu.make_async_copy(held[20], block_out, store_sems.at[18]),
        pltpu.make_async_copy(held[21], input_grad, store_sems.at[19]),
        pltpu.make_async_copy(grad_norm, norm_out, store_sems.at[20]),
    ]
    owned, total = held[:2]
    masters, firsts, seconds = held[2:8], held[8:14], held[14:20]
    loads[1].wait()
    loads[22].wait()
    place = lax.axis_index("outer") * lax.axis_size("inner") + lax.axis_index("inner")
    mp = lax.axis_index("mp")
    local = masters[0].shape[2]
    width = total.shape[1]
    lane = lax.broadcasted_iota(jnp.int32, (4, width), 1)
    head, hidden = total[6:10, :], total[10:14, :]
    head = jnp.where((lane < local) | (lane >= 3 * local), head, 0.0)

    def square(v):
        return jnp.sum(jnp.sum(v * v, 0, keepdims=True), 1, keepdims=True)

    squares = jnp.sum(held[22][0:1, :], 1, keepdims=True) + square(total[0:6, :]) + square(head) + square(hidden)
    norm = jnp.sqrt(squares)
    grad_norm[...] = norm
    passed[2].start()
    factor = jnp.minimum(1.0, clip_limit / norm)
    mine = lax.broadcasted_iota(jnp.int32, (4, width), 0) == mp
    head = jnp.sum(jnp.where(mine, head, 0.0), 0, keepdims=True)
    hidden = jnp.sum(jnp.where(mine, hidden, 0.0), 0, keepdims=True)
    line = jnp.concatenate([head[:, : 2 * local] + head[:, 2 * local :], hidden], 1)
    part, piece = masters[4].shape[2], masters[5].shape[1]
    line = jnp.broadcast_to(line, (8, line.shape[1]))
    line = pltpu.roll(line, lax.rem(line.shape[1] - place * piece, line.shape[1]), 1)[0:1, :piece]
    norms = pltpu.roll(total[0:8, :], lax.rem(width - (mp * local + place * part), width), 1)

    def update(k, at, grad):
        values = adam_update(masters[k][at], grad, firsts[k][at], seconds[k][at], factor, k < 4, learn_rates[k])
        for n, value in enumerate(values):
            outs[n * 6 + k][at] = value

    def ready(k):
        for n in range(3):
            loads[2 + n * 6 + k].wait()

    def done(k):
        for n in range(3):
            stores[n * 6 + k].start()

    loads[0].wait()
    everything = (slice(None), slice(None))
    for k, grad in ((2, owned[1]), (3, owned[2])):
        ready(k)
        update(k, everything, grad)
        done(k)
    attention = owned[0]
    ready(0)
    update(0, 0, attention[:, :local])
    update(0, 1, attention[:, 2 * local : 3 * local])
    update(0, 2, attention[:, 3 * local :])
    done(0)
    ready(1)
    update(1, everything, attention[:, local : 2 * local].T)
    done(1)
    ready(4)
    for k in range(6):
        update(4, k, norms[k : k + 1, :part])
    done(4)
    ready(5)
    update(5, everything, line)
    done(5)
    for k in range(2):
        loads[20 + k].wait()
        passed[k].start()
    for copy in stores + passed:
        copy.wait()


def update(owned, total, squares, block_out, input_grad, masters, firsts, seconds):
    anywhere = pl.BlockSpec(memory_space=pl.ANY)
    given = [owned, total, *masters, *firsts, *seconds, block_out, input_grad, squares]

    def like(v):
        return jax.ShapeDtypeStruct(v.shape, v.dtype)

    return pl.pallas_call(
        update_kernel,
        out_shape=[like(block_out), like(input_grad), jax.ShapeDtypeStruct((1, 1), F32)] + [like(m) for m in masters] * 3,
        in_specs=[anywhere] * len(given),
        out_specs=[anywhere] * 21,
        scratch_shapes=[pltpu.VMEM(v.shape, v.dtype) for v in given]
        + [pltpu.VMEM((1, 1), F32), pltpu.SemaphoreType.DMA((len(given),)), pltpu.SemaphoreType.DMA((21,))],
        compiler_params=pltpu.CompilerParams(vmem_limit_bytes=62 * 2**20),
        name="update",
    )(*given)


def body(tokens, out_grad, segment_ids, group_ids, answer_ids, pad_lengths, *states):
    def turned(values):
        return [v.T if k == 3 else v for k, v in enumerate(values)]

    masters, firsts, seconds = turned(states[:6]), turned(states[6:12]), turned(states[12:])
    inner = lax.axis_size("inner")
    shared = masters
    if inner > 1:
        shared = [lax.all_gather(v, "inner", axis=d, tiled=True) for v, d in zip(masters, (1, 1, 0, 0, 2, 1))]
    block_out, input_grad, owned, total, squares = run_layer(
        shared, tokens, out_grad, segment_ids, group_ids, answer_ids, pad_lengths
    )
    if inner > 1:
        owned = lax.psum_scatter(owned, "inner", scatter_dimension=1, tiled=True)
        total = lax.psum(total, "inner")
        squares = lax.psum(jnp.sum(owned * owned), ("outer", "inner", "mp"))
        squares = jnp.full((8, 128), squares / 128)
    results = update(owned, total, squares, block_out, input_grad, masters, firsts, seconds)
    updated = [v for n in range(3) for v in turned(results[3 + 6 * n : 9 + 6 * n])]
    return (results[0], results[1], results[2][0, 0]) + tuple(updated)


def solution(mesh):
    dp = mesh.shape["dp"]
    outer = 8
    grid = Mesh(mesh.devices.reshape(outer, dp // outer, mesh.shape["mp"]), ("outer", "inner", "mp"))
    d = ("outer", "inner")
    both = P(d + ("mp",), None)
    states = (P(None, d, "mp"), P("mp", d), P(d, "mp"), P("mp", d), P(None, "mp", d), P("mp", d))
    in_specs = (both, both, P(d, None), P(d, None), P(d, None), P(d)) + states * 3
    out_specs = (both, both, P()) + states * 3
    return jax.shard_map(body, mesh=grid, in_specs=in_specs, out_specs=out_specs, check_vma=False)
```

```python
import functools
import jax
import jax.numpy as jnp
import numpy as np
from jax import lax
from jax.sharding import Mesh, PartitionSpec as P
from jax.experimental import pallas as pl
from jax.experimental.pallas import tpu as pltpu

MESH = pl.DeviceIdType.MESH
F32 = jnp.float32
BF16 = jnp.bfloat16
HD = 64
STEP = 5

norm_epsilon = 1e-06
adam_epsilon = 1e-08
learn_rates = (0.02, 0.1, 0.02, 0.02, 0.5, 0.5)
beta_first = 0.5
beta_second = 0.5
decay_rate = 0.01
clip_limit = 0.05
mask_fill = -1000000000.0
score_scale = 0.125

ATT, UP, DOWN = 0, 1, 2
NEAR, LONG, DIRECT = 0, 1, 2


def pick(index, values):
    out = values[-1]
    for k in range(len(values) - 1):
        out = jnp.where(index == k, values[k], out)
    return out


class Place:
    def __init__(self):
        outer = lax.axis_index("outer")
        self.sub = lax.axis_index("inner")
        self.m = lax.axis_index("mp")
        self.z = outer // 2
        self.x = lax.rem(outer, 2)
        self.y = self.m // 2
        self.c = lax.rem(self.m, 2)
        self.first = self.c == 0
        self.sib = self.at(c=1 - self.c)
        x, y = self.line(1, 0)
        self.second = self.at(x=x, y=y)
        x, y = self.line(0, 1)
        self.third = self.at(x=x, y=y)

    def at(self, z=None, x=None, y=None, c=None):
        z = self.z if z is None else z
        x = self.x if x is None else x
        y = self.y if y is None else y
        c = self.c if c is None else c
        return (z * 2 + x, self.sub, y * 2 + c)

    def mate(self, m):
        return (self.z * 2 + self.x, self.sub, m)

    def line(self, side, far, other_core=False):
        first = (1 - self.c if other_core else self.c) == 0
        x = jnp.where(first, side, far)
        y = jnp.where(first, far, side)
        return self.x + x - 2 * self.x * x, self.y + y - 2 * self.y * y

    def order(self, t):
        return pick(self.z, [(0, 1, 2, 3), (1, 0, 3, 2), (2, 2, 1, 1), (3, 3, 0, 0)][t])


def remote(src, dst, send, recv, device):
    return pltpu.make_async_remote_copy(
        src_ref=src, dst_ref=dst, send_sem=send, recv_sem=recv, device_id=device, device_id_type=MESH
    )


def peers(place):
    z, x, y, c = place.z, place.x, place.y, place.c

    def other(v, bit):
        return 1 - v if bit else v

    plane = [place.at(x=other(x, k & 4), y=other(y, k & 2), c=other(c, k & 1)) for k in range(1, 8)]
    return plane + [place.at(z=across(z, k)) for k in range(1, 4)]


def across(z, k):
    low, high = lax.rem(z, 2), z // 2
    return (1 - high if k & 2 else high) * 2 + (1 - low if k & 1 else low)


def greet(place):
    barrier = pltpu.get_barrier_semaphore()
    for device in peers(place):
        pl.semaphore_signal(barrier, inc=1, device_id=device, device_id_type=MESH)
    return lambda: pl.semaphore_wait(barrier, 10)


class Gather:
    def __init__(self, place, g, chunks, sems):
        self.p, self.g, self.chunks = place, g, chunks
        self.zs, self.zr, self.ps, self.pr, self.ts, self.tr, self.cs, self.cr = sems
        self.width = g.shape[4] // 4
        self.sent = []

    def piece(self, j, z, side, far, core=False):
        x, y = self.p.line(side, far, core)
        c = 1 - self.p.c if core else self.p.c
        a, low, w, _ = self.chunks[j]
        cols = pl.ds(pl.multiple_of((y * 2 + c) * self.width + low, 128), w)
        if z is None:
            return self.g.at[a, :, x, :, cols]
        return self.g.at[a, z, x, :, cols]

    def go(self, ref, send, recv, device, when=None):
        copy = remote(ref, ref, send, recv, device)
        if when is None:
            copy.start()
        else:
            pl.when(when)(copy.start)
        self.sent.append((copy, when))

    def arrived(self, ref, recv):
        remote(ref, ref, recv, recv, self.p.sib).wait_recv()

    def z_send(self, j, side, src, index, to, when):
        self.go(self.piece(j, src, side, 0), self.zs.at[j, side, index], self.zr.at[j, side, src], self.p.at(z=to), when)

    def z_both(self, j, side):
        z = self.p.z
        self.z_send(j, side, z, z, z + 1, z < 3)
        self.z_send(j, side, z, 4, z - 1, z > 0)

    def third(self, j, side, src):
        k = side * 4 + src
        self.go(self.piece(j, src, side, 0), self.ts.at[j, k], self.tr.at[j, k], self.p.third)

    def second(self, j, src):
        self.go(self.piece(j, src, 0, 0), self.ps.at[j, src], self.pr.at[j, src], self.p.second)

    def to_sibling(self, j, side, far):
        k = side + 2 * far
        self.go(self.piece(j, None, side, far), self.cs.at[j, k], self.cr.at[j, k], self.p.sib)

    def own(self, j):
        self.second(j, self.p.z)
        self.z_both(j, 0)
        self.third(j, 0, self.p.z)

    def z_step(self, j, t, side=0):
        z = self.p.z
        src = self.p.order(t)
        self.arrived(self.piece(j, src, side, 0), self.zr.at[j, side, src])
        to = jnp.where(z > src, z + 1, z - 1)
        self.z_send(j, side, src, src, to, (to >= 0) & (to <= 3))
        if self.chunks[j][3] != LONG:
            self.second(j, src)
        self.third(j, side, src)
        if t == 3:
            self.to_sibling(j, side, 0)

    def p_step(self, j, t):
        src = self.p.order(t)
        self.arrived(self.piece(j, src, 1, 0), self.pr.at[j, src])
        if self.chunks[j][3] == LONG:
            self.z_both(j, 1)
        self.third(j, 1, src)
        if t == 3:
            self.to_sibling(j, 1, 0)

    def t_step(self, j, side):
        for t in range(4):
            src = self.p.order(t)
            self.arrived(self.piece(j, src, side, 1), self.tr.at[j, side * 4 + src])
        self.to_sibling(j, side, 1)

    def core_wait(self, j):
        for k, (side, far) in enumerate(((0, 0), (1, 0), (0, 1), (1, 1))):
            self.arrived(self.piece(j, None, side, far, True), self.cr.at[j, k])

    def finish(self):
        for copy, when in self.sent:
            if when is None:
                copy.wait_send()
            else:
                pl.when(when)(copy.wait_send)
        self.sent = []


def gather_sems(chunks):
    sizes = ((2, 5), (2, 4), (4,), (4,), (8,), (8,), (4,), (4,))
    return [pltpu.SemaphoreType.DMA((chunks,) + n) for n in sizes]


def overlaps(rows, length):
    pairs = []
    for m in range(3):
        edge = (m + 1) * rows
        low = edge // length * length
        if low == edge:
            continue
        pairs.append((m, m + 1, max(low, m * rows), edge))
        pairs.append((m + 1, m, edge, min(low + length, edge + rows)))
    return pairs


class Share:
    def __init__(self, place, pairs, src, dst, sems):
        self.p, self.pairs, self.src, self.dst, self.sems = place, pairs, src, dst, sems

    def copy(self, pair):
        source, target, low, high = pair
        k = 0 if source < target else 1
        return remote(self.src(low, high, target), self.dst(low, high, target), self.sems.at[k], self.sems.at[2 + k], self.p.mate(target))

    def start(self):
        for pair in self.pairs:
            pl.when(self.p.m == pair[0])(self.copy(pair).start)

    def wait_recv(self):
        for pair in self.pairs:
            pl.when(self.p.m == pair[1])(self.copy(pair).wait_recv)

    def wait_send(self):
        for pair in self.pairs:
            pl.when(self.p.m == pair[0])(self.copy(pair).wait_send)


class Sum5:
    def __init__(self, place, table, slots, sems):
        self.p, self.table, self.slots, self.sems = place, table, slots, sems
        z = place.z
        self.peers = [
            place.at(z=z + 1 - 2 * lax.rem(z, 2)),
            place.at(z=z + 2 - 4 * (z // 2)),
            place.at(x=1 - place.x),
            place.at(y=1 - place.y),
            place.sib,
        ]

    def copy(self, k):
        return remote(self.slots.at[5 + k], self.slots.at[k], self.sems.at[k], self.sems.at[5 + k], self.peers[k])

    def start(self, k):
        self.slots[5 + k] = self.table[...]
        self.copy(k).start()

    def end(self, k):
        self.copy(k).wait_recv()
        self.table[...] = self.table[...] + self.slots[k]

    def finish(self):
        for k in range(5):
            self.copy(k).wait_send()


class Total:
    def __init__(self, place, tile, slots, sems):
        self.p, self.tile, self.slots, self.sems = place, tile, slots, sems
        self.copies = [remote(slots.at[0 if k < 7 else 11], slots.at[1 + k], sems.at[k], sems.at[10 + k], d) for k, d in enumerate(peers(place))]

    def run(self):
        for first, ks in ((0, range(7)), (11, range(7, 10))):
            self.slots[first] = self.tile[...]
            for k in ks:
                self.copies[k].start()
            total = self.tile[...]
            for k in ks:
                self.copies[k].wait_recv()
                total = total + self.slots[1 + k]
            self.tile[...] = total

    def finish(self):
        for copy in self.copies:
            copy.wait_send()


class Scatter:
    def __init__(self, place, grads, chunks, rc, r3, r2, rz, sems, emit):
        self.p, self.grads, self.chunks = place, grads, chunks
        self.rc, self.r3, self.r2, self.rz = rc, r3, r2, rz
        self.cs, self.cr, self.ts, self.tr, self.ps, self.pr, self.us, self.ds, self.zr = sems
        self.emit = emit
        self.width = grads[0].shape[3] // 4
        self.sent = []
        self.seconds, self.lines, _, _ = scatter_slots(chunks)

    def region(self, j, side, far, core=False):
        x, y = self.p.line(side, far, core)
        c = 1 - self.p.c if core else self.p.c
        a, low, w, _ = self.chunks[j]
        return a, x, pl.ds(pl.multiple_of((y * 2 + c) * self.width + low, 128), w)

    def block(self, j, side, far, core=False):
        a, x, cols = self.region(j, side, far, core)
        return self.grads[a].at[:, x, :, cols]

    def shard(self, j, side, z):
        a, x, cols = self.region(j, side, 0)
        return self.grads[a].at[z, x, :, cols]

    def go(self, src, dst, send, recv, device, when=None):
        copy = remote(src, dst, send, recv, device)
        if when is None:
            copy.start()
        else:
            pl.when(when)(copy.start)
        self.sent.append((copy, when))

    def arrived(self, ref, recv):
        remote(ref, ref, recv, recv, self.p.sib).wait_recv()

    def core_start(self, j):
        for far in (1, 0):
            for side in (1, 0):
                k = far * 2 + side
                self.go(self.block(j, side, far, True), self.rc.at[j, k], self.cs.at[j, k], self.cr.at[j, k], self.p.sib)

    def add(self, j, side, far, other):
        a, x, cols = self.region(j, side, far)

        def step(k):
            here = self.grads[a].at[k, x, :, cols]
            here[...] = (here[...].astype(F32) + other[k].astype(F32)).astype(BF16)

        pl.loop(0, 4)(step)

    def core_end(self, j, far):
        for side in (1, 0):
            k = far * 2 + side
            self.arrived(self.rc.at[j, k], self.cr.at[j, k])
            self.add(j, side, far, self.rc.at[j, k])
            if far == 1:
                self.go(self.block(j, side, 1), self.r3.at[j, side], self.ts.at[j, side], self.tr.at[j, side], self.p.third)

    def third_end(self, j, side):
        self.arrived(self.r3.at[j, side], self.tr.at[j, side])
        self.add(j, side, 0, self.r3.at[j, side])
        if self.chunks[j][3] == LONG:
            self.line_start(j, side)
        elif side == 1:
            slot = self.r2.at[pl.ds(self.seconds[j], 4)]
            self.go(self.block(j, 1, 0), slot, self.ps.at[j], self.pr.at[j], self.p.second)

    def second_end(self, j):
        slot = self.r2.at[pl.ds(self.seconds[j], 4)]
        self.arrived(slot, self.pr.at[j])
        self.add(j, 0, 0, slot)
        if self.chunks[j][3] != DIRECT:
            self.line_start(j, 0)
            return
        n = self.lines[j]
        for k in (3, 2, 1):
            to = across(self.p.z, k)
            self.go(self.shard(j, 0, to), self.rz.at[n, k], self.us.at[n, k], self.zr.at[n, k], self.p.at(z=to))

    def up(self, j, side, d, when):
        n = self.lines[j] + side
        self.go(self.shard(j, side, d), self.rz.at[n, d], self.us.at[n, d], self.zr.at[n, d], self.p.at(z=self.p.z + 1), when)

    def down(self, j, side, d, when):
        n = self.lines[j] + side
        slot = jnp.where(d == self.p.z - 1, 4, d)
        self.go(self.shard(j, side, d), self.rz.at[n, slot], self.ds.at[n, d], self.zr.at[n, slot], self.p.at(z=self.p.z - 1), when)

    def line_start(self, j, side):
        z = self.p.z
        for d in range(3):
            self.up(j, side, 3 - d, z == 0)
            self.down(j, side, d, z == 3)

    def fold(self, j, side, d, slot):
        n = self.lines[j] + side
        self.arrived(self.rz.at[n, slot], self.zr.at[n, slot])
        ref = self.shard(j, side, d)
        ref[...] = (ref[...].astype(F32) + self.rz[n, slot].astype(F32)).astype(BF16)

    def relay(self, j, side, d, send, when):
        pl.when(when)(lambda: self.fold(j, side, d, d))
        send(j, side, d, when)

    def z_step(self, j, side, t):
        z = self.p.z
        if t < 2:
            self.relay(j, side, 3 - t, self.up, z == 1)
            self.relay(j, side, t, self.down, z == 2)
        else:
            self.relay(j, side, 3, self.up, z == 2)
            self.relay(j, side, 0, self.down, z == 1)

    def z_last(self, j, side):
        z = self.p.z
        pl.when(z > 0)(lambda: self.fold(j, side, z, z))
        pl.when(z < 3)(lambda: self.fold(j, side, z, 4))
        if side == 1:
            slot = self.r2.at[self.seconds[j]]
            self.go(self.shard(j, 1, z), slot, self.ps.at[j], self.pr.at[j], self.p.second)

    def last(self, j):
        z = self.p.z
        if self.chunks[j][3] == DIRECT:
            n = self.lines[j]
            total = self.shard(j, 0, z)[...].astype(F32)
            for k in (1, 2, 3):
                self.arrived(self.rz.at[n, k], self.zr.at[n, k])
                total = total + self.rz[n, k].astype(F32)
            self.emit(j, total)
        elif self.chunks[j][3] == LONG:
            slot = self.r2.at[self.seconds[j]]
            self.arrived(slot, self.pr.at[j])
            self.emit(j, self.shard(j, 0, z)[...].astype(F32) + slot[...].astype(F32))
        else:
            self.z_last(j, 0)
            self.emit(j, self.shard(j, 0, z)[...].astype(F32))

    def finish(self):
        for copy, when in self.sent:
            if when is None:
                copy.wait_send()
            else:
                pl.when(when)(copy.wait_send)
        self.sent = []


def scatter_slots(chunks):
    seconds, lines, n, m = [], [], 0, 0
    for chunk in chunks:
        seconds.append(n)
        lines.append(m)
        n += 1 if chunk[3] == LONG else 4
        m += 2 if chunk[3] == LONG else 1
    return seconds, lines, n, m


def scatter_scratch(chunks, rows):
    n, w = len(chunks), chunks[0][2]
    _, _, seconds, lines = scatter_slots(chunks)
    shapes = ((n, 4, 4), (n, 2, 4), (seconds,), (lines, 5))
    sems = ((n, 4), (n, 4), (n, 2), (n, 2), (n,), (n,), (lines, 4), (lines, 4), (lines, 5))
    return [pltpu.VMEM(s + (rows, w), BF16) for s in shapes], [pltpu.SemaphoreType.DMA(s) for s in sems]


def nt(a, b):
    return lax.dot_general(a, b, (((1,), (1,)), ((), ())), preferred_element_type=F32)


def tn(a, b):
    return lax.dot_general(a, b, (((0,), (0,)), ((), ())), preferred_element_type=F32)


def nn(a, b):
    return jnp.dot(a, b, preferred_element_type=F32)


def even_lanes(shape):
    return lax.broadcasted_iota(jnp.int32, shape, 1) < HD


def keep(values, even):
    mask = even_lanes(values.shape)
    zero = jnp.zeros_like(values)
    return jnp.where(mask, values, zero) if even else jnp.where(mask, zero, values)


def col_sum(values):
    return jnp.sum(values, 0, keepdims=True)


class Layer:
    def __init__(self, refs, place):
        self.__dict__.update(refs)
        self.p = place
        self.rows, self.width = self.tok.shape
        self.length = self.seg.shape[1]
        self.blocks = self.rows // 128
        self.cols = self.g.shape[4] // 4
        self.hidden = self.g.shape[4]
        self.s0 = self.rows * place.m // self.length
        self.s1 = (self.rows * place.m + self.rows - 1) // self.length
        self.window = self.kv.shape[1]

    def w(self, a, low, size):
        return self.g[a, :, :, :, low : low + size].reshape(self.width, size)

    def put(self, ref, low, value):
        size = value.shape[1]
        ref[:, :, :, low : low + size] = value.astype(BF16).reshape(ref.shape[:3] + (size,))

    def gain(self, row):
        return self.tab[pl.ds(row, 1), :]

    def blk(self, i):
        return pl.ds(pl.multiple_of(i * 128, 128), 128)

    def seq_of(self, i):
        return (self.rows * self.p.m + 128 * i) // self.length

    def each_seq(self, run):
        for s in range(self.window):
            if s == 0:
                run(s)
            else:
                pl.when(self.s0 + s <= self.s1)(functools.partial(run, s))

    def masks(self):
        n = self.length
        for i in range(self.blocks):
            s = self.seq_of(i)
            at = lax.rem(self.rows * self.p.m + 128 * i, n)
            seg = self.seg[pl.ds(s, 1), :]
            grp = self.grp[pl.ds(s, 1), :]
            ans = self.ans[pl.ds(s, 1), :]
            seg_q = pick(at // 128, [seg[:, k : k + 128] for k in range(0, n, 128)])
            grp_q = pick(at // 128, [grp[:, k : k + 128] for k in range(0, n, 128)])
            code = jnp.where(seg_q == 0, -1, grp_q).astype(F32)
            code = jnp.transpose(jnp.broadcast_to(code, (8, 128)))[:, :1]
            open_key = (seg == 0) | (ans == 1)
            rule = (code == grp.astype(F32)) | (code < 0.0) | open_key
            position = lax.broadcasted_iota(jnp.int32, (1, n), 1)
            seen = rule & (position < self.pad[s])
            self.bias[i] = jnp.where(seen, 0.0, mask_fill)

    def queries(self, b):
        c = self.cols
        lanes = lax.broadcasted_iota(jnp.int32, (1, 256), 1) < c // 4
        q = nn(self.tok[...], self.w(ATT, b * c, 256)) + self.tab[6 + b : 7 + b, :256]
        self.q[b] = jnp.where(lanes, q * score_scale, 0.0).astype(BF16)

    def keys_values(self, b):
        c = self.cols
        wkv = self.w(ATT, b * c + c // 2, c // 2)

        def one(s):
            self.kv[b, s] = (nn(self.tokw[s], wkv) + self.tab[6 + b : 7 + b, c // 2 :]).astype(BF16)

        self.each_seq(one)

    def heads(self, b, i):
        s = self.seq_of(i) - self.s0
        q0 = self.q[b, self.blk(i), :128]
        q2 = self.q[b, self.blk(i), 128:]
        return s, keep(q0, True), keep(q0, False), q2

    def attend(self, b):
        @pl.loop(0, self.blocks)
        def _(i):
            s, q0, q1, q2 = self.heads(b, i)
            bias = self.bias[i]

            def softmax(scores):
                scores = scores + bias
                e = jnp.exp(scores - jnp.max(scores, -1, keepdims=True))
                return (e * (1.0 / jnp.sum(e, -1, keepdims=True))).astype(BF16)

            t0, t1, t2 = (self.kv[b, s, :, 128 * t : 128 * t + 128] for t in range(3))
            s01 = nt(jnp.concatenate([q0, q1], 0), t0)
            p0, p1, p2 = softmax(s01[:128]), softmax(s01[128:]), softmax(nt(q2, t1))
            self.shares[b, i, 0] = p0
            self.shares[b, i, 1] = p1
            self.shares[b, i, 2] = p2
            o12 = nn(jnp.concatenate([p1, p2], 0), t2)
            self.o[b, self.blk(i), :128] = keep(nn(p0, t1), False).astype(BF16)
            self.o[b, self.blk(i), 128:] = jnp.where(even_lanes((128, 128)), o12[:128], o12[128:]).astype(BF16)

    def row_loop(self, step, sums):
        n = 48

        def run(k, carry):
            at = pl.ds(pl.multiple_of(k * n, n), n)
            return step(at, carry)

        zero = tuple(jnp.zeros((1, self.width), F32) for _ in range(sums))
        return lax.fori_loop(0, self.rows // n, run, zero)

    def accumulate(self, value, first):
        self.acc[...] = value if first else self.acc[...] + value

    def branch(self, b):
        self.accumulate(nt(self.o[b], self.w(ATT, b * self.cols + 128, 256)), b == 0)

    def first_norm(self):
        g1, b1, co = self.gain(0), self.gain(1), self.gain(2)

        def step(at, carry):
            r = self.tok[at, :].astype(F32) + (self.acc[at, :] + co)
            r = r - jnp.mean(r, -1, keepdims=True)
            rs = lax.rsqrt(jnp.mean(r * r, -1, keepdims=True) + norm_epsilon)
            xh = r * rs
            self.xh[at, :] = xh
            self.rs[at, :] = rs
            self.hb[at, :] = (xh * g1 + b1).astype(BF16)
            return carry

        self.row_loop(step, 0)

    def part(self, b, k):
        n = self.cols // PARTS
        return b * self.cols + k * n, n

    def hidden_ref(self, which):
        return self.hid.at[2 * which : 2 * which + 2]

    def get_hidden(self, which, low, n):
        return self.hidden_ref(which)[:, :, :, low : low + n].reshape(self.rows, n)

    def set_hidden(self, which, low, value):
        ref = self.hidden_ref(which)
        ref[:, :, :, low : low + value.shape[1]] = value.astype(BF16).reshape(ref.shape[:3] + value.shape[1:])

    def up(self, b, k):
        low, n = self.part(b, k)
        u = nn(self.hb[...], self.w(UP, low, n)) + self.tab[10 + b : 11 + b, k * n : k * n + n]
        share = 0.5 + 0.5 * lax.erf(u * np.float32(np.sqrt(0.5)))
        self.set_hidden(0, low, u * share)
        self.set_hidden(1, low, share + u * (jnp.exp(-0.5 * (u * u)) * np.float32(1 / np.sqrt(2 * np.pi))))

    def down(self, b, k):
        low, n = self.part(b, k)
        self.accumulate(nt(self.get_hidden(0, low, n), self.w(DOWN, low, n)), b == 0 and k == 0)

    def second_norm(self):
        g1, b1, g2, b2, cd = self.gain(0), self.gain(1), self.gain(3), self.gain(4), self.gain(5)

        def step(at, carry):
            r = (self.xh[at, :] * g1 + b1) + (self.acc[at, :] + cd)
            r = r - jnp.mean(r, -1, keepdims=True)
            rs = lax.rsqrt(jnp.mean(r * r, -1, keepdims=True) + norm_epsilon)
            xh = r * rs
            self.block_out[at, :] = (xh * g2 + b2).astype(BF16)
            grad = self.out_grad[at, :].astype(F32)
            inner = grad * g2
            back = rs * (inner - jnp.mean(inner, -1, keepdims=True) - xh * jnp.mean(inner * xh, -1, keepdims=True))
            self.acc[at, :] = back
            low = back.astype(BF16)
            self.dz[at, :] = low
            return carry[0] + col_sum(grad * xh), carry[1] + col_sum(grad), carry[2] + col_sum(low.astype(F32))

        dg, db, dc = self.row_loop(step, 3)
        self.sums[3:4, :] = dg
        self.sums[4:5, :] = db
        self.sums[5:6, :] = dc

    def hidden_back(self, b, k):
        if b == 0 and k == 0:
            self.turned[...] = self.dz[...].T
        low, n = self.part(b, k)
        du = nn(self.dz[...], self.w(DOWN, low, n)) * self.get_hidden(1, low, n).astype(F32)
        du = du.astype(BF16)
        self.set_hidden(1, low, du)
        self.sums[10 + b : 11 + b, k * n : k * n + n] = col_sum(du.astype(F32))
        self.put(self.g.at[DOWN], low, nn(self.turned[...], self.get_hidden(0, low, n)))

    def up_back(self, b):
        low = b * self.cols
        self.acc[...] += nt(self.get_hidden(1, low, self.cols), self.w(UP, low, self.cols))

    def up_grad(self, b, k):
        if b == 0 and k == 0:
            self.turned[...] = self.hb[...].T
        low, n = self.part(b, k)
        self.put(self.g.at[UP], low, nn(self.turned[...], self.get_hidden(1, low, n)))

    def first_back(self):
        g1 = self.gain(0)

        def step(at, carry):
            grad = self.acc[at, :]
            xh = self.xh[at, :]
            inner = grad * g1
            back = self.rs[at, :] * (
                inner - jnp.mean(inner, -1, keepdims=True) - xh * jnp.mean(inner * xh, -1, keepdims=True)
            )
            self.acc[at, :] = back
            low = back.astype(BF16)
            self.dz[at, :] = low
            return carry[0] + col_sum(grad * xh), carry[1] + col_sum(grad), carry[2] + col_sum(low.astype(F32))

        dg, db, dc = self.row_loop(step, 3)
        self.sums[0:1, :] = dg
        self.sums[1:2, :] = db
        self.sums[2:3, :] = dc

    def mixed_back(self, b):
        do = nn(self.dz[...], self.w(ATT, b * self.cols + 128, 256))
        lanes = lax.broadcasted_iota(jnp.int32, (1, 256), 1) >= HD
        self.do[...] = jnp.where(lanes, do, 0.0).astype(BF16)
        self.dkv_acc[...] = jnp.zeros_like(self.dkv_acc)

    def attend_back(self, b, i):
        s, q0, q1, q2 = self.heads(b, i)
        t0, t1, t2 = (self.kv[b, s, :, 128 * t : 128 * t + 128] for t in range(3))
        do0 = self.do[self.blk(i), :128]
        do12 = self.do[self.blk(i), 128:]
        do1, do2 = keep(do12, True), keep(do12, False)
        dp12 = nt(jnp.concatenate([do1, do2], 0), t2)

        def back(h, dp):
            low = self.shares[b, i, h]
            p = low.astype(F32)
            scaled = p * dp
            return low, (scaled - p * jnp.sum(scaled, -1, keepdims=True)).astype(BF16)

        p0, ds0 = back(0, nt(do0, t1))
        p1, ds1 = back(1, dp12[:128])
        p2, ds2 = back(2, dp12[128:])
        dq01 = nn(jnp.concatenate([ds0, ds1], 0), t0)
        dq0 = jnp.where(even_lanes((128, 128)), dq01[:128], dq01[128:])
        dq2 = keep(nn(ds2, t1), True)
        self.q[b, self.blk(i), :128] = (dq0 * score_scale).astype(BF16)
        self.q[b, self.blk(i), 128:] = (dq2 * score_scale).astype(BF16)
        rows = jnp.concatenate
        self.dkv_acc[s, :, :128] += tn(rows([ds0, ds1], 0), rows([q0, q1], 0))
        self.dkv_acc[s, :, 128:256] += tn(rows([ds2, p0], 0), rows([q2, do0], 0))
        self.dkv_acc[s, :, 256:] += tn(rows([p1, p2], 0), rows([do1, do2], 0))

    def keys_back(self, b):
        c = self.cols
        total = jnp.zeros((1, c // 2), F32)
        for s in range(self.window):
            low = self.dkv_acc[s].astype(BF16)
            self.kv[b, s] = low
            total = total + col_sum(low.astype(F32))
        first = col_sum(self.q[b].astype(F32))
        gap = jnp.zeros((1, c // 2 - 256), F32)
        self.sums[6 + b : 7 + b, :] = jnp.concatenate([first, gap, total], 1)

    def turn(self):
        self.turned[...] = self.tok[...].T
        self.turned2[...] = self.dz[...].T

        def one(s):
            self.turnedw[s] = self.tokw[s].T

        self.each_seq(one)

    def query_grad(self, b):
        c = self.cols
        dq = nn(self.turned[...], self.q[b])
        do = nn(self.turned2[...], self.o[b])
        self.put(self.hid, b * c, dq[:, :128])
        self.put(self.hid, b * c + 128, dq[:, 128:] + do[:, :128])
        self.put(self.hid, b * c + 256, do[:, 128:])

    def keys_grad(self, b):
        c = self.cols

        def finish(count):
            total = nn(self.turnedw[0], self.kv[b, 0])
            for s in range(1, count):
                total = total + nn(self.turnedw[s], self.kv[b, s])
            self.put(self.hid, b * c + c // 2, total)

        for count in range(1, self.window + 1):
            pl.when(self.s1 - self.s0 + 1 == count)(functools.partial(finish, count))

    def query_input(self, b):
        self.acc[...] += nt(self.q[b], self.w(ATT, b * self.cols, 256))

    def window_input(self, s):
        c, half = self.cols, self.width // 2

        def run():
            for k in range(2):
                for b in range(4):
                    w = self.g[ATT, 2 * k : 2 * k + 2, :, :, b * c + c // 2 : b * c + c].reshape(half, c // 2)
                    part = nt(self.kv[b, s], w)
                    self.dkv_acc[k] = part if b == 0 else self.dkv_acc[k] + part
                self.xw[s, :, k * half : k * half + half] = self.dkv_acc[k].astype(BF16)

        if s == 0:
            run()
        else:
            pl.when(self.s0 + s <= self.s1)(run)


PARTS = 2
WAYS = (NEAR, LONG, LONG, NEAR, LONG, LONG)
BACK_WAYS = (DIRECT, LONG, DIRECT, LONG, DIRECT, DIRECT)


def chunks_of(order, cols, ways):
    w = cols // PARTS
    return [(order[k // PARTS], k % PARTS * w, w, ways[k]) for k in range(3 * PARTS)]


ORDER = (
    ("own", 0), ("own", 1), ("share",), ("rest",), ("sp", 0), ("z", 0, 1, 0), ("start",), ("p", 1, 0),
    ("sp", 1), ("z", 0, 2, 0), ("z", 0, 3, 0), ("sp", 2), ("own", 2), ("own", 3), ("own", 4), ("p", 0, 0),
    ("p", 0, 1), ("p", 0, 2), ("p", 0, 3), ("z", 1, 1, 0), ("z", 1, 1, 1), ("z", 1, 2, 0), ("z", 1, 2, 1),
    ("z", 1, 3, 0), ("z", 1, 3, 1), ("masks",), ("p", 4, 0), ("z", 3, 1, 0), ("p", 2, 0), ("t", 0, 0),
    ("sp", 3), ("own", 5), ("t", 0, 1), ("z", 3, 2, 0), ("z", 3, 3, 0), ("sp", 4), ("z", 4, 1, 0), ("t", 1, 0),
    ("t", 1, 1), ("z", 2, 1, 0), ("z", 4, 2, 0), ("cw", 0), ("q", 0), ("q", 1), ("q", 2), ("q", 3),
    ("z", 2, 2, 0), ("p", 3, 0), ("shared",), ("cw", 1), ("kv", 0), ("kv", 1), ("kv", 2), ("z", 2, 1, 1),
    ("z", 2, 2, 1), ("z", 2, 3, 0), ("kv", 3), ("att", 0), ("z", 2, 3, 1), ("p", 5, 0), ("att", 1), ("p", 3, 1),
    ("p", 3, 2), ("p", 3, 3), ("z", 5, 1, 0), ("z", 4, 3, 0), ("t", 3, 0), ("att", 2), ("z", 5, 2, 0),
    ("z", 4, 1, 1), ("z", 4, 2, 1), ("att", 3), ("br", 0), ("z", 5, 1, 1), ("t", 2, 0), ("t", 2, 1), ("br", 1),
    ("z", 4, 3, 1), ("z", 5, 3, 0), ("br", 2), ("br", 3), ("n1",), ("z", 5, 2, 1), ("t", 3, 1), ("cw", 2),
    ("up", 0, 0), ("up", 1, 0), ("t", 4, 0), ("z", 5, 3, 1), ("up", 2, 0), ("up", 3, 0), ("t", 4, 1), ("cw", 3),
    ("up", 0, 1), ("t", 5, 0), ("up", 1, 1), ("up", 2, 1), ("up", 3, 1), ("t", 5, 1), ("cw", 4), ("dn", 0, 0),
    ("dn", 1, 0), ("dn", 2, 0), ("dn", 3, 0), ("cw", 5), ("dn", 0, 1), ("dn", 1, 1), ("dn", 2, 1), ("dn", 3, 1),
    ("n2",), ("sent",), ("hb", 0, 0), ("hb", 1, 0), ("hb", 2, 0), ("hb", 3, 0), ("cs", 0), ("hb", 0, 1),
    ("hb", 1, 1), ("hb", 2, 1), ("hb", 3, 1), ("ce", 0, 1), ("cs", 1), ("ub", 0), ("ub", 1), ("ub", 2),
    ("ub", 3), ("n1b",), ("gu", 0, 0), ("gu", 1, 0), ("ce", 1, 1), ("ce", 1, 0), ("gu", 2, 0), ("gu", 3, 0),
    ("cs", 2), ("gu", 0, 1), ("gu", 1, 1), ("gu", 2, 1), ("gu", 3, 1), ("ce", 0, 0), ("te", 0, 1), ("te", 0, 0),
    ("cs", 3), ("mb", 0), ("ab", 0, 0), ("ab", 0, 1), ("ab", 0, 2), ("kb", 0), ("te", 1, 1), ("mb", 1),
    ("ab", 1, 0), ("ce", 2, 1), ("te", 1, 0), ("ab", 1, 1), ("ab", 1, 2), ("kb", 1), ("mb", 2), ("ab", 2, 0),
    ("ab", 2, 1), ("ab", 2, 2), ("kb", 2), ("se", 0), ("mb", 3), ("ab", 3, 0), ("ce", 3, 1), ("zs", 1, 1, 0),
    ("zs", 1, 1, 1), ("ce", 2, 0), ("ab", 3, 1), ("ab", 3, 2), ("kb", 3), ("te", 2, 1), ("sm0",), ("turn",),
    ("aq", 0), ("ak", 0), ("aq", 1), ("ak", 1), ("aq", 2), ("ak", 2), ("aq", 3), ("ak", 3), ("cs", 4),
    ("zs", 1, 0, 0), ("ce", 3, 0), ("zs", 1, 0, 1), ("te", 3, 1), ("zs", 1, 1, 2), ("te", 2, 0), ("zl", 1, 1),
    ("ce", 4, 1), ("sm", 0), ("se", 2), ("zs", 3, 1, 0), ("la", 0), ("te", 3, 0), ("ce", 4, 0), ("te", 4, 1),
    ("zs", 3, 1, 1), ("cs", 5), ("ce", 5, 1), ("zs", 1, 0, 2), ("sm", 1), ("ce", 5, 0), ("te", 4, 0), ("se", 4),
    ("la", 2), ("zs", 3, 0, 0), ("te", 5, 1), ("wi", 0), ("wi", 1), ("zl", 1, 0), ("sm", 2), ("home",),
    ("zs", 3, 1, 2), ("qi", 0), ("te", 5, 0), ("zs", 3, 0, 1), ("qi", 1), ("zs", 3, 0, 2), ("se", 5), ("sm", 3),
    ("la", 1), ("zl", 3, 1), ("zl", 3, 0), ("qi", 2), ("sm", 4), ("qi", 3), ("la", 4), ("own_in",), ("take",),
    ("la", 3), ("la", 5),
)

INPUTS = ("m_qkv", "m_out", "m_up", "m_down", "m_norm", "m_bias", "tok", "out_grad", "seg", "grp", "ans")
OUTPUTS = ("block_out", "input_grad", "owned", "sums", "squares")


def kernel(names, chunks, back_chunks, pairs, *refs):
    r = dict(zip(names, refs))
    pc = Place()
    loads = {n: pltpu.make_async_copy(r["hbm_" + n], r[n], r["load_sems"].at[k]) for k, n in enumerate(INPUTS)}
    stores = {n: pltpu.make_async_copy(r[n], r["hbm_" + n], r["store_sems"].at[k]) for k, n in enumerate(OUTPUTS)}
    for copy in loads.values():
        copy.start()
    all_here = greet(pc)
    r["squares"][...] = jnp.zeros_like(r["squares"])
    for n in INPUTS[:2]:
        loads[n].wait()
    gather = Gather(pc, r["g"], chunks, [r["gs%d" % k] for k in range(8)])
    lower_heads(r, pc, chunks, gather)
    layer = Layer(r, pc)
    rows, length = layer.rows, layer.length
    tok, tokw, window, xr, owned = r["tok"], r["tokw"], r["xw"], r["xrecv"], r["owned"]
    share = Share(
        pc,
        pairs,
        lambda low, high, target: tok.at[pl.ds(low % rows, high - low)],
        lambda low, high, target: tokw.at[in_window(low, high, target, rows, length)],
        r["share_sems"],
    )
    home = Share(
        pc,
        [(t, s, low, high) for s, t, low, high in pairs],
        lambda low, high, target: window.at[in_window(low, high, other_end(pairs, target, low), rows, length)],
        lambda low, high, target: xr.at[1 if low % rows == 0 else 0, pl.ds(0, high - low)],
        r["home_sems"],
    )
    spread = Sum5(pc, r["table"], r["table_slots"], r["table_sems"])
    total = Sum5(pc, r["sums"], r["sum_slots"], r["sum_sems"])

    def emit(j, value):
        a, low, w, _ = back_chunks[j]
        owned[a, :, low : low + w] = value
        line = col_sum(value * value)
        r["squares"][...] += sum(line[:, k : k + 128] for k in range(0, w, 128))

    grads = (r["hid"], r["g"].at[UP], r["g"].at[DOWN])
    back = Scatter(
        pc, grads, back_chunks, r["rc"], r["r3"], r["r2"], r["rz"], [r["ss%d" % k] for k in range(9)], emit
    )

    def start():
        for m in range(4):

            def own_tokens(m=m):
                for at, where in own_parts(m, rows, length):
                    tokw[where[0], where[1], :] = tok[at, :]

            pl.when(pc.m == m)(own_tokens)

    def share_start():
        loads["tok"].wait()
        share.start()

    def masks():
        for n in ("seg", "grp", "ans"):
            loads[n].wait()
        layer.masks()

    def second_norm():
        loads["out_grad"].wait()
        layer.second_norm()
        stores["block_out"].start()

    def rest():
        for n in INPUTS[2:6]:
            loads[n].wait()
        lower_rest(r, pc, chunks, gather)
        spread.start(0)

    def table_step(k):
        spread.end(k)
        if k < 4:
            spread.start(k + 1)
        else:
            r["tab"][...] = r["table"][...].astype(F32)

    def sums_start():
        r["sums"][14:16, :] = jnp.zeros_like(r["sums"][14:16, :])
        total.start(0)

    def sums_step(k):
        total.end(k)
        if k < 4:
            total.start(k + 1)
        else:
            stores["sums"].start()

    def sent():
        gather.finish()
        share.wait_send()
        spread.finish()

    def homeward():
        for m in range(4):

            def own_rows(m=m):
                for at, where in own_parts(m, rows, length):
                    r["acc"][at, :] += window[where[0], where[1], :].astype(F32)

            pl.when(pc.m == m)(own_rows)

    def take():
        home.wait_recv()
        for source, target, low, high in home.pairs:

            def add(source=source, target=target, low=low, high=high):
                at = slice(low - target * rows, high - target * rows)
                k = 1 if low % rows == 0 else 0
                r["acc"][at, :] += xr[k, : high - low, :].astype(F32)

            pl.when(pc.m == target)(add)
        r["input_grad"][...] = r["acc"][...].astype(BF16)
        stores["input_grad"].start()

    steps = {
        "own": gather.own,
        "z": gather.z_step,
        "p": gather.p_step,
        "t": gather.t_step,
        "cw": gather.core_wait,
        "share": share_start,
        "shared": share.wait_recv,
        "rest": rest,
        "sp": table_step,
        "sent": sent,
        "start": start,
        "masks": masks,
        "q": layer.queries,
        "kv": layer.keys_values,
        "att": layer.attend,
        "br": layer.branch,
        "n1": layer.first_norm,
        "up": layer.up,
        "dn": layer.down,
        "n2": second_norm,
        "hb": layer.hidden_back,
        "ub": layer.up_back,
        "n1b": layer.first_back,
        "gu": layer.up_grad,
        "mb": layer.mixed_back,
        "ab": layer.attend_back,
        "kb": layer.keys_back,
        "sm0": sums_start,
        "sm": sums_step,
        "turn": layer.turn,
        "aq": layer.query_grad,
        "ak": layer.keys_grad,
        "qi": layer.query_input,
        "wi": layer.window_input,
        "home": home.start,
        "own_in": homeward,
        "take": take,
        "cs": back.core_start,
        "ce": back.core_end,
        "te": back.third_end,
        "se": back.second_end,
        "zs": back.z_step,
        "zl": back.z_last,
        "la": back.last,
    }
    all_here()
    for name, *at in ORDER:
        steps[name](*at)

    stores["owned"].start()
    norm = Total(pc, r["squares"], r["norm_slots"], r["norm_sems"])
    norm.run()
    stores["squares"].start()
    home.wait_send()
    back.finish()
    total.finish()
    norm.finish()
    for copy in stores.values():
        copy.wait()


def lower_heads(r, pc, chunks, gather):
    qkv = r["m_qkv"]
    heads = jnp.concatenate([qkv[0], r["m_out"][...].T, qkv[1], qkv[2]], 1)
    for j, (a, low, w, _) in enumerate(chunks):
        if a == ATT:
            ref = gather.piece(j, pc.z, 0, 0)
            ref[...] = heads[:, low : low + w].astype(BF16)


def lower_rest(r, pc, chunks, gather):
    table, local = r["table"], r["m_qkv"].shape[2]
    for j, (a, low, w, _) in enumerate(chunks):
        if a != ATT:
            ref = gather.piece(j, pc.z, 0, 0)
            ref[...] = r["m_up" if a == UP else "m_down"][:, low : low + w].astype(BF16)
    outer = pc.z * 2 + pc.x
    norm, bias = r["m_norm"], r["m_bias"]
    part, piece = norm.shape[2], bias.shape[1]
    width, columns = table.shape[1], 8 * piece
    wide = r["norm_wide"]
    wide[...] = jnp.zeros_like(wide)
    for k in range(6):
        wide[k : k + 1, :part] = norm[k]
    rows = pltpu.roll(wide[...], pc.m * local + outer * part, 1)
    line = r["bias_wide"]
    line[...] = jnp.zeros_like(line)
    line[0:1, :piece] = bias[...]
    line = pltpu.roll(line[...], outer * piece, 1)[0:1]
    head = line[:, : 2 * local]
    early = lax.broadcasted_iota(jnp.int32, head.shape, 1) < local
    attention = jnp.concatenate([jnp.where(early, head, 0.0), jnp.where(early, 0.0, head)], 1)
    hidden = line[:, 2 * local :]
    row = lax.broadcasted_iota(jnp.int32, (8, width), 0)
    top = jnp.where(row < 6, rows, 0.0)
    top = jnp.where(row == 6 + pc.m, attention, top)
    top = jnp.where(row == 10 + pc.m, hidden, top)
    low = jnp.where(row + 8 == 6 + pc.m, attention, 0.0)
    low = jnp.where(row + 8 == 10 + pc.m, hidden, low)
    table[...] = jnp.concatenate([top, low], 0).astype(BF16)


def other_end(pairs, owner, low):
    return [t for s, t, first, _ in pairs if s == owner and first == low][0]


def in_window(low, high, m, rows, length):
    return low // length - m * rows // length, pl.ds(low % length, high - low)


def own_parts(m, rows, length):
    parts, low = [], m * rows
    while low < (m + 1) * rows:
        high = min((m + 1) * rows, (low // length + 1) * length)
        parts.append((slice(low - m * rows, high - m * rows), in_window(low, high, m, rows, length)))
        low = high
    return parts


def run_layer(masters, tok, out_grad, seg, grp, ans, pad):
    per, cols = masters[2].shape
    rows, width = tok.shape
    length = seg.shape[1]
    hidden = 4 * cols
    window = max((m * rows + rows - 1) // length - m * rows // length + 1 for m in range(4))
    blocks = rows // 128
    pairs = overlaps(rows, length)
    chunks = chunks_of((ATT, UP, DOWN), cols, WAYS)
    back_chunks = chunks_of((DOWN, UP, ATT), cols, BACK_WAYS)
    most = max(high - low for _, _, low, high in pairs)
    bufs, sems = scatter_scratch(back_chunks, per)
    scratch = {
        "g": pltpu.VMEM((3, 4, 2, per, hidden), BF16),
        "table": pltpu.VMEM((16, width), BF16),
        "norm_wide": pltpu.VMEM((8, width), F32),
        "bias_wide": pltpu.VMEM((8, 8 * masters[5].shape[1]), F32),
        "tab": pltpu.VMEM((16, width), F32),
        "table_slots": pltpu.VMEM((10, 16, width), BF16),
        "tokw": pltpu.VMEM((window, length, width), BF16),
        "bias": pltpu.VMEM((blocks, 128, length), F32),
        "q": pltpu.VMEM((4, rows, 256), BF16),
        "kv": pltpu.VMEM((4, window, length, cols // 2), BF16),
        "shares": pltpu.VMEM((4, blocks, 3, 128, length), BF16),
        "o": pltpu.VMEM((4, rows, 256), BF16),
        "do": pltpu.VMEM((rows, 256), BF16),
        "dkv_acc": pltpu.VMEM((window, length, cols // 2), F32),
        "acc": pltpu.VMEM((rows, width), F32),
        "xh": pltpu.VMEM((rows, width), F32),
        "rs": pltpu.VMEM((rows, 1), F32),
        "hb": pltpu.VMEM((rows, width), BF16),
        "dz": pltpu.VMEM((rows, width), BF16),
        "hid": pltpu.VMEM((4, 2, per, hidden), BF16),
        "turned": pltpu.VMEM((width, rows), BF16),
        "turned2": pltpu.VMEM((width, rows), BF16),
        "turnedw": pltpu.VMEM((window, width, length), BF16),
        "xw": pltpu.VMEM((window, length, width), BF16),
        "xrecv": pltpu.VMEM((2, most, width), BF16),
        "sum_slots": pltpu.VMEM((10, 16, width), F32),
        "share_sems": pltpu.SemaphoreType.DMA((4,)),
        "home_sems": pltpu.SemaphoreType.DMA((4,)),
        "table_sems": pltpu.SemaphoreType.DMA((10,)),
        "norm_slots": pltpu.VMEM((12, 8, 128), F32),
        "norm_sems": pltpu.SemaphoreType.DMA((20,)),
        "sum_sems": pltpu.SemaphoreType.DMA((10,)),
    }
    scratch.update(zip(("rc", "r3", "r2", "rz"), bufs))
    scratch.update(("gs%d" % k, s) for k, s in enumerate(gather_sems(len(chunks))))
    scratch.update(("ss%d" % k, s) for k, s in enumerate(sems))
    given = dict(zip(INPUTS, list(masters) + [tok, out_grad, seg, grp, ans]))
    scratch.update((n, pltpu.VMEM(v.shape, v.dtype)) for n, v in given.items())
    made = dict(
        block_out=jax.ShapeDtypeStruct((rows, width), BF16),
        input_grad=jax.ShapeDtypeStruct((rows, width), BF16),
        owned=jax.ShapeDtypeStruct((3, per, cols), F32),
        sums=jax.ShapeDtypeStruct((16, width), F32),
        squares=jax.ShapeDtypeStruct((8, 128), F32),
    )
    scratch.update((n, pltpu.VMEM(v.shape, v.dtype)) for n, v in made.items())
    scratch["load_sems"] = pltpu.SemaphoreType.DMA((len(INPUTS),))
    scratch["store_sems"] = pltpu.SemaphoreType.DMA((len(OUTPUTS),))
    names = tuple("hbm_" + n for n in INPUTS) + ("pad",) + tuple("hbm_" + n for n in OUTPUTS) + tuple(scratch)
    anywhere = pl.BlockSpec(memory_space=pl.ANY)
    return pl.pallas_call(
        functools.partial(kernel, names, chunks, back_chunks, pairs),
        out_shape=list(made.values()),
        in_specs=[anywhere] * len(INPUTS) + [pl.BlockSpec(memory_space=pltpu.SMEM)],
        out_specs=[anywhere] * len(OUTPUTS),
        scratch_shapes=list(scratch.values()),
        compiler_params=pltpu.CompilerParams(collective_id=0, has_side_effects=True, vmem_limit_bytes=62 * 2**20),
        name="layer",
    )(*masters, tok, out_grad, seg, grp, ans, pad)


def adam_update(weight, grad, first, second, factor, decayed, rate):
    clipped = grad * factor
    first_new = beta_first * first + (1.0 - beta_first) * clipped
    second_new = beta_second * second + (1.0 - beta_second) * clipped * clipped
    ratio = (
        first_new
        / (1.0 - beta_first**STEP)
        / (jnp.sqrt(second_new / (1.0 - beta_second**STEP)) + adam_epsilon)
    )
    if decayed:
        ratio = ratio + decay_rate * weight
    return (weight - rate * ratio, first_new, second_new)


def update_kernel(*refs):
    given, (block_out, input_grad, norm_out), made = refs[:23], refs[23:26], refs[26:44]
    held, (grad_norm, load_sems, store_sems) = refs[44:67], refs[67:]
    loads = [pltpu.make_async_copy(a, b, load_sems.at[k]) for k, (a, b) in enumerate(zip(given, held))]
    outs = [held[2 + n * 6 + k] for n in range(3) for k in range(6)]
    stores = [pltpu.make_async_copy(a, b, store_sems.at[k]) for k, (a, b) in enumerate(zip(outs, made))]
    order = [1, 22, 0] + [2 + n * 6 + k for k in (2, 3, 0, 1, 4, 5) for n in range(3)] + [20, 21]
    for k in order:
        loads[k].start()
    passed = [
        pltpu.make_async_copy(held[20], block_out, store_sems.at[18]),
        pltpu.make_async_copy(held[21], input_grad, store_sems.at[19]),
        pltpu.make_async_copy(grad_norm, norm_out, store_sems.at[20]),
    ]
    owned, total = held[:2]
    masters, firsts, seconds = held[2:8], held[8:14], held[14:20]
    loads[1].wait()
    loads[22].wait()
    place = lax.axis_index("outer") * lax.axis_size("inner") + lax.axis_index("inner")
    mp = lax.axis_index("mp")
    local = masters[0].shape[2]
    width = total.shape[1]
    lane = lax.broadcasted_iota(jnp.int32, (4, width), 1)
    head, hidden = total[6:10, :], total[10:14, :]
    head = jnp.where((lane < local) | (lane >= 3 * local), head, 0.0)

    def square(v):
        return jnp.sum(jnp.sum(v * v, 0, keepdims=True), 1, keepdims=True)

    squares = jnp.sum(held[22][0:1, :], 1, keepdims=True) + square(total[0:6, :]) + square(head) + square(hidden)
    norm = jnp.sqrt(squares)
    grad_norm[...] = norm
    passed[2].start()
    factor = jnp.minimum(1.0, clip_limit / norm)
    mine = lax.broadcasted_iota(jnp.int32, (4, width), 0) == mp
    head = jnp.sum(jnp.where(mine, head, 0.0), 0, keepdims=True)
    hidden = jnp.sum(jnp.where(mine, hidden, 0.0), 0, keepdims=True)
    line = jnp.concatenate([head[:, : 2 * local] + head[:, 2 * local :], hidden], 1)
    part, piece = masters[4].shape[2], masters[5].shape[1]
    line = jnp.broadcast_to(line, (8, line.shape[1]))
    line = pltpu.roll(line, lax.rem(line.shape[1] - place * piece, line.shape[1]), 1)[0:1, :piece]
    norms = pltpu.roll(total[0:8, :], lax.rem(width - (mp * local + place * part), width), 1)

    def update(k, at, grad):
        values = adam_update(masters[k][at], grad, firsts[k][at], seconds[k][at], factor, k < 4, learn_rates[k])
        for n, value in enumerate(values):
            outs[n * 6 + k][at] = value

    def ready(k):
        for n in range(3):
            loads[2 + n * 6 + k].wait()

    def done(k):
        for n in range(3):
            stores[n * 6 + k].start()

    loads[0].wait()
    everything = (slice(None), slice(None))
    for k, grad in ((2, owned[1]), (3, owned[2])):
        ready(k)
        update(k, everything, grad)
        done(k)
    attention = owned[0]
    ready(0)
    update(0, 0, attention[:, :local])
    update(0, 1, attention[:, 2 * local : 3 * local])
    update(0, 2, attention[:, 3 * local :])
    done(0)
    ready(1)
    update(1, everything, attention[:, local : 2 * local].T)
    done(1)
    ready(4)
    for k in range(6):
        update(4, k, norms[k : k + 1, :part])
    done(4)
    ready(5)
    update(5, everything, line)
    done(5)
    for k in range(2):
        loads[20 + k].wait()
        passed[k].start()
    for copy in stores + passed:
        copy.wait()


def update(owned, total, squares, block_out, input_grad, masters, firsts, seconds):
    anywhere = pl.BlockSpec(memory_space=pl.ANY)
    given = [owned, total, *masters, *firsts, *seconds, block_out, input_grad, squares]

    def like(v):
        return jax.ShapeDtypeStruct(v.shape, v.dtype)

    return pl.pallas_call(
        update_kernel,
        out_shape=[like(block_out), like(input_grad), jax.ShapeDtypeStruct((1, 1), F32)] + [like(m) for m in masters] * 3,
        in_specs=[anywhere] * len(given),
        out_specs=[anywhere] * 21,
        scratch_shapes=[pltpu.VMEM(v.shape, v.dtype) for v in given]
        + [pltpu.VMEM((1, 1), F32), pltpu.SemaphoreType.DMA((len(given),)), pltpu.SemaphoreType.DMA((21,))],
        compiler_params=pltpu.CompilerParams(vmem_limit_bytes=62 * 2**20),
        name="update",
    )(*given)


def body(tokens, out_grad, segment_ids, group_ids, answer_ids, pad_lengths, *states):
    def turned(values):
        return [v.T if k == 3 else v for k, v in enumerate(values)]

    masters, firsts, seconds = turned(states[:6]), turned(states[6:12]), turned(states[12:])
    inner = lax.axis_size("inner")
    shared = masters
    if inner > 1:
        shared = [lax.all_gather(v, "inner", axis=d, tiled=True) for v, d in zip(masters, (1, 1, 0, 0, 2, 1))]
    block_out, input_grad, owned, total, squares = run_layer(
        shared, tokens, out_grad, segment_ids, group_ids, answer_ids, pad_lengths
    )
    if inner > 1:
        owned = lax.psum_scatter(owned, "inner", scatter_dimension=1, tiled=True)
        total = lax.psum(total, "inner")
        squares = lax.psum(jnp.sum(owned * owned), ("outer", "inner", "mp"))
        squares = jnp.full((8, 128), squares / 128)
    results = update(owned, total, squares, block_out, input_grad, masters, firsts, seconds)
    updated = [v for n in range(3) for v in turned(results[3 + 6 * n : 9 + 6 * n])]
    return (results[0], results[1], results[2][0, 0]) + tuple(updated)


def solution(mesh):
    dp = mesh.shape["dp"]
    outer = 8
    grid = Mesh(mesh.devices.reshape(outer, dp // outer, mesh.shape["mp"]), ("outer", "inner", "mp"))
    d = ("outer", "inner")
    both = P(d + ("mp",), None)
    states = (P(None, d, "mp"), P("mp", d), P(d, "mp"), P("mp", d), P(None, "mp", d), P("mp", d))
    in_specs = (both, both, P(d, None), P(d, None), P(d, None), P(d)) + states * 3
    out_specs = (both, both, P()) + states * 3
    return jax.shard_map(body, mesh=grid, in_specs=in_specs, out_specs=out_specs, check_vma=False)
```

```python
import functools
import jax
import jax.numpy as jnp
import numpy as np
from jax import lax
from jax.sharding import Mesh, PartitionSpec as P
from jax.experimental import pallas as pl
from jax.experimental.pallas import tpu as pltpu

MESH = pl.DeviceIdType.MESH
F32 = jnp.float32
BF16 = jnp.bfloat16
HD = 64
STEP = 5

norm_epsilon = 1e-06
adam_epsilon = 1e-08
learn_rates = (0.02, 0.1, 0.02, 0.02, 0.5, 0.5)
beta_first = 0.5
beta_second = 0.5
decay_rate = 0.01
clip_limit = 0.05
mask_fill = -1000000000.0
score_scale = 0.125

ATT, UP, DOWN = 0, 1, 2
NEAR, LONG, DIRECT = 0, 1, 2


def pick(index, values):
    out = values[-1]
    for k in range(len(values) - 1):
        out = jnp.where(index == k, values[k], out)
    return out


class Place:
    def __init__(self):
        outer = lax.axis_index("outer")
        self.sub = lax.axis_index("inner")
        self.m = lax.axis_index("mp")
        self.z = outer // 2
        self.x = lax.rem(outer, 2)
        self.y = self.m // 2
        self.c = lax.rem(self.m, 2)
        self.first = self.c == 0
        self.sib = self.at(c=1 - self.c)
        x, y = self.line(1, 0)
        self.second = self.at(x=x, y=y)
        x, y = self.line(0, 1)
        self.third = self.at(x=x, y=y)

    def at(self, z=None, x=None, y=None, c=None):
        z = self.z if z is None else z
        x = self.x if x is None else x
        y = self.y if y is None else y
        c = self.c if c is None else c
        return (z * 2 + x, self.sub, y * 2 + c)

    def mate(self, m):
        return (self.z * 2 + self.x, self.sub, m)

    def line(self, side, far, other_core=False):
        first = (1 - self.c if other_core else self.c) == 0
        x = jnp.where(first, side, far)
        y = jnp.where(first, far, side)
        return self.x + x - 2 * self.x * x, self.y + y - 2 * self.y * y

    def order(self, t):
        return pick(self.z, [(0, 1, 2, 3), (1, 0, 3, 2), (2, 2, 1, 1), (3, 3, 0, 0)][t])


def remote(src, dst, send, recv, device):
    return pltpu.make_async_remote_copy(
        src_ref=src, dst_ref=dst, send_sem=send, recv_sem=recv, device_id=device, device_id_type=MESH
    )


def peers(place):
    z, x, y, c = place.z, place.x, place.y, place.c

    def other(v, bit):
        return 1 - v if bit else v

    plane = [place.at(x=other(x, k & 4), y=other(y, k & 2), c=other(c, k & 1)) for k in (7, 6, 5, 3, 4, 2, 1)]
    return plane + [place.at(z=across(z, k)) for k in (3, 2, 1)]


def across(z, k):
    low, high = lax.rem(z, 2), z // 2
    return (1 - high if k & 2 else high) * 2 + (1 - low if k & 1 else low)


def greet(place):
    barrier = pltpu.get_barrier_semaphore()
    for device in peers(place):
        pl.semaphore_signal(barrier, inc=1, device_id=device, device_id_type=MESH)
    return lambda: pl.semaphore_wait(barrier, 10)


class Gather:
    def __init__(self, place, g, chunks, sems):
        self.p, self.g, self.chunks = place, g, chunks
        self.zs, self.zr, self.ps, self.pr, self.ts, self.tr, self.cs, self.cr = sems
        self.width = g.shape[4] // 4
        self.sent = []

    def piece(self, j, z, side, far, core=False):
        x, y = self.p.line(side, far, core)
        c = 1 - self.p.c if core else self.p.c
        a, low, w, _ = self.chunks[j]
        cols = pl.ds(pl.multiple_of((y * 2 + c) * self.width + low, 128), w)
        if z is None:
            return self.g.at[a, :, x, :, cols]
        return self.g.at[a, z, x, :, cols]

    def go(self, ref, send, recv, device, when=None):
        copy = remote(ref, ref, send, recv, device)
        if when is None:
            copy.start()
        else:
            pl.when(when)(copy.start)
        self.sent.append((copy, when))

    def arrived(self, ref, recv):
        remote(ref, ref, recv, recv, self.p.sib).wait_recv()

    def z_send(self, j, side, src, index, to, when):
        self.go(self.piece(j, src, side, 0), self.zs.at[j, side, index], self.zr.at[j, side, src], self.p.at(z=to), when)

    def z_both(self, j, side):
        z = self.p.z
        self.z_send(j, side, z, z, z + 1, z < 3)
        self.z_send(j, side, z, 4, z - 1, z > 0)

    def third(self, j, side, src):
        k = side * 4 + src
        self.go(self.piece(j, src, side, 0), self.ts.at[j, k], self.tr.at[j, k], self.p.third)

    def second(self, j, src):
        self.go(self.piece(j, src, 0, 0), self.ps.at[j, src], self.pr.at[j, src], self.p.second)

    def to_sibling(self, j, side, far):
        k = side + 2 * far
        self.go(self.piece(j, None, side, far), self.cs.at[j, k], self.cr.at[j, k], self.p.sib)

    def own(self, j):
        self.second(j, self.p.z)
        self.z_both(j, 0)
        self.third(j, 0, self.p.z)

    def z_step(self, j, t, side=0):
        z = self.p.z
        src = self.p.order(t)
        self.arrived(self.piece(j, src, side, 0), self.zr.at[j, side, src])
        to = jnp.where(z > src, z + 1, z - 1)
        self.z_send(j, side, src, src, to, (to >= 0) & (to <= 3))
        if self.chunks[j][3] != LONG:
            self.second(j, src)
        self.third(j, side, src)
        if t == 3:
            self.to_sibling(j, side, 0)

    def p_step(self, j, t):
        src = self.p.order(t)
        self.arrived(self.piece(j, src, 1, 0), self.pr.at[j, src])
        if self.chunks[j][3] == LONG:
            self.z_both(j, 1)
        self.third(j, 1, src)
        if t == 3:
            self.to_sibling(j, 1, 0)

    def t_step(self, j, side):
        for t in range(4):
            src = self.p.order(t)
            self.arrived(self.piece(j, src, side, 1), self.tr.at[j, side * 4 + src])
        self.to_sibling(j, side, 1)

    def core_wait(self, j):
        for k, (side, far) in enumerate(((0, 0), (1, 0), (0, 1), (1, 1))):
            self.arrived(self.piece(j, None, side, far, True), self.cr.at[j, k])

    def finish(self):
        for copy, when in self.sent:
            if when is None:
                copy.wait_send()
            else:
                pl.when(when)(copy.wait_send)
        self.sent = []


def gather_sems(chunks):
    sizes = ((2, 5), (2, 4), (4,), (4,), (8,), (8,), (4,), (4,))
    return [pltpu.SemaphoreType.DMA((chunks,) + n) for n in sizes]


def overlaps(rows, length):
    pairs = []
    for m in range(3):
        edge = (m + 1) * rows
        low = edge // length * length
        if low == edge:
            continue
        pairs.append((m, m + 1, max(low, m * rows), edge))
        pairs.append((m + 1, m, edge, min(low + length, edge + rows)))
    return pairs


class Share:
    def __init__(self, place, pairs, src, dst, sems):
        self.p, self.pairs, self.src, self.dst, self.sems = place, pairs, src, dst, sems

    def copy(self, pair):
        source, target, low, high = pair
        k = 0 if source < target else 1
        return remote(self.src(low, high, target), self.dst(low, high, target), self.sems.at[k], self.sems.at[2 + k], self.p.mate(target))

    def start(self):
        for pair in self.pairs:
            pl.when(self.p.m == pair[0])(self.copy(pair).start)

    def wait_recv(self):
        for pair in self.pairs:
            pl.when(self.p.m == pair[1])(self.copy(pair).wait_recv)

    def wait_send(self):
        for pair in self.pairs:
            pl.when(self.p.m == pair[0])(self.copy(pair).wait_send)


class Sum5:
    def __init__(self, place, table, slots, sems):
        self.p, self.table, self.slots, self.sems = place, table, slots, sems
        z = place.z
        self.peers = [
            place.at(z=z + 1 - 2 * lax.rem(z, 2)),
            place.at(z=z + 2 - 4 * (z // 2)),
            place.at(x=1 - place.x),
            place.at(y=1 - place.y),
            place.sib,
        ]

    def copy(self, k):
        return remote(self.slots.at[5 + k], self.slots.at[k], self.sems.at[k], self.sems.at[5 + k], self.peers[k])

    def start(self, k):
        self.slots[5 + k] = self.table[...]
        self.copy(k).start()

    def end(self, k):
        self.copy(k).wait_recv()
        self.table[...] = self.table[...] + self.slots[k]

    def finish(self):
        for k in range(5):
            self.copy(k).wait_send()


class Total:
    def __init__(self, place, tile, slots, sems):
        self.p, self.tile, self.slots, self.sems = place, tile, slots, sems
        self.copies = [remote(slots.at[0 if k < 7 else 11], slots.at[1 + k], sems.at[k], sems.at[10 + k], d) for k, d in enumerate(peers(place))]

    def run(self):
        for first, ks in ((0, range(7)), (11, range(7, 10))):
            self.slots[first] = self.tile[...]
            for k in ks:
                self.copies[k].start()
            total = self.tile[...]
            for k in ks:
                self.copies[k].wait_recv()
                total = total + self.slots[1 + k]
            self.tile[...] = total

    def finish(self):
        for copy in self.copies:
            copy.wait_send()


class Scatter:
    def __init__(self, place, grads, chunks, rc, r3, r2, rz, sems, emit):
        self.p, self.grads, self.chunks = place, grads, chunks
        self.rc, self.r3, self.r2, self.rz = rc, r3, r2, rz
        self.cs, self.cr, self.ts, self.tr, self.ps, self.pr, self.us, self.ds, self.zr = sems
        self.emit = emit
        self.width = grads[0].shape[3] // 4
        self.sent = []
        self.seconds, self.lines, _, _ = scatter_slots(chunks)

    def region(self, j, side, far, core=False):
        x, y = self.p.line(side, far, core)
        c = 1 - self.p.c if core else self.p.c
        a, low, w, _ = self.chunks[j]
        return a, x, pl.ds(pl.multiple_of((y * 2 + c) * self.width + low, 128), w)

    def block(self, j, side, far, core=False):
        a, x, cols = self.region(j, side, far, core)
        return self.grads[a].at[:, x, :, cols]

    def shard(self, j, side, z):
        a, x, cols = self.region(j, side, 0)
        return self.grads[a].at[z, x, :, cols]

    def go(self, src, dst, send, recv, device, when=None):
        copy = remote(src, dst, send, recv, device)
        if when is None:
            copy.start()
        else:
            pl.when(when)(copy.start)
        self.sent.append((copy, when))

    def arrived(self, ref, recv):
        remote(ref, ref, recv, recv, self.p.sib).wait_recv()

    def core_start(self, j):
        for far in (1, 0):
            for side in (1, 0):
                k = far * 2 + side
                self.go(self.block(j, side, far, True), self.rc.at[j, k], self.cs.at[j, k], self.cr.at[j, k], self.p.sib)

    def add(self, j, side, far, other):
        a, x, cols = self.region(j, side, far)

        def step(k):
            here = self.grads[a].at[k, x, :, cols]
            here[...] = (here[...].astype(F32) + other[k].astype(F32)).astype(BF16)

        pl.loop(0, 4)(step)

    def core_end(self, j, far):
        for side in (1, 0):
            k = far * 2 + side
            self.arrived(self.rc.at[j, k], self.cr.at[j, k])
            self.add(j, side, far, self.rc.at[j, k])
            if far == 1:
                self.go(self.block(j, side, 1), self.r3.at[j, side], self.ts.at[j, side], self.tr.at[j, side], self.p.third)

    def third_end(self, j, side):
        self.arrived(self.r3.at[j, side], self.tr.at[j, side])
        self.add(j, side, 0, self.r3.at[j, side])
        if self.chunks[j][3] == LONG:
            self.line_start(j, side)
        elif side == 1:
            slot = self.r2.at[pl.ds(self.seconds[j], 4)]
            self.go(self.block(j, 1, 0), slot, self.ps.at[j], self.pr.at[j], self.p.second)

    def second_end(self, j):
        slot = self.r2.at[pl.ds(self.seconds[j], 4)]
        self.arrived(slot, self.pr.at[j])
        self.add(j, 0, 0, slot)
        if self.chunks[j][3] != DIRECT:
            self.line_start(j, 0)
            return
        n = self.lines[j]
        for k in (3, 2, 1):
            to = across(self.p.z, k)
            self.go(self.shard(j, 0, to), self.rz.at[n, k], self.us.at[n, k], self.zr.at[n, k], self.p.at(z=to))

    def up(self, j, side, d, when):
        n = self.lines[j] + side
        self.go(self.shard(j, side, d), self.rz.at[n, d], self.us.at[n, d], self.zr.at[n, d], self.p.at(z=self.p.z + 1), when)

    def down(self, j, side, d, when):
        n = self.lines[j] + side
        slot = jnp.where(d == self.p.z - 1, 4, d)
        self.go(self.shard(j, side, d), self.rz.at[n, slot], self.ds.at[n, d], self.zr.at[n, slot], self.p.at(z=self.p.z - 1), when)

    def line_start(self, j, side):
        z = self.p.z
        for d in range(3):
            self.up(j, side, 3 - d, z == 0)
            self.down(j, side, d, z == 3)

    def fold(self, j, side, d, slot):
        n = self.lines[j] + side
        self.arrived(self.rz.at[n, slot], self.zr.at[n, slot])
        ref = self.shard(j, side, d)
        ref[...] = (ref[...].astype(F32) + self.rz[n, slot].astype(F32)).astype(BF16)

    def relay(self, j, side, d, send, when):
        pl.when(when)(lambda: self.fold(j, side, d, d))
        send(j, side, d, when)

    def z_step(self, j, side, t):
        z = self.p.z
        if t < 2:
            self.relay(j, side, 3 - t, self.up, z == 1)
            self.relay(j, side, t, self.down, z == 2)
        else:
            self.relay(j, side, 3, self.up, z == 2)
            self.relay(j, side, 0, self.down, z == 1)

    def z_last(self, j, side):
        z = self.p.z
        pl.when(z > 0)(lambda: self.fold(j, side, z, z))
        pl.when(z < 3)(lambda: self.fold(j, side, z, 4))
        if side == 1:
            slot = self.r2.at[self.seconds[j]]
            self.go(self.shard(j, 1, z), slot, self.ps.at[j], self.pr.at[j], self.p.second)

    def last(self, j):
        z = self.p.z
        if self.chunks[j][3] == DIRECT:
            n = self.lines[j]
            total = self.shard(j, 0, z)[...].astype(F32)
            for k in (1, 2, 3):
                self.arrived(self.rz.at[n, k], self.zr.at[n, k])
                total = total + self.rz[n, k].astype(F32)
            self.emit(j, total)
        elif self.chunks[j][3] == LONG:
            slot = self.r2.at[self.seconds[j]]
            self.arrived(slot, self.pr.at[j])
            self.emit(j, self.shard(j, 0, z)[...].astype(F32) + slot[...].astype(F32))
        else:
            self.z_last(j, 0)
            self.emit(j, self.shard(j, 0, z)[...].astype(F32))

    def finish(self):
        for copy, when in self.sent:
            if when is None:
                copy.wait_send()
            else:
                pl.when(when)(copy.wait_send)
        self.sent = []


def scatter_slots(chunks):
    seconds, lines, n, m = [], [], 0, 0
    for chunk in chunks:
        seconds.append(n)
        lines.append(m)
        n += 1 if chunk[3] == LONG else 4
        m += 2 if chunk[3] == LONG else 1
    return seconds, lines, n, m


def scatter_scratch(chunks, rows):
    n, w = len(chunks), chunks[0][2]
    _, _, seconds, lines = scatter_slots(chunks)
    shapes = ((n, 4, 4), (n, 2, 4), (seconds,), (lines, 5))
    sems = ((n, 4), (n, 4), (n, 2), (n, 2), (n,), (n,), (lines, 4), (lines, 4), (lines, 5))
    return [pltpu.VMEM(s + (rows, w), BF16) for s in shapes], [pltpu.SemaphoreType.DMA(s) for s in sems]


def nt(a, b):
    return lax.dot_general(a, b, (((1,), (1,)), ((), ())), preferred_element_type=F32)


def tn(a, b):
    return lax.dot_general(a, b, (((0,), (0,)), ((), ())), preferred_element_type=F32)


def nn(a, b):
    return jnp.dot(a, b, preferred_element_type=F32)


def even_lanes(shape):
    return lax.broadcasted_iota(jnp.int32, shape, 1) < HD


def keep(values, even):
    mask = even_lanes(values.shape)
    zero = jnp.zeros_like(values)
    return jnp.where(mask, values, zero) if even else jnp.where(mask, zero, values)


def col_sum(values):
    return jnp.sum(values, 0, keepdims=True)


class Layer:
    def __init__(self, refs, place):
        self.__dict__.update(refs)
        self.p = place
        self.rows, self.width = self.tok.shape
        self.length = self.seg.shape[1]
        self.blocks = self.rows // 128
        self.cols = self.g.shape[4] // 4
        self.hidden = self.g.shape[4]
        self.s0 = self.rows * place.m // self.length
        self.s1 = (self.rows * place.m + self.rows - 1) // self.length
        self.window = self.kv.shape[1]

    def w(self, a, low, size):
        return self.g[a, :, :, :, low : low + size].reshape(self.width, size)

    def put(self, ref, low, value):
        size = value.shape[1]
        ref[:, :, :, low : low + size] = value.astype(BF16).reshape(ref.shape[:3] + (size,))

    def gain(self, row):
        return self.tab[pl.ds(row, 1), :]

    def blk(self, i):
        return pl.ds(pl.multiple_of(i * 128, 128), 128)

    def seq_of(self, i):
        return (self.rows * self.p.m + 128 * i) // self.length

    def each_seq(self, run):
        for s in range(self.window):
            if s == 0:
                run(s)
            else:
                pl.when(self.s0 + s <= self.s1)(functools.partial(run, s))

    def masks(self):
        n = self.length
        for i in range(self.blocks):
            s = self.seq_of(i)
            at = lax.rem(self.rows * self.p.m + 128 * i, n)
            seg = self.seg[pl.ds(s, 1), :]
            grp = self.grp[pl.ds(s, 1), :]
            ans = self.ans[pl.ds(s, 1), :]
            seg_q = pick(at // 128, [seg[:, k : k + 128] for k in range(0, n, 128)])
            grp_q = pick(at // 128, [grp[:, k : k + 128] for k in range(0, n, 128)])
            code = jnp.where(seg_q == 0, -1, grp_q).astype(F32)
            code = jnp.transpose(jnp.broadcast_to(code, (8, 128)))[:, :1]
            open_key = (seg == 0) | (ans == 1)
            rule = (code == grp.astype(F32)) | (code < 0.0) | open_key
            position = lax.broadcasted_iota(jnp.int32, (1, n), 1)
            seen = rule & (position < self.pad[s])
            self.bias[i] = jnp.where(seen, 0.0, mask_fill)

    def queries(self, b):
        c = self.cols
        lanes = lax.broadcasted_iota(jnp.int32, (1, 256), 1) < c // 4
        q = nn(self.tok[...], self.w(ATT, b * c, 256)) + self.tab[6 + b : 7 + b, :256]
        self.q[b] = jnp.where(lanes, q * score_scale, 0.0).astype(BF16)

    def keys_values(self, b):
        c = self.cols
        wkv = self.w(ATT, b * c + c // 2, c // 2)

        def one(s):
            self.kv[b, s] = (nn(self.tokw[s], wkv) + self.tab[6 + b : 7 + b, c // 2 :]).astype(BF16)

        self.each_seq(one)

    def heads(self, b, i):
        s = self.seq_of(i) - self.s0
        q0 = self.q[b, self.blk(i), :128]
        q2 = self.q[b, self.blk(i), 128:]
        return s, keep(q0, True), keep(q0, False), q2

    def attend(self, b):
        @pl.loop(0, self.blocks)
        def _(i):
            s, q0, q1, q2 = self.heads(b, i)
            bias = self.bias[i]

            def softmax(scores):
                scores = scores + bias
                e = jnp.exp(scores - jnp.max(scores, -1, keepdims=True))
                return (e * (1.0 / jnp.sum(e, -1, keepdims=True))).astype(BF16)

            t0, t1, t2 = (self.kv[b, s, :, 128 * t : 128 * t + 128] for t in range(3))
            s01 = nt(jnp.concatenate([q0, q1], 0), t0)
            p0, p1, p2 = softmax(s01[:128]), softmax(s01[128:]), softmax(nt(q2, t1))
            self.shares[b, i, 0] = p0
            self.shares[b, i, 1] = p1
            self.shares[b, i, 2] = p2
            o12 = nn(jnp.concatenate([p1, p2], 0), t2)
            self.o[b, self.blk(i), :128] = keep(nn(p0, t1), False).astype(BF16)
            self.o[b, self.blk(i), 128:] = jnp.where(even_lanes((128, 128)), o12[:128], o12[128:]).astype(BF16)

    def row_loop(self, step, sums):
        n = 48

        def run(k, carry):
            at = pl.ds(pl.multiple_of(k * n, n), n)
            return step(at, carry)

        zero = tuple(jnp.zeros((1, self.width), F32) for _ in range(sums))
        return lax.fori_loop(0, self.rows // n, run, zero)

    def accumulate(self, value, first):
        self.acc[...] = value if first else self.acc[...] + value

    def branch(self, b):
        self.accumulate(nt(self.o[b], self.w(ATT, b * self.cols + 128, 256)), b == 0)

    def first_norm(self):
        g1, b1, co = self.gain(0), self.gain(1), self.gain(2)

        def step(at, carry):
            r = self.tok[at, :].astype(F32) + (self.acc[at, :] + co)
            r = r - jnp.mean(r, -1, keepdims=True)
            rs = lax.rsqrt(jnp.mean(r * r, -1, keepdims=True) + norm_epsilon)
            xh = r * rs
            self.xh[at, :] = xh
            self.rs[at, :] = rs
            self.hb[at, :] = (xh * g1 + b1).astype(BF16)
            return carry

        self.row_loop(step, 0)

    def part(self, b, k):
        n = self.cols // PARTS
        return b * self.cols + k * n, n

    def hidden_ref(self, which):
        return self.hid.at[2 * which : 2 * which + 2]

    def get_hidden(self, which, low, n):
        return self.hidden_ref(which)[:, :, :, low : low + n].reshape(self.rows, n)

    def set_hidden(self, which, low, value):
        ref = self.hidden_ref(which)
        ref[:, :, :, low : low + value.shape[1]] = value.astype(BF16).reshape(ref.shape[:3] + value.shape[1:])

    def up(self, b, k):
        low, n = self.part(b, k)
        u = nn(self.hb[...], self.w(UP, low, n)) + self.tab[10 + b : 11 + b, k * n : k * n + n]
        share = 0.5 + 0.5 * lax.erf(u * np.float32(np.sqrt(0.5)))
        self.set_hidden(0, low, u * share)
        self.set_hidden(1, low, share + u * (jnp.exp(-0.5 * (u * u)) * np.float32(1 / np.sqrt(2 * np.pi))))

    def down(self, b, k):
        low, n = self.part(b, k)
        self.accumulate(nt(self.get_hidden(0, low, n), self.w(DOWN, low, n)), b == 0 and k == 0)

    def second_norm(self):
        g1, b1, g2, b2, cd = self.gain(0), self.gain(1), self.gain(3), self.gain(4), self.gain(5)

        def step(at, carry):
            r = (self.xh[at, :] * g1 + b1) + (self.acc[at, :] + cd)
            r = r - jnp.mean(r, -1, keepdims=True)
            rs = lax.rsqrt(jnp.mean(r * r, -1, keepdims=True) + norm_epsilon)
            xh = r * rs
            self.block_out[at, :] = (xh * g2 + b2).astype(BF16)
            grad = self.out_grad[at, :].astype(F32)
            inner = grad * g2
            back = rs * (inner - jnp.mean(inner, -1, keepdims=True) - xh * jnp.mean(inner * xh, -1, keepdims=True))
            self.acc[at, :] = back
            low = back.astype(BF16)
            self.dz[at, :] = low
            return carry[0] + col_sum(grad * xh), carry[1] + col_sum(grad), carry[2] + col_sum(low.astype(F32))

        dg, db, dc = self.row_loop(step, 3)
        self.sums[3:4, :] = dg
        self.sums[4:5, :] = db
        self.sums[5:6, :] = dc

    def hidden_back(self, b, k):
        if b == 0 and k == 0:
            self.turned[...] = self.dz[...].T
        low, n = self.part(b, k)
        du = nn(self.dz[...], self.w(DOWN, low, n)) * self.get_hidden(1, low, n).astype(F32)
        du = du.astype(BF16)
        self.set_hidden(1, low, du)
        self.sums[10 + b : 11 + b, k * n : k * n + n] = col_sum(du.astype(F32))
        self.put(self.g.at[DOWN], low, nn(self.turned[...], self.get_hidden(0, low, n)))

    def up_back(self, b):
        low = b * self.cols
        self.acc[...] += nt(self.get_hidden(1, low, self.cols), self.w(UP, low, self.cols))

    def up_grad(self, b, k):
        if b == 0 and k == 0:
            self.turned[...] = self.hb[...].T
        low, n = self.part(b, k)
        self.put(self.g.at[UP], low, nn(self.turned[...], self.get_hidden(1, low, n)))

    def first_back(self):
        g1 = self.gain(0)

        def step(at, carry):
            grad = self.acc[at, :]
            xh = self.xh[at, :]
            inner = grad * g1
            back = self.rs[at, :] * (
                inner - jnp.mean(inner, -1, keepdims=True) - xh * jnp.mean(inner * xh, -1, keepdims=True)
            )
            self.acc[at, :] = back
            low = back.astype(BF16)
            self.dz[at, :] = low
            return carry[0] + col_sum(grad * xh), carry[1] + col_sum(grad), carry[2] + col_sum(low.astype(F32))

        dg, db, dc = self.row_loop(step, 3)
        self.sums[0:1, :] = dg
        self.sums[1:2, :] = db
        self.sums[2:3, :] = dc

    def mixed_back(self, b):
        do = nn(self.dz[...], self.w(ATT, b * self.cols + 128, 256))
        lanes = lax.broadcasted_iota(jnp.int32, (1, 256), 1) >= HD
        self.do[...] = jnp.where(lanes, do, 0.0).astype(BF16)
        self.dkv_acc[...] = jnp.zeros_like(self.dkv_acc)

    def attend_back(self, b, i):
        s, q0, q1, q2 = self.heads(b, i)
        t0, t1, t2 = (self.kv[b, s, :, 128 * t : 128 * t + 128] for t in range(3))
        do0 = self.do[self.blk(i), :128]
        do12 = self.do[self.blk(i), 128:]
        do1, do2 = keep(do12, True), keep(do12, False)
        dp12 = nt(jnp.concatenate([do1, do2], 0), t2)

        def back(h, dp):
            low = self.shares[b, i, h]
            p = low.astype(F32)
            scaled = p * dp
            return low, (scaled - p * jnp.sum(scaled, -1, keepdims=True)).astype(BF16)

        p0, ds0 = back(0, nt(do0, t1))
        p1, ds1 = back(1, dp12[:128])
        p2, ds2 = back(2, dp12[128:])
        dq01 = nn(jnp.concatenate([ds0, ds1], 0), t0)
        dq0 = jnp.where(even_lanes((128, 128)), dq01[:128], dq01[128:])
        dq2 = keep(nn(ds2, t1), True)
        self.q[b, self.blk(i), :128] = (dq0 * score_scale).astype(BF16)
        self.q[b, self.blk(i), 128:] = (dq2 * score_scale).astype(BF16)
        rows = jnp.concatenate
        self.dkv_acc[s, :, :128] += tn(rows([ds0, ds1], 0), rows([q0, q1], 0))
        self.dkv_acc[s, :, 128:256] += tn(rows([ds2, p0], 0), rows([q2, do0], 0))
        self.dkv_acc[s, :, 256:] += tn(rows([p1, p2], 0), rows([do1, do2], 0))

    def keys_back(self, b):
        c = self.cols
        total = jnp.zeros((1, c // 2), F32)
        for s in range(self.window):
            low = self.dkv_acc[s].astype(BF16)
            self.kv[b, s] = low
            total = total + col_sum(low.astype(F32))
        first = col_sum(self.q[b].astype(F32))
        gap = jnp.zeros((1, c // 2 - 256), F32)
        self.sums[6 + b : 7 + b, :] = jnp.concatenate([first, gap, total], 1)

    def turn(self):
        self.turned[...] = self.tok[...].T
        self.turned2[...] = self.dz[...].T

        def one(s):
            self.turnedw[s] = self.tokw[s].T

        self.each_seq(one)

    def query_grad(self, b):
        c = self.cols
        dq = nn(self.turned[...], self.q[b])
        do = nn(self.turned2[...], self.o[b])
        self.put(self.hid, b * c, dq[:, :128])
        self.put(self.hid, b * c + 128, dq[:, 128:] + do[:, :128])
        self.put(self.hid, b * c + 256, do[:, 128:])

    def keys_grad(self, b):
        c = self.cols

        def finish(count):
            total = nn(self.turnedw[0], self.kv[b, 0])
            for s in range(1, count):
                total = total + nn(self.turnedw[s], self.kv[b, s])
            self.put(self.hid, b * c + c // 2, total)

        for count in range(1, self.window + 1):
            pl.when(self.s1 - self.s0 + 1 == count)(functools.partial(finish, count))

    def query_input(self, b):
        self.acc[...] += nt(self.q[b], self.w(ATT, b * self.cols, 256))

    def window_input(self, s):
        c, half = self.cols, self.width // 2

        def run():
            for k in range(2):
                for b in range(4):
                    w = self.g[ATT, 2 * k : 2 * k + 2, :, :, b * c + c // 2 : b * c + c].reshape(half, c // 2)
                    part = nt(self.kv[b, s], w)
                    self.dkv_acc[k] = part if b == 0 else self.dkv_acc[k] + part
                self.xw[s, :, k * half : k * half + half] = self.dkv_acc[k].astype(BF16)

        if s == 0:
            run()
        else:
            pl.when(self.s0 + s <= self.s1)(run)


PARTS = 2
WAYS = (NEAR, LONG, LONG, NEAR, LONG, LONG)
BACK_WAYS = (DIRECT, LONG, DIRECT, LONG, DIRECT, DIRECT)


def chunks_of(order, cols, ways):
    w = cols // PARTS
    return [(order[k // PARTS], k % PARTS * w, w, ways[k]) for k in range(3 * PARTS)]


ORDER = (
    ("own", 0), ("own", 1), ("share",), ("rest",), ("sp", 0), ("z", 0, 1, 0), ("start",), ("p", 1, 0),
    ("sp", 1), ("z", 0, 2, 0), ("z", 0, 3, 0), ("sp", 2), ("own", 2), ("own", 3), ("own", 4), ("p", 0, 0),
    ("p", 0, 1), ("p", 0, 2), ("p", 0, 3), ("z", 1, 1, 0), ("z", 1, 1, 1), ("z", 1, 2, 0), ("z", 1, 2, 1),
    ("z", 1, 3, 0), ("z", 1, 3, 1), ("masks",), ("p", 4, 0), ("z", 3, 1, 0), ("p", 2, 0), ("t", 0, 0),
    ("sp", 3), ("own", 5), ("t", 0, 1), ("z", 3, 2, 0), ("z", 3, 3, 0), ("sp", 4), ("z", 4, 1, 0), ("t", 1, 0),
    ("t", 1, 1), ("z", 2, 1, 0), ("z", 4, 2, 0), ("cw", 0), ("q", 0), ("q", 1), ("q", 2), ("q", 3),
    ("z", 2, 2, 0), ("p", 3, 0), ("shared",), ("cw", 1), ("kv", 0), ("kv", 1), ("kv", 2), ("z", 2, 1, 1),
    ("z", 2, 2, 1), ("z", 2, 3, 0), ("kv", 3), ("att", 0), ("z", 2, 3, 1), ("p", 5, 0), ("att", 1), ("p", 3, 1),
    ("p", 3, 2), ("p", 3, 3), ("z", 5, 1, 0), ("z", 4, 3, 0), ("t", 3, 0), ("att", 2), ("z", 5, 2, 0),
    ("z", 4, 1, 1), ("z", 4, 2, 1), ("att", 3), ("br", 0), ("z", 5, 1, 1), ("t", 2, 0), ("t", 2, 1), ("br", 1),
    ("z", 4, 3, 1), ("z", 5, 3, 0), ("br", 2), ("br", 3), ("n1",), ("z", 5, 2, 1), ("t", 3, 1), ("cw", 2),
    ("up", 0, 0), ("up", 1, 0), ("t", 4, 0), ("z", 5, 3, 1), ("up", 2, 0), ("up", 3, 0), ("t", 4, 1), ("cw", 3),
    ("up", 0, 1), ("t", 5, 0), ("up", 1, 1), ("up", 2, 1), ("up", 3, 1), ("t", 5, 1), ("cw", 4), ("dn", 0, 0),
    ("dn", 1, 0), ("dn", 2, 0), ("dn", 3, 0), ("cw", 5), ("dn", 0, 1), ("dn", 1, 1), ("dn", 2, 1), ("dn", 3, 1),
    ("n2",), ("sent",), ("hb", 0, 0), ("hb", 1, 0), ("hb", 2, 0), ("hb", 3, 0), ("cs", 0), ("hb", 0, 1),
    ("hb", 1, 1), ("hb", 2, 1), ("hb", 3, 1), ("ce", 0, 1), ("cs", 1), ("ub", 0), ("ub", 1), ("ub", 2),
    ("ub", 3), ("n1b",), ("gu", 0, 0), ("gu", 1, 0), ("ce", 1, 1), ("ce", 1, 0), ("gu", 2, 0), ("gu", 3, 0),
    ("cs", 2), ("gu", 0, 1), ("gu", 1, 1), ("gu", 2, 1), ("gu", 3, 1), ("ce", 0, 0), ("te", 0, 1), ("te", 0, 0),
    ("cs", 3), ("mb", 0), ("ab", 0, 0), ("ab", 0, 1), ("ab", 0, 2), ("kb", 0), ("te", 1, 1), ("mb", 1),
    ("ab", 1, 0), ("ce", 2, 1), ("te", 1, 0), ("ab", 1, 1), ("ab", 1, 2), ("kb", 1), ("mb", 2), ("ab", 2, 0),
    ("ab", 2, 1), ("ab", 2, 2), ("kb", 2), ("se", 0), ("mb", 3), ("ab", 3, 0), ("ce", 3, 1), ("zs", 1, 1, 0),
    ("zs", 1, 1, 1), ("ce", 2, 0), ("ab", 3, 1), ("ab", 3, 2), ("kb", 3), ("te", 2, 1), ("sm0",), ("turn",),
    ("aq", 0), ("ak", 0), ("aq", 1), ("ak", 1), ("aq", 2), ("ak", 2), ("aq", 3), ("ak", 3), ("cs", 4),
    ("zs", 1, 0, 0), ("ce", 3, 0), ("zs", 1, 0, 1), ("te", 3, 1), ("zs", 1, 1, 2), ("te", 2, 0), ("zl", 1, 1),
    ("ce", 4, 1), ("sm", 0), ("se", 2), ("zs", 3, 1, 0), ("la", 0), ("te", 3, 0), ("ce", 4, 0), ("te", 4, 1),
    ("zs", 3, 1, 1), ("cs", 5), ("ce", 5, 1), ("zs", 1, 0, 2), ("sm", 1), ("ce", 5, 0), ("te", 4, 0), ("se", 4),
    ("la", 2), ("zs", 3, 0, 0), ("te", 5, 1), ("wi", 0), ("wi", 1), ("zl", 1, 0), ("sm", 2), ("home",),
    ("zs", 3, 1, 2), ("qi", 0), ("te", 5, 0), ("zs", 3, 0, 1), ("qi", 1), ("zs", 3, 0, 2), ("se", 5), ("sm", 3),
    ("la", 1), ("zl", 3, 1), ("zl", 3, 0), ("qi", 2), ("sm", 4), ("qi", 3), ("la", 4), ("own_in",), ("take",),
    ("la", 3), ("la", 5),
)

INPUTS = ("m_qkv", "m_out", "m_up", "m_down", "m_norm", "m_bias", "tok", "out_grad", "seg", "grp", "ans")
OUTPUTS = ("block_out", "input_grad", "owned", "sums", "squares")


def kernel(names, chunks, back_chunks, pairs, *refs):
    r = dict(zip(names, refs))
    pc = Place()
    loads = {n: pltpu.make_async_copy(r["hbm_" + n], r[n], r["load_sems"].at[k]) for k, n in enumerate(INPUTS)}
    stores = {n: pltpu.make_async_copy(r[n], r["hbm_" + n], r["store_sems"].at[k]) for k, n in enumerate(OUTPUTS)}
    for copy in loads.values():
        copy.start()
    all_here = greet(pc)
    r["squares"][...] = jnp.zeros_like(r["squares"])
    for n in INPUTS[:2]:
        loads[n].wait()
    gather = Gather(pc, r["g"], chunks, [r["gs%d" % k] for k in range(8)])
    lower_heads(r, pc, chunks, gather)
    layer = Layer(r, pc)
    rows, length = layer.rows, layer.length
    tok, tokw, window, xr, owned = r["tok"], r["tokw"], r["xw"], r["xrecv"], r["owned"]
    share = Share(
        pc,
        pairs,
        lambda low, high, target: tok.at[pl.ds(low % rows, high - low)],
        lambda low, high, target: tokw.at[in_window(low, high, target, rows, length)],
        r["share_sems"],
    )
    home = Share(
        pc,
        [(t, s, low, high) for s, t, low, high in pairs],
        lambda low, high, target: window.at[in_window(low, high, other_end(pairs, target, low), rows, length)],
        lambda low, high, target: xr.at[1 if low % rows == 0 else 0, pl.ds(0, high - low)],
        r["home_sems"],
    )
    spread = Sum5(pc, r["table"], r["table_slots"], r["table_sems"])
    total = Sum5(pc, r["sums"], r["sum_slots"], r["sum_sems"])

    def emit(j, value):
        a, low, w, _ = back_chunks[j]
        owned[a, :, low : low + w] = value
        line = col_sum(value * value)
        r["squares"][...] += sum(line[:, k : k + 128] for k in range(0, w, 128))

    grads = (r["hid"], r["g"].at[UP], r["g"].at[DOWN])
    back = Scatter(
        pc, grads, back_chunks, r["rc"], r["r3"], r["r2"], r["rz"], [r["ss%d" % k] for k in range(9)], emit
    )

    def start():
        for m in range(4):

            def own_tokens(m=m):
                for at, where in own_parts(m, rows, length):
                    tokw[where[0], where[1], :] = tok[at, :]

            pl.when(pc.m == m)(own_tokens)

    def share_start():
        loads["tok"].wait()
        share.start()

    def masks():
        for n in ("seg", "grp", "ans"):
            loads[n].wait()
        layer.masks()

    def second_norm():
        loads["out_grad"].wait()
        layer.second_norm()
        stores["block_out"].start()

    def rest():
        for n in INPUTS[2:6]:
            loads[n].wait()
        lower_rest(r, pc, chunks, gather)
        spread.start(0)

    def table_step(k):
        spread.end(k)
        if k < 4:
            spread.start(k + 1)
        else:
            r["tab"][...] = r["table"][...].astype(F32)

    def sums_start():
        r["sums"][14:16, :] = jnp.zeros_like(r["sums"][14:16, :])
        total.start(0)

    def sums_step(k):
        total.end(k)
        if k < 4:
            total.start(k + 1)
        else:
            stores["sums"].start()

    def sent():
        gather.finish()
        share.wait_send()
        spread.finish()

    def homeward():
        for m in range(4):

            def own_rows(m=m):
                for at, where in own_parts(m, rows, length):
                    r["acc"][at, :] += window[where[0], where[1], :].astype(F32)

            pl.when(pc.m == m)(own_rows)

    def take():
        home.wait_recv()
        for source, target, low, high in home.pairs:

            def add(source=source, target=target, low=low, high=high):
                at = slice(low - target * rows, high - target * rows)
                k = 1 if low % rows == 0 else 0
                r["acc"][at, :] += xr[k, : high - low, :].astype(F32)

            pl.when(pc.m == target)(add)
        r["input_grad"][...] = r["acc"][...].astype(BF16)
        stores["input_grad"].start()

    steps = {
        "own": gather.own,
        "z": gather.z_step,
        "p": gather.p_step,
        "t": gather.t_step,
        "cw": gather.core_wait,
        "share": share_start,
        "shared": share.wait_recv,
        "rest": rest,
        "sp": table_step,
        "sent": sent,
        "start": start,
        "masks": masks,
        "q": layer.queries,
        "kv": layer.keys_values,
        "att": layer.attend,
        "br": layer.branch,
        "n1": layer.first_norm,
        "up": layer.up,
        "dn": layer.down,
        "n2": second_norm,
        "hb": layer.hidden_back,
        "ub": layer.up_back,
        "n1b": layer.first_back,
        "gu": layer.up_grad,
        "mb": layer.mixed_back,
        "ab": layer.attend_back,
        "kb": layer.keys_back,
        "sm0": sums_start,
        "sm": sums_step,
        "turn": layer.turn,
        "aq": layer.query_grad,
        "ak": layer.keys_grad,
        "qi": layer.query_input,
        "wi": layer.window_input,
        "home": home.start,
        "own_in": homeward,
        "take": take,
        "cs": back.core_start,
        "ce": back.core_end,
        "te": back.third_end,
        "se": back.second_end,
        "zs": back.z_step,
        "zl": back.z_last,
        "la": back.last,
    }
    all_here()
    for name, *at in ORDER:
        steps[name](*at)

    stores["owned"].start()
    norm = Total(pc, r["squares"], r["norm_slots"], r["norm_sems"])
    norm.run()
    stores["squares"].start()
    home.wait_send()
    back.finish()
    total.finish()
    norm.finish()
    for copy in stores.values():
        copy.wait()


def lower_heads(r, pc, chunks, gather):
    qkv = r["m_qkv"]
    heads = jnp.concatenate([qkv[0], r["m_out"][...].T, qkv[1], qkv[2]], 1)
    for j, (a, low, w, _) in enumerate(chunks):
        if a == ATT:
            ref = gather.piece(j, pc.z, 0, 0)
            ref[...] = heads[:, low : low + w].astype(BF16)


def lower_rest(r, pc, chunks, gather):
    table, local = r["table"], r["m_qkv"].shape[2]
    for j, (a, low, w, _) in enumerate(chunks):
        if a != ATT:
            ref = gather.piece(j, pc.z, 0, 0)
            ref[...] = r["m_up" if a == UP else "m_down"][:, low : low + w].astype(BF16)
    outer = pc.z * 2 + pc.x
    norm, bias = r["m_norm"], r["m_bias"]
    part, piece = norm.shape[2], bias.shape[1]
    width, columns = table.shape[1], 8 * piece
    wide = r["norm_wide"]
    wide[...] = jnp.zeros_like(wide)
    for k in range(6):
        wide[k : k + 1, :part] = norm[k]
    rows = pltpu.roll(wide[...], pc.m * local + outer * part, 1)
    line = r["bias_wide"]
    line[...] = jnp.zeros_like(line)
    line[0:1, :piece] = bias[...]
    line = pltpu.roll(line[...], outer * piece, 1)[0:1]
    head = line[:, : 2 * local]
    early = lax.broadcasted_iota(jnp.int32, head.shape, 1) < local
    attention = jnp.concatenate([jnp.where(early, head, 0.0), jnp.where(early, 0.0, head)], 1)
    hidden = line[:, 2 * local :]
    row = lax.broadcasted_iota(jnp.int32, (8, width), 0)
    top = jnp.where(row < 6, rows, 0.0)
    top = jnp.where(row == 6 + pc.m, attention, top)
    top = jnp.where(row == 10 + pc.m, hidden, top)
    low = jnp.where(row + 8 == 6 + pc.m, attention, 0.0)
    low = jnp.where(row + 8 == 10 + pc.m, hidden, low)
    table[...] = jnp.concatenate([top, low], 0).astype(BF16)


def other_end(pairs, owner, low):
    return [t for s, t, first, _ in pairs if s == owner and first == low][0]


def in_window(low, high, m, rows, length):
    return low // length - m * rows // length, pl.ds(low % length, high - low)


def own_parts(m, rows, length):
    parts, low = [], m * rows
    while low < (m + 1) * rows:
        high = min((m + 1) * rows, (low // length + 1) * length)
        parts.append((slice(low - m * rows, high - m * rows), in_window(low, high, m, rows, length)))
        low = high
    return parts


def run_layer(masters, tok, out_grad, seg, grp, ans, pad):
    per, cols = masters[2].shape
    rows, width = tok.shape
    length = seg.shape[1]
    hidden = 4 * cols
    window = max((m * rows + rows - 1) // length - m * rows // length + 1 for m in range(4))
    blocks = rows // 128
    pairs = overlaps(rows, length)
    chunks = chunks_of((ATT, UP, DOWN), cols, WAYS)
    back_chunks = chunks_of((DOWN, UP, ATT), cols, BACK_WAYS)
    most = max(high - low for _, _, low, high in pairs)
    bufs, sems = scatter_scratch(back_chunks, per)
    scratch = {
        "g": pltpu.VMEM((3, 4, 2, per, hidden), BF16),
        "table": pltpu.VMEM((16, width), BF16),
        "norm_wide": pltpu.VMEM((8, width), F32),
        "bias_wide": pltpu.VMEM((8, 8 * masters[5].shape[1]), F32),
        "tab": pltpu.VMEM((16, width), F32),
        "table_slots": pltpu.VMEM((10, 16, width), BF16),
        "tokw": pltpu.VMEM((window, length, width), BF16),
        "bias": pltpu.VMEM((blocks, 128, length), F32),
        "q": pltpu.VMEM((4, rows, 256), BF16),
        "kv": pltpu.VMEM((4, window, length, cols // 2), BF16),
        "shares": pltpu.VMEM((4, blocks, 3, 128, length), BF16),
        "o": pltpu.VMEM((4, rows, 256), BF16),
        "do": pltpu.VMEM((rows, 256), BF16),
        "dkv_acc": pltpu.VMEM((window, length, cols // 2), F32),
        "acc": pltpu.VMEM((rows, width), F32),
        "xh": pltpu.VMEM((rows, width), F32),
        "rs": pltpu.VMEM((rows, 1), F32),
        "hb": pltpu.VMEM((rows, width), BF16),
        "dz": pltpu.VMEM((rows, width), BF16),
        "hid": pltpu.VMEM((4, 2, per, hidden), BF16),
        "turned": pltpu.VMEM((width, rows), BF16),
        "turned2": pltpu.VMEM((width, rows), BF16),
        "turnedw": pltpu.VMEM((window, width, length), BF16),
        "xw": pltpu.VMEM((window, length, width), BF16),
        "xrecv": pltpu.VMEM((2, most, width), BF16),
        "sum_slots": pltpu.VMEM((10, 16, width), F32),
        "share_sems": pltpu.SemaphoreType.DMA((4,)),
        "home_sems": pltpu.SemaphoreType.DMA((4,)),
        "table_sems": pltpu.SemaphoreType.DMA((10,)),
        "norm_slots": pltpu.VMEM((12, 8, 128), F32),
        "norm_sems": pltpu.SemaphoreType.DMA((20,)),
        "sum_sems": pltpu.SemaphoreType.DMA((10,)),
    }
    scratch.update(zip(("rc", "r3", "r2", "rz"), bufs))
    scratch.update(("gs%d" % k, s) for k, s in enumerate(gather_sems(len(chunks))))
    scratch.update(("ss%d" % k, s) for k, s in enumerate(sems))
    given = dict(zip(INPUTS, list(masters) + [tok, out_grad, seg, grp, ans]))
    scratch.update((n, pltpu.VMEM(v.shape, v.dtype)) for n, v in given.items())
    made = dict(
        block_out=jax.ShapeDtypeStruct((rows, width), BF16),
        input_grad=jax.ShapeDtypeStruct((rows, width), BF16),
        owned=jax.ShapeDtypeStruct((3, per, cols), F32),
        sums=jax.ShapeDtypeStruct((16, width), F32),
        squares=jax.ShapeDtypeStruct((8, 128), F32),
    )
    scratch.update((n, pltpu.VMEM(v.shape, v.dtype)) for n, v in made.items())
    scratch["load_sems"] = pltpu.SemaphoreType.DMA((len(INPUTS),))
    scratch["store_sems"] = pltpu.SemaphoreType.DMA((len(OUTPUTS),))
    names = tuple("hbm_" + n for n in INPUTS) + ("pad",) + tuple("hbm_" + n for n in OUTPUTS) + tuple(scratch)
    anywhere = pl.BlockSpec(memory_space=pl.ANY)
    return pl.pallas_call(
        functools.partial(kernel, names, chunks, back_chunks, pairs),
        out_shape=list(made.values()),
        in_specs=[anywhere] * len(INPUTS) + [pl.BlockSpec(memory_space=pltpu.SMEM)],
        out_specs=[anywhere] * len(OUTPUTS),
        scratch_shapes=list(scratch.values()),
        compiler_params=pltpu.CompilerParams(collective_id=0, has_side_effects=True, vmem_limit_bytes=62 * 2**20),
        name="layer",
    )(*masters, tok, out_grad, seg, grp, ans, pad)


def adam_update(weight, grad, first, second, factor, decayed, rate):
    clipped = grad * factor
    first_new = beta_first * first + (1.0 - beta_first) * clipped
    second_new = beta_second * second + (1.0 - beta_second) * clipped * clipped
    ratio = (
        first_new
        / (1.0 - beta_first**STEP)
        / (jnp.sqrt(second_new / (1.0 - beta_second**STEP)) + adam_epsilon)
    )
    if decayed:
        ratio = ratio + decay_rate * weight
    return (weight - rate * ratio, first_new, second_new)


def update_kernel(*refs):
    given, (block_out, input_grad, norm_out), made = refs[:23], refs[23:26], refs[26:44]
    held, (grad_norm, load_sems, store_sems) = refs[44:67], refs[67:]
    loads = [pltpu.make_async_copy(a, b, load_sems.at[k]) for k, (a, b) in enumerate(zip(given, held))]
    outs = [held[2 + n * 6 + k] for n in range(3) for k in range(6)]
    stores = [pltpu.make_async_copy(a, b, store_sems.at[k]) for k, (a, b) in enumerate(zip(outs, made))]
    order = [1, 22, 0] + [2 + n * 6 + k for k in (2, 3, 0, 1, 4, 5) for n in range(3)] + [20, 21]
    for k in order:
        loads[k].start()
    passed = [
        pltpu.make_async_copy(held[20], block_out, store_sems.at[18]),
        pltpu.make_async_copy(held[21], input_grad, store_sems.at[19]),
        pltpu.make_async_copy(grad_norm, norm_out, store_sems.at[20]),
    ]
    owned, total = held[:2]
    masters, firsts, seconds = held[2:8], held[8:14], held[14:20]
    loads[1].wait()
    loads[22].wait()
    place = lax.axis_index("outer") * lax.axis_size("inner") + lax.axis_index("inner")
    mp = lax.axis_index("mp")
    local = masters[0].shape[2]
    width = total.shape[1]
    lane = lax.broadcasted_iota(jnp.int32, (4, width), 1)
    head, hidden = total[6:10, :], total[10:14, :]
    head = jnp.where((lane < local) | (lane >= 3 * local), head, 0.0)

    def square(v):
        return jnp.sum(jnp.sum(v * v, 0, keepdims=True), 1, keepdims=True)

    squares = jnp.sum(held[22][0:1, :], 1, keepdims=True) + square(total[0:6, :]) + square(head) + square(hidden)
    norm = jnp.sqrt(squares)
    grad_norm[...] = norm
    passed[2].start()
    factor = jnp.minimum(1.0, clip_limit / norm)
    mine = lax.broadcasted_iota(jnp.int32, (4, width), 0) == mp
    head = jnp.sum(jnp.where(mine, head, 0.0), 0, keepdims=True)
    hidden = jnp.sum(jnp.where(mine, hidden, 0.0), 0, keepdims=True)
    line = jnp.concatenate([head[:, : 2 * local] + head[:, 2 * local :], hidden], 1)
    part, piece = masters[4].shape[2], masters[5].shape[1]
    line = jnp.broadcast_to(line, (8, line.shape[1]))
    line = pltpu.roll(line, lax.rem(line.shape[1] - place * piece, line.shape[1]), 1)[0:1, :piece]
    norms = pltpu.roll(total[0:8, :], lax.rem(width - (mp * local + place * part), width), 1)

    def update(k, at, grad):
        values = adam_update(masters[k][at], grad, firsts[k][at], seconds[k][at], factor, k < 4, learn_rates[k])
        for n, value in enumerate(values):
            outs[n * 6 + k][at] = value

    def ready(k):
        for n in range(3):
            loads[2 + n * 6 + k].wait()

    def done(k):
        for n in range(3):
            stores[n * 6 + k].start()

    loads[0].wait()
    everything = (slice(None), slice(None))
    for k, grad in ((2, owned[1]), (3, owned[2])):
        ready(k)
        update(k, everything, grad)
        done(k)
    attention = owned[0]
    ready(0)
    update(0, 0, attention[:, :local])
    update(0, 1, attention[:, 2 * local : 3 * local])
    update(0, 2, attention[:, 3 * local :])
    done(0)
    ready(1)
    update(1, everything, attention[:, local : 2 * local].T)
    done(1)
    ready(4)
    for k in range(6):
        update(4, k, norms[k : k + 1, :part])
    done(4)
    ready(5)
    update(5, everything, line)
    done(5)
    for k in range(2):
        loads[20 + k].wait()
        passed[k].start()
    for copy in stores + passed:
        copy.wait()


def update(owned, total, squares, block_out, input_grad, masters, firsts, seconds):
    anywhere = pl.BlockSpec(memory_space=pl.ANY)
    given = [owned, total, *masters, *firsts, *seconds, block_out, input_grad, squares]

    def like(v):
        return jax.ShapeDtypeStruct(v.shape, v.dtype)

    return pl.pallas_call(
        update_kernel,
        out_shape=[like(block_out), like(input_grad), jax.ShapeDtypeStruct((1, 1), F32)] + [like(m) for m in masters] * 3,
        in_specs=[anywhere] * len(given),
        out_specs=[anywhere] * 21,
        scratch_shapes=[pltpu.VMEM(v.shape, v.dtype) for v in given]
        + [pltpu.VMEM((1, 1), F32), pltpu.SemaphoreType.DMA((len(given),)), pltpu.SemaphoreType.DMA((21,))],
        compiler_params=pltpu.CompilerParams(vmem_limit_bytes=62 * 2**20),
        name="update",
    )(*given)


def body(tokens, out_grad, segment_ids, group_ids, answer_ids, pad_lengths, *states):
    def turned(values):
        return [v.T if k == 3 else v for k, v in enumerate(values)]

    masters, firsts, seconds = turned(states[:6]), turned(states[6:12]), turned(states[12:])
    inner = lax.axis_size("inner")
    shared = masters
    if inner > 1:
        shared = [lax.all_gather(v, "inner", axis=d, tiled=True) for v, d in zip(masters, (1, 1, 0, 0, 2, 1))]
    block_out, input_grad, owned, total, squares = run_layer(
        shared, tokens, out_grad, segment_ids, group_ids, answer_ids, pad_lengths
    )
    if inner > 1:
        owned = lax.psum_scatter(owned, "inner", scatter_dimension=1, tiled=True)
        total = lax.psum(total, "inner")
        squares = lax.psum(jnp.sum(owned * owned), ("outer", "inner", "mp"))
        squares = jnp.full((8, 128), squares / 128)
    results = update(owned, total, squares, block_out, input_grad, masters, firsts, seconds)
    updated = [v for n in range(3) for v in turned(results[3 + 6 * n : 9 + 6 * n])]
    return (results[0], results[1], results[2][0, 0]) + tuple(updated)


def solution(mesh):
    dp = mesh.shape["dp"]
    outer = 8
    grid = Mesh(mesh.devices.reshape(outer, dp // outer, mesh.shape["mp"]), ("outer", "inner", "mp"))
    d = ("outer", "inner")
    both = P(d + ("mp",), None)
    states = (P(None, d, "mp"), P("mp", d), P(d, "mp"), P("mp", d), P(None, "mp", d), P("mp", d))
    in_specs = (both, both, P(d, None), P(d, None), P(d, None), P(d)) + states * 3
    out_specs = (both, both, P()) + states * 3
    return jax.shard_map(body, mesh=grid, in_specs=in_specs, out_specs=out_specs, check_vma=False)
```
